512 devices in a mesh: ctx: 32 (over x, y), head: 16 (over z, core).
Axes of the slice: x: 4, y: 8, z: 8, core: 2. Of those that a mesh axis runs over, the one named last changes fastest.
Arguments:
- context: bfloat16 [32768, 2048], P('ctx'), may hold values from -6 to 6
- w_attn: bfloat16 [3, 2048, 2048], P(None, 'ctx', 'head')
- w_out: bfloat16 [2048, 2048], P('head', 'ctx'), may hold values from -0.125 to 0.125
- w_latent: bfloat16 [3, 2048, 2048], P(None, 'ctx', 'head')
- w_latent_out: bfloat16 [2048, 2048], P('head', 'ctx'), may hold values from -0.125 to 0.125
- w_mlp: bfloat16 [2, 2048, 8192], P(None, 'ctx', 'head'), may hold values from -0.125 to 0.125
- w_down: bfloat16 [8192, 2048], P('head', 'ctx'), may hold values from -0.0625 to 0.0625
- gains: float32 [3, 2048], replicated, may hold values from 0.1 to 1.9
- valid_len: int32 [32], P('ctx'), may hold values from 1 to 1024, as said below
- last_visible: int32 [1024], replicated, may hold values from 31744 to 32767, as said below
Outputs:
- latent_out: bfloat16 [1024, 2048], P('ctx', 'head')
The draws below stay inside these ranges and needn't reach their ends.
Inputs may be any that keep to these rules, and one draw needn't show every extreme that they name: `valid_len`: the last entry is 1024; one other entry is 1. `last_visible`: some latent stands at 31744 and some at 32767; several latents may share a position.
All inputs are finite; a program needn't handle non-finite values.
Results may differ from the reference program's by a relative error of at most 0.022.
Values may be sent and summed in bfloat16 or wider, within the bound.
No kernel may reach another device: no remote copies, remote signals or barrier semaphores. Data moves between devices by JAX's collectives and lax.ppermute only.
A program may use at most 128 MiB of HBM per device.

```python
import math
import jax
import jax.numpy as jnp
from jax import lax

D = 2048
HEADS = 16
HD = 128
FF = 8192
NL = 1024
TOK_DEV = 1024
CONTEXT = 32768
N_CTX = 32


def stack_weights(key, low_scale, high_scale):
    key_shared, key_private, key_values, key_strength = jax.random.split(key, 4)
    shared = jax.random.normal(key_shared, (D, D), jnp.float32)
    private = jax.random.normal(key_private, (D, D), jnp.float32)
    values_raw = jax.random.normal(key_values, (D, D), jnp.float32)
    strength = jax.random.uniform(key_strength, (HEADS,), jnp.float32, low_scale, high_scale)
    column_scale = jnp.repeat(strength, HD)
    query_part = 3.0 * shared
    key_part = private * column_scale[None, :]
    return jnp.stack([query_part, key_part, values_raw]) / math.sqrt(D)


def draw_w_attn(key, part):
    key = jax.random.fold_in(key, 5)
    return stack_weights(key, 1.0, 1.0).astype(jnp.bfloat16)


def draw_w_latent(key, part):
    key = jax.random.fold_in(key, 7)
    return stack_weights(key, 1.0, 1.0).astype(jnp.bfloat16)


def draw_valid_len(key, part):
    key = jax.random.fold_in(key, 11)
    key_len, key_spot = jax.random.split(key)
    lengths = jax.random.randint(key_len, (N_CTX,), 1, TOK_DEV + 1, jnp.int32)
    short_spot = jax.random.randint(key_spot, (), 0, N_CTX - 1, jnp.int32)
    lengths = lengths.at[short_spot].set(1)
    return lengths.at[N_CTX - 1].set(TOK_DEV).astype(jnp.int32)


def draw_last_visible(key, part):
    key = jax.random.fold_in(key, 13)
    context_len = TOK_DEV * N_CTX
    spots = jax.random.randint(key, (NL,), context_len - NL, context_len, jnp.int32)
    spots = spots.at[0].set(context_len - NL)
    return spots.at[NL - 1].set(context_len - 1).astype(jnp.int32)


def shard_levels(key, extent, pieces, least, top_value):
    gain = 1.0
    for dim, parts in pieces:
        heights = jax.random.uniform(jax.random.fold_in(jax.random.fold_in(key, 6), dim), (parts,), jnp.float32, least / len(pieces), top_value / len(pieces))
        gain = gain * jnp.repeat(jnp.exp(heights), extent[dim] // parts).reshape((-1,) + (1,) * (len(extent) - 1 - dim))
    return gain


def noise(stream_key, extent, width, most, pieces=(), kind=jnp.bfloat16):
    drawn = jax.random.normal(stream_key, extent, jnp.float32) * width
    if len(pieces) > 0:
        drawn = shard_levels(stream_key, extent, pieces, -0.22, 0.18) * drawn
    return jnp.clip(drawn, min=-most, max=most).astype(kind)


def setup_inputs(seed: int = 0) -> dict:
    key_of = jax.random.split(jax.random.key(seed), 11)
    context = noise(key_of[0], (CONTEXT, D), 1.0, 6.0, ((0, 32),))
    w_attn = draw_w_attn(jax.random.fold_in(key_of[10], 71), 0)
    w_out = noise(key_of[2], (D, D), D ** -0.5, 0.125, ((0, 16), (1, 32)))
    w_latent = draw_w_latent(jax.random.fold_in(key_of[10], 71), 0)
    w_latent_out = noise(key_of[4], (D, D), D ** -0.5, 0.125, ((0, 16), (1, 32)))
    w_mlp = noise(key_of[5], (2, D, FF), D ** -0.5, 0.125, ((1, 32), (2, 16)))
    w_down = noise(key_of[6], (FF, D), FF ** -0.5, 0.0625, ((0, 16), (1, 32)))
    gains = jnp.clip(1.0 + 0.18 * jax.random.normal(key_of[7], (3, D), jnp.float32), 0.1, 1.9)
    valid_len = draw_valid_len(jax.random.fold_in(key_of[10], 71), 0)
    last_visible = draw_last_visible(jax.random.fold_in(key_of[10], 71), 0)
    return dict(context=context, w_attn=w_attn, w_out=w_out, w_latent=w_latent, w_latent_out=w_latent_out, w_mlp=w_mlp, w_down=w_down, gains=gains, valid_len=valid_len, last_visible=last_visible)


epsilon = 1e-05
masked_score = -1e+30

def unit_rows(rows):
    widened = rows.astype(jnp.float32)
    return widened * lax.rsqrt(lax.optimization_barrier(jnp.mean(widened * widened, axis=-1, keepdims=True)) + epsilon)

def widen(values_in):
    return lax.optimization_barrier(values_in).astype(jnp.float32)

def merge_parts(first, second):
    top_a, total_a, out_a = first
    top_b, total_b, out_b = second
    row_top = jnp.maximum(top_a, top_b)
    scale_a = jnp.exp(top_a - row_top)
    scale_b = jnp.exp(top_b - row_top)
    return (row_top, total_a * scale_a + total_b * scale_b, out_a * scale_a[..., None] + out_b * scale_b[..., None])

def reference(context, w_attn, w_out, w_latent, w_latent_out, w_mlp, w_down, gains, valid_len, last_visible):
    score_scale = HD ** (-0.5)
    normed = (unit_rows(context) * gains[0]).astype(jnp.bfloat16)
    lat_raw = jnp.take(context, last_visible, axis=0)
    lat_norm = jnp.take(normed, last_visible, axis=0)
    queries = jnp.dot(lat_norm, w_attn[0], preferred_element_type=jnp.float32).astype(jnp.bfloat16)
    query_heads = widen(queries.reshape(NL, HEADS, HD))
    key_local = jnp.arange(TOK_DEV, dtype=jnp.int32)

    def block_step(carry, block):
        rows = lax.dynamic_slice_in_dim(normed, block * TOK_DEV, TOK_DEV, 0)
        keys = jnp.dot(rows, w_attn[1], preferred_element_type=jnp.float32).astype(jnp.bfloat16)
        values = jnp.dot(rows, w_attn[2], preferred_element_type=jnp.float32).astype(jnp.bfloat16)
        key_pos = block * TOK_DEV + key_local
        limit = lax.dynamic_slice_in_dim(valid_len, block, 1, 0)
        key_kept = (key_pos[None, :] <= last_visible[:, None]) & (key_local < limit[0])[None, :]
        score = jnp.einsum('qhd,khd->hqk', query_heads, widen(keys.reshape(TOK_DEV, HEADS, HD))) * score_scale
        score = jnp.where(key_kept[None], score, masked_score)
        row_top = lax.optimization_barrier(jnp.max(score, axis=2))
        prob = jnp.where(key_kept[None], jnp.exp(score - row_top[:, :, None]), 0.0)
        row_total = lax.optimization_barrier(jnp.sum(prob, axis=2))
        row_out = jnp.einsum('hqk,khd->hqd', widen(prob.astype(jnp.bfloat16)), widen(values.reshape(TOK_DEV, HEADS, HD)))
        return (merge_parts(carry, (row_top, row_total, row_out)), None)
    start = (jnp.full((HEADS, NL), masked_score, jnp.float32), jnp.zeros((HEADS, NL), jnp.float32), jnp.zeros((HEADS, NL, HD), jnp.float32))
    blocks = jnp.arange(N_CTX, dtype=jnp.int32)
    (row_top, row_total, row_out), unused = lax.scan(block_step, start, blocks)
    attended = (row_out / row_total[:, :, None]).astype(jnp.bfloat16).transpose(1, 0, 2).reshape(NL, D)
    h_first = (lat_raw.astype(jnp.float32) + jnp.dot(attended, w_out, preferred_element_type=jnp.float32)).astype(jnp.bfloat16)
    n_second = (unit_rows(h_first) * gains[1]).astype(jnp.bfloat16)
    latent_q = jnp.dot(n_second, w_latent[0], preferred_element_type=jnp.float32).astype(jnp.bfloat16)
    latent_k = jnp.dot(n_second, w_latent[1], preferred_element_type=jnp.float32).astype(jnp.bfloat16)
    latent_v = jnp.dot(n_second, w_latent[2], preferred_element_type=jnp.float32).astype(jnp.bfloat16)
    key_seen = last_visible[None, :] <= last_visible[:, None]
    self_score = jnp.einsum('qhd,khd->hqk', widen(latent_q.reshape(NL, HEADS, HD)), widen(latent_k.reshape(NL, HEADS, HD))) * score_scale
    self_score = jnp.where(key_seen[None], self_score, masked_score)
    self_top = lax.optimization_barrier(jnp.max(self_score, axis=2, keepdims=True))
    self_prob = jnp.where(key_seen[None], jnp.exp(self_score - self_top), 0.0)
    self_prob = (self_prob / lax.optimization_barrier(jnp.sum(self_prob, axis=2, keepdims=True))).astype(jnp.bfloat16)
    mixed = jnp.einsum('hqk,khd->qhd', widen(self_prob), widen(latent_v.reshape(NL, HEADS, HD))).reshape(NL, D).astype(jnp.bfloat16)
    h_second = (h_first.astype(jnp.float32) + jnp.dot(mixed, w_latent_out, preferred_element_type=jnp.float32)).astype(jnp.bfloat16)
    n_third = (unit_rows(h_second) * gains[2]).astype(jnp.bfloat16)
    gate = jnp.dot(n_third, w_mlp[0], preferred_element_type=jnp.float32)
    upward = jnp.dot(n_third, w_mlp[1], preferred_element_type=jnp.float32)
    hidden = (jax.nn.silu(gate) * upward).astype(jnp.bfloat16)
    return (h_second.astype(jnp.float32) + jnp.dot(hidden, w_down, preferred_element_type=jnp.float32)).astype(jnp.bfloat16)
```

```python
import jax
import jax.numpy as jnp
from jax import lax
from jax.sharding import PartitionSpec as P

HD = 128

epsilon = 1e-05
masked_score = -1e30
f32 = jnp.float32
bf16 = jnp.bfloat16


def unit_rows(rows, gain):
    wide = rows.astype(f32)
    return (wide * lax.rsqrt(jnp.mean(wide * wide, axis=-1, keepdims=True) + epsilon) * gain).astype(bf16)


def swap(x, axis):
    return lax.all_to_all(x, axis, 0, 0)


def spread(x, axis):
    count = lax.axis_size(axis)
    return swap(jnp.broadcast_to(x[None], (count,) + x.shape), axis)


def nt(a, b):
    return lax.dot_general(a, b, (((1,), (1,)), ((), ())), preferred_element_type=f32)


def nn(a, b):
    return jnp.dot(a, b, preferred_element_type=f32)


def body(
    context, w_attn, w_out, w_latent, w_latent_out, w_mlp, w_down, gains, valid_len, last_visible
):
    tokens, width = context.shape
    cols = w_attn.shape[2]
    latents = last_visible.shape[0]
    ctxs = lax.axis_size("ctx")
    heads = lax.axis_size("head")
    rows = latents // ctxs
    ctx_index = lax.axis_index("ctx")
    own_start = ctx_index * rows
    scale = HD ** (-0.5)

    pack_a = jnp.concatenate([w_out.T, w_latent[0], w_latent[1], w_latent[2], w_latent_out.T], axis=1)
    pack_b = jnp.concatenate([w_mlp[0], w_mlp[1], w_down.T], axis=1)
    wa = lax.all_gather(pack_a, "ctx", axis=0, tiled=True)
    wb = lax.all_gather(pack_b, "ctx", axis=0, tiled=True)

    wq = spread(jnp.concatenate([w_attn[0], w_attn[1], w_attn[2]], axis=1), "ctx").reshape(width, 3 * cols)

    pick = jnp.clip(last_visible - (ctxs - 1) * tokens, 0, tokens - 1)
    mine = lax.dynamic_slice_in_dim(context, lax.axis_index("head") * cols, cols, 1)
    picked = jnp.take(mine, pick, axis=0).reshape(ctxs, rows, cols)
    own_raw = swap(picked, "ctx")[ctxs - 1]
    raw_rows = spread(own_raw, "head").transpose(1, 0, 2).reshape(rows, width)
    q_own = nn(unit_rows(raw_rows, gains[0]), wq[:, :cols]).astype(bf16)
    queries = spread(q_own, "ctx").reshape(latents, cols)

    normed = unit_rows(context, gains[0])
    keyval = nn(normed, wq[:, cols:]).astype(bf16)
    keys, values = keyval[:, :cols], keyval[:, cols:]

    key_local = jnp.arange(tokens, dtype=jnp.int32)
    kept = ((ctx_index * tokens + key_local)[None, :] <= last_visible[:, None]) & (
        key_local < valid_len[0]
    )[None, :]
    score = jnp.where(kept, nt(queries, keys) * scale, masked_score)
    top = jnp.max(score, axis=1)
    prob = jnp.where(kept, jnp.exp(score - top[:, None]), 0.0)
    total = jnp.sum(prob, axis=1)
    out = nn(prob.astype(bf16), values) / total[:, None]
    lse = top + jnp.log(total)
    hi = lax.reduce_precision(lse, 8, 7)
    mid = lax.reduce_precision(lse - hi, 8, 7)
    low = lse - hi - mid
    parts = jnp.stack([hi, mid, low]).astype(bf16).reshape(3, ctxs, rows).transpose(1, 0, 2)
    parts = jnp.pad(parts.reshape(ctxs, 1, 3 * rows), ((0, 0), (0, 7), (0, cols - 3 * rows)))
    sent = jnp.concatenate([out.astype(bf16).reshape(ctxs, rows, cols), parts], axis=1)
    got = swap(sent, "ctx")
    lse = got[:, rows, : 3 * rows].reshape(ctxs, 3, rows).astype(f32)
    lse = lse[:, 0] + lse[:, 1] + lse[:, 2]
    weight = jnp.exp(lse - jnp.max(lse, axis=0))
    weight = weight / jnp.sum(weight, axis=0)
    attended = jnp.sum(got[:, :rows].astype(f32) * weight[:, :, None], axis=0).astype(bf16)

    def summed(partial):
        chunks = partial.astype(bf16).reshape(rows, heads, cols).transpose(1, 0, 2)
        return jnp.sum(swap(chunks, "head").astype(f32), axis=0)

    def all_columns(own):
        return spread(own, "head").transpose(1, 0, 2).reshape(rows, width)

    h_first = (own_raw.astype(f32) + summed(nt(attended, wa[:, :cols]))).astype(bf16)
    n_second = unit_rows(all_columns(h_first), gains[1])
    qkv = nn(n_second, wa[:, cols : 4 * cols]).astype(bf16)
    pair = spread(qkv[:, cols:], "ctx").reshape(latents, 2 * cols)
    own_pos = lax.dynamic_slice_in_dim(last_visible, own_start, rows, 0)
    seen = last_visible[None, :] <= own_pos[:, None]
    score = jnp.where(seen, nt(qkv[:, :cols], pair[:, :cols]) * scale, masked_score)
    prob = jnp.where(seen, jnp.exp(score - jnp.max(score, axis=1, keepdims=True)), 0.0)
    prob = (prob / jnp.sum(prob, axis=1, keepdims=True)).astype(bf16)
    mixed = nn(prob, pair[:, cols:]).astype(bf16)
    h_second = (h_first.astype(f32) + summed(nt(mixed, wa[:, 4 * cols :]))).astype(bf16)
    n_third = unit_rows(all_columns(h_second), gains[2])
    ff = w_mlp.shape[2]
    gate_up = nn(n_third, wb[:, : 2 * ff])
    hidden = (jax.nn.silu(gate_up[:, :ff]) * gate_up[:, ff:]).astype(bf16)
    return (h_second.astype(f32) + summed(nt(hidden, wb[:, 2 * ff :]))).astype(bf16)


def solution(mesh):
    in_specs = (
        P("ctx", None),
        P(None, "ctx", "head"),
        P("head", "ctx"),
        P(None, "ctx", "head"),
        P("head", "ctx"),
        P(None, "ctx", "head"),
        P("head", "ctx"),
        P(),
        P("ctx"),
        P(),
    )
    out_specs = P("ctx", "head")
    return jax.shard_map(body, mesh=mesh, in_specs=in_specs, out_specs=out_specs, check_vma=False)
```

```python
import jax
import jax.numpy as jnp
from jax import lax
from jax.experimental import pallas as pl
from jax.experimental.pallas import tpu as pltpu
from jax.sharding import PartitionSpec as P

HD = 128

epsilon = 1e-05
masked_score = -1e30
f32 = jnp.float32
bf16 = jnp.bfloat16


def unit_rows(rows, gain):
    wide = rows.astype(f32)
    return (wide * lax.rsqrt(jnp.mean(wide * wide, axis=-1, keepdims=True) + epsilon) * gain).astype(bf16)


def swap(x, axis):
    return lax.all_to_all(x, axis, 0, 0)


def spread(x, axis):
    count = lax.axis_size(axis)
    return swap(jnp.broadcast_to(x[None], (count,) + x.shape), axis)


def shifted(x, step, inner):
    if inner:
        pairs = [(i * 8 + j, i * 8 + (j + step) % 8) for i in range(4) for j in range(8)]
    else:
        pairs = [(i * 8 + j, (i + step) % 4 * 8 + j) for i in range(4) for j in range(8)]
    return lax.ppermute(x, "ctx", pairs)


def place_kernel(first_ref, *refs):
    parts, out_ref = refs[:-1], refs[-1]
    size = parts[0].shape[0]
    for k, part in enumerate(parts):
        slot = lax.rem(first_ref[0] + len(parts) - k, len(parts))
        out_ref[pl.ds(pl.multiple_of(slot * size, size), size), :] = part[...]


def placed(parts, first):
    rows, columns = parts[0].shape
    return pl.pallas_call(
        place_kernel,
        out_shape=jax.ShapeDtypeStruct((len(parts) * rows, columns), parts[0].dtype),
        in_specs=[pl.BlockSpec(memory_space=pltpu.SMEM)]
        + [pl.BlockSpec(memory_space=pltpu.VMEM)] * len(parts),
        out_specs=pl.BlockSpec(memory_space=pltpu.VMEM),
        compiler_params=pltpu.CompilerParams(vmem_limit_bytes=32 * 2**20),
    )(first.reshape(1), *parts)


def over_x(near):
    first = lax.div(lax.axis_index("ctx"), 8)
    return placed([near] + [shifted(near, k, False) for k in range(1, 4)], first)


def over_y(x):
    groups = [[i * 8 + j for j in range(8)] for i in range(4)]
    near = lax.all_to_all(
        jnp.broadcast_to(x[None], (8,) + x.shape), "ctx", 0, 0, axis_index_groups=groups
    )
    return near.reshape(8 * x.shape[0], x.shape[1])


def over_y_steps(x):
    first = lax.rem(lax.axis_index("ctx"), 8)
    return placed([x] + [shifted(x, k, True) for k in range(1, 8)], first)


def nt(a, b):
    return lax.dot_general(a, b, (((1,), (1,)), ((), ())), preferred_element_type=f32)


def nn(a, b):
    return jnp.dot(a, b, preferred_element_type=f32)


def body(
    context, w_attn, w_out, w_latent, w_latent_out, w_mlp, w_down, gains, valid_len, last_visible
):
    tokens, width = context.shape
    cols = w_attn.shape[2]
    latents = last_visible.shape[0]
    ctxs = lax.axis_size("ctx")
    heads = lax.axis_size("head")
    rows = latents // ctxs
    ctx_index = lax.axis_index("ctx")
    own_start = ctx_index * rows
    scale = HD ** (-0.5)

    pack_b = jnp.concatenate([w_latent_out.T, w_mlp[0], w_mlp[1], w_down.T], axis=1)
    wb = lax.all_gather(pack_b, "ctx", axis=0, tiled=True)
    wlo, wb = wb[:, :cols], wb[:, cols:]

    near_all = over_y(jnp.concatenate([w_attn[0], w_attn[1], w_attn[2]], axis=1))
    near_a = over_y_steps(
        jnp.concatenate([w_out.T, w_latent[0], w_latent[1], w_latent[2]], axis=1)
    )
    w_all = over_x(near_all)
    wq, wkv = w_all[:, :cols], w_all[:, cols:]

    pick = jnp.clip(last_visible - (ctxs - 1) * tokens, 0, tokens - 1)
    mine = lax.dynamic_slice_in_dim(context, lax.axis_index("head") * cols, cols, 1)
    picked = jnp.take(mine, pick, axis=0).reshape(ctxs, rows, cols)
    own_raw = swap(picked, "ctx")[ctxs - 1]
    raw_rows = spread(own_raw, "head").transpose(1, 0, 2).reshape(rows, width)
    raw_rows, near_a = lax.optimization_barrier((raw_rows, near_a))
    wa = over_x(near_a)
    q_own = nn(unit_rows(raw_rows, gains[0]), wq).astype(bf16)
    queries = spread(q_own, "ctx").reshape(latents, cols)

    normed = unit_rows(context, gains[0])
    keyval = nn(normed, wkv).astype(bf16)
    keys, values = keyval[:, :cols], keyval[:, cols:]

    key_local = jnp.arange(tokens, dtype=jnp.int32)
    kept = ((ctx_index * tokens + key_local)[None, :] <= last_visible[:, None]) & (
        key_local < valid_len[0]
    )[None, :]
    score = jnp.where(kept, nt(queries, keys) * scale, masked_score)
    top = jnp.max(score, axis=1)
    prob = jnp.where(kept, jnp.exp(score - top[:, None]), 0.0)
    total = jnp.sum(prob, axis=1)
    out = nn(prob.astype(bf16), values) / total[:, None]
    lse = top + jnp.log(total)
    hi = lax.reduce_precision(lse, 8, 7)
    mid = lax.reduce_precision(lse - hi, 8, 7)
    low = lse - hi - mid
    parts = jnp.stack([hi, mid, low]).astype(bf16).reshape(3, ctxs, rows).transpose(1, 0, 2)
    parts = jnp.pad(parts.reshape(ctxs, 1, 3 * rows), ((0, 0), (0, 7), (0, cols - 3 * rows)))
    sent = jnp.concatenate([out.astype(bf16).reshape(ctxs, rows, cols), parts], axis=1)
    sent, wa = lax.optimization_barrier((sent, wa))
    got = swap(sent, "ctx")
    lse = got[:, rows, : 3 * rows].reshape(ctxs, 3, rows).astype(f32)
    lse = lse[:, 0] + lse[:, 1] + lse[:, 2]
    weight = jnp.exp(lse - jnp.max(lse, axis=0))
    weight = weight / jnp.sum(weight, axis=0)
    attended = jnp.sum(got[:, :rows].astype(f32) * weight[:, :, None], axis=0).astype(bf16)

    def summed(partial):
        chunks = partial.astype(bf16).reshape(rows, heads, cols).transpose(1, 0, 2)
        return jnp.sum(swap(chunks, "head").astype(f32), axis=0)

    def all_columns(own):
        return spread(own, "head").transpose(1, 0, 2).reshape(rows, width)

    h_first = (own_raw.astype(f32) + summed(nt(attended, wa[:, :cols]))).astype(bf16)
    n_second = unit_rows(all_columns(h_first), gains[1])
    qkv = nn(n_second, wa[:, cols : 4 * cols]).astype(bf16)
    pair = spread(qkv[:, cols:], "ctx").reshape(latents, 2 * cols)
    own_pos = lax.dynamic_slice_in_dim(last_visible, own_start, rows, 0)
    seen = last_visible[None, :] <= own_pos[:, None]
    score = jnp.where(seen, nt(qkv[:, :cols], pair[:, :cols]) * scale, masked_score)
    prob = jnp.where(seen, jnp.exp(score - jnp.max(score, axis=1, keepdims=True)), 0.0)
    prob = (prob / jnp.sum(prob, axis=1, keepdims=True)).astype(bf16)
    mixed = nn(prob, pair[:, cols:]).astype(bf16)
    h_second = (h_first.astype(f32) + summed(nt(mixed, wlo))).astype(bf16)
    n_third = unit_rows(all_columns(h_second), gains[2])
    ff = w_mlp.shape[2]
    gate_up = nn(n_third, wb[:, : 2 * ff])
    hidden = (jax.nn.silu(gate_up[:, :ff]) * gate_up[:, ff:]).astype(bf16)
    return (h_second.astype(f32) + summed(nt(hidden, wb[:, 2 * ff :]))).astype(bf16)


def solution(mesh):
    in_specs = (
        P("ctx", None),
        P(None, "ctx", "head"),
        P("head", "ctx"),
        P(None, "ctx", "head"),
        P("head", "ctx"),
        P(None, "ctx", "head"),
        P("head", "ctx"),
        P(),
        P("ctx"),
        P(),
    )
    out_specs = P("ctx", "head")
    return jax.shard_map(body, mesh=mesh, in_specs=in_specs, out_specs=out_specs, check_vma=False)
```

```python
import jax
import jax.numpy as jnp
from jax import lax
from jax.experimental import pallas as pl
from jax.experimental.pallas import tpu as pltpu
from jax.sharding import PartitionSpec as P

HD = 128
epsilon = 1e-05
masked_score = -1e30
score_scale = HD ** (-0.5)
f32 = jnp.float32
bf16 = jnp.bfloat16
TAIL = 16
VMEM = pl.BlockSpec(memory_space=pltpu.VMEM)
SMEM = pl.BlockSpec(memory_space=pltpu.SMEM)


def nt(a, b):
    return lax.dot_general(a, b, (((1,), (1,)), ((), ())), preferred_element_type=f32)


def nn(a, b):
    return jnp.dot(a, b, preferred_element_type=f32)


def call(kernel, out_shape, *args, specs=None, scratch=()):
    return pl.pallas_call(
        kernel,
        grid=(1,),
        out_shape=out_shape,
        in_specs=specs if specs is not None else [VMEM] * len(args),
        out_specs=jax.tree.map(lambda _: VMEM, out_shape),
        scratch_shapes=scratch,
        compiler_params=pltpu.CompilerParams(vmem_limit_bytes=40 * 2**20),
    )(*args)


def part(shape, *index):
    return pl.BlockSpec(shape, lambda i: index)


def pack_kernel(attn_ref, out_w_ref, latent_ref, latent_out_ref, mlp_ref, down_ref, early_ref, late_ref):
    early_ref[:3] = attn_ref[...]
    early_ref[3] = out_w_ref[...]
    blocks = [latent_ref[i] for i in range(3)] + [latent_out_ref[...]]
    blocks += [mlp_ref[0], mlp_ref[1], down_ref[...]]
    at = 0
    for block in blocks:
        late_ref[:, at : at + block.shape[1]] = block
        at += block.shape[1]


def query_kernel(rows_ref, raw_ref, w_ref, out_ref):
    depth = w_ref.shape[2]
    total = nn(rows_ref[:, :depth], w_ref[0, 0])
    for x in range(1, w_ref.shape[0]):
        total += nn(rows_ref[:, x * depth : (x + 1) * depth], w_ref[x, 0])
    count, double, cols = out_ref.shape
    out_ref[:, : double // 2, :] = total.astype(bf16).reshape(count, double // 2, cols)
    out_ref[:, double // 2 :, :] = raw_ref[...].reshape(count, double // 2, cols)


def keyval_kernel(rows_ref, k_w_ref, v_w_ref, key_ref, value_ref):
    depth = k_w_ref.shape[2]
    step = 256

    def tile(i, carry):
        at = pl.ds(pl.multiple_of(i * step, step), step)
        rows = rows_ref[at, :]
        key = nn(rows[:, :depth], k_w_ref[0, 0])
        value = nn(rows[:, :depth], v_w_ref[0, 0])
        for x in range(1, k_w_ref.shape[0]):
            piece = rows[:, x * depth : (x + 1) * depth]
            key += nn(piece, k_w_ref[x, 0])
            value += nn(piece, v_w_ref[x, 0])
        key_ref[at, :] = key.astype(bf16)
        value_ref[:, at] = value.T.astype(bf16)
        return carry

    lax.fori_loop(0, rows_ref.shape[0] // step, tile, 0)


def attend_kernel(info_ref, seen_ref, q_ref, k_ref, v_ref, out_ref):
    keys, cols = k_ref.shape
    count, rows = out_ref.shape[0], out_ref.shape[1] - TAIL
    step = 256
    chunks = step // rows
    key = lax.broadcasted_iota(jnp.int32, (keys, step), 0)
    inside = key < info_ref[0]
    position = key + info_ref[1]
    for t in range(count * rows // step):
        at = slice(t * step, (t + 1) * step)
        kept = inside & (position <= seen_ref[:, at])
        score = jnp.where(kept, nt(k_ref[...], q_ref[at, :]) * score_scale, masked_score)
        top = jnp.max(score, axis=0, keepdims=True)
        prob = jnp.where(kept, jnp.exp(score - top), 0.0)
        total = jnp.sum(prob, axis=0, keepdims=True)
        out = (nn(v_ref[...], prob.astype(bf16)) / total).T.astype(bf16)
        out_ref[t * chunks : (t + 1) * chunks, :rows, :] = out.reshape(chunks, rows, cols)
        lse = top + jnp.log(total)
        high = lse.astype(bf16).astype(f32)
        middle = (lse - high).astype(bf16).astype(f32)
        low = lse - high - middle
        pieces = jnp.concatenate([high, middle, low, jnp.zeros((TAIL - 3, step), f32)])
        pieces = pieces.astype(bf16)
        per = cols // rows
        for g in range(step // cols):
            first = t * chunks + g * per
            out_ref[first : first + per, rows:, :] = jnp.broadcast_to(
                pieces[:, g * cols : (g + 1) * cols][None], (per, TAIL, cols)
            )


def merge_kernel(info_ref, got_ref, w_ref, out_ref):
    count, height, cols = got_ref.shape
    rows = height - TAIL
    lse = jnp.sum(got_ref[:, rows:, :].astype(f32), axis=1)
    weight = jnp.exp(lse - jnp.max(lse, axis=0, keepdims=True))
    weight = (weight / jnp.sum(weight, axis=0, keepdims=True)).T
    own = jnp.zeros((rows, count), f32)
    for i in range(cols // rows):
        own = jnp.where(info_ref[0] == i, weight[i * rows : (i + 1) * rows, :], own)
    total = jnp.zeros((rows, cols), f32)
    for s in range(count):
        total += own[:, s : s + 1] * got_ref[s, :rows, :].astype(f32)
    project(total.astype(bf16), lambda h: w_ref[h // 4, 0, h % 4 * cols : (h % 4 + 1) * cols, :], out_ref)


def project(acts, weight_rows, out_ref):
    for h in range(out_ref.shape[0]):
        out_ref[h] = nt(acts, weight_rows(h)).astype(bf16)


def add_kernel(base_ref, terms_ref, out_ref, wide_ref):
    total = base_ref[...].astype(f32) + jnp.sum(terms_ref[...].astype(f32), axis=0)
    out_ref[...] = total.astype(bf16)
    wide_ref[...] = jnp.broadcast_to(total.astype(bf16)[None], wide_ref.shape)


def last_kernel(base_ref, terms_ref, out_ref):
    total = base_ref[...].astype(f32) + jnp.sum(terms_ref[...].astype(f32), axis=0)
    out_ref[...] = total.astype(bf16)


def unit(all_ref, gain_ref):
    wide = jnp.concatenate([all_ref[h] for h in range(all_ref.shape[0])], axis=1).astype(f32)
    scale = lax.rsqrt(jnp.mean(wide * wide, axis=1, keepdims=True) + epsilon)
    return (wide * scale * gain_ref[...]).astype(bf16)


def latent_kernel(all_ref, gain_ref, w_ref, q_ref, pair_ref):
    qkv = nn(unit(all_ref, gain_ref), w_ref[...]).astype(bf16)
    cols = q_ref.shape[1]
    q_ref[...] = qkv[:, :cols]
    pair_ref[...] = jnp.broadcast_to(qkv[:, cols:][None], pair_ref.shape)


def mix_kernel(own_ref, seen_ref, q_ref, pair_ref, w_ref, out_ref):
    cols = q_ref.shape[1]
    pair = pair_ref[...].reshape(-1, 2 * cols)
    seen = seen_ref[...] <= own_ref[...]
    score = jnp.where(seen, nt(q_ref[...], pair[:, :cols]) * score_scale, masked_score)
    prob = jnp.where(seen, jnp.exp(score - jnp.max(score, axis=1, keepdims=True)), 0.0)
    prob = (prob / jnp.sum(prob, axis=1, keepdims=True)).astype(bf16)
    mixed = nn(prob, pair[:, cols:]).astype(bf16)
    project(mixed, lambda h: w_ref[h * cols : (h + 1) * cols, :], out_ref)


def feed_kernel(all_ref, gain_ref, gate_ref, up_ref, down_ref, out_ref):
    acts = unit(all_ref, gain_ref)
    gate = nn(acts, gate_ref[...])
    hidden = (gate / (1.0 + jnp.exp(-gate)) * nn(acts, up_ref[...])).astype(bf16)
    cols = out_ref.shape[2]
    project(hidden, lambda h: down_ref[h * cols : (h + 1) * cols, :], out_ref)


def swap(x, axis):
    return lax.all_to_all(x, axis, 0, 0)


def body(
    context, w_attn, w_out, w_latent, w_latent_out, w_mlp, w_down, gains, valid_len, last_visible
):
    tokens, width = context.shape
    cols = w_attn.shape[2]
    ff = w_mlp.shape[2]
    latents = last_visible.shape[0]
    ctxs = lax.axis_size("ctx")
    heads = lax.axis_size("head")
    rows = latents // ctxs
    ctx_index = lax.axis_index("ctx")
    shape = jax.ShapeDtypeStruct
    ys = [[i * 8 + j for j in range(8)] for i in range(4)]
    xs = [[i * 8 + j for i in range(4)] for j in range(8)]

    piece = w_attn.shape[1]
    early, late = call(
        pack_kernel,
        (shape((4, piece, cols), bf16), shape((piece, 4 * cols + 3 * ff), bf16)),
        w_attn, w_out.T, w_latent, w_latent_out.T, w_mlp, w_down.T,
    )
    late = lax.all_gather(late, "ctx", axis=0, tiled=True)

    near = lax.all_gather(early, "ctx", axis=1, tiled=True, axis_index_groups=ys)
    far = lax.all_to_all(
        jnp.broadcast_to(near[None], (4,) + near.shape), "ctx", 0, 0, axis_index_groups=xs
    )
    kind = (4, 1, 8 * piece, cols)

    pick = jnp.clip(last_visible - (ctxs - 1) * tokens, 0, tokens - 1)
    mine = lax.dynamic_slice_in_dim(context, lax.axis_index("head") * cols, cols, 1)
    raw = jnp.take(mine, pick, axis=0)
    wide = context.astype(f32)
    normed = wide * lax.rsqrt(jnp.mean(wide * wide, axis=-1, keepdims=True) + epsilon) * gains[0]
    normed = normed.astype(bf16)
    source = jnp.take(normed, pick, axis=0)

    sent = call(
        query_kernel,
        shape((ctxs, 2 * rows, cols), bf16),
        source, raw, far,
        specs=[VMEM, VMEM, part(kind, 0, 0, 0, 0)],
    )
    got = swap(sent, "ctx")[ctxs - 1]
    own_raw = got[rows:]
    queries = swap(jnp.broadcast_to(got[None, :rows], (ctxs, rows, cols)), "ctx")
    keys, values = call(
        keyval_kernel,
        (shape((tokens, cols), bf16), shape((cols, tokens), bf16)),
        normed, far, far,
        specs=[VMEM, part(kind, 0, 1, 0, 0), part(kind, 0, 2, 0, 0)],
    )

    info = jnp.stack([valid_len[0], ctx_index * tokens])
    seen = last_visible.reshape(1, latents)
    sent = call(
        attend_kernel,
        shape((ctxs, rows + TAIL, cols), bf16),
        info, seen, queries.reshape(latents, cols), keys, values,
        specs=[SMEM, VMEM, VMEM, VMEM, VMEM],
    )
    got = swap(sent, "ctx")
    spot = lax.rem(ctx_index, cols // rows).reshape(1)
    chunk = shape((heads, rows, cols), bf16)
    own = shape((rows, cols), bf16)
    terms = call(
        merge_kernel, chunk, spot, got, far, specs=[SMEM, VMEM, part(kind, 0, 3, 0, 0)]
    )
    first, wide = call(add_kernel, (own, chunk), own_raw, swap(terms, "head"))
    query, pair = call(
        latent_kernel,
        (own, shape((ctxs, rows, 2 * cols), bf16)),
        swap(wide, "head"), gains[1:2], late,
        specs=[VMEM, VMEM, part((width, 3 * cols), 0, 0)],
    )
    place = lax.dynamic_slice_in_dim(last_visible, ctx_index * rows, rows, 0).reshape(rows, 1)
    terms = call(
        mix_kernel,
        chunk,
        place, seen, query, swap(pair, "ctx"), late,
        specs=[VMEM, VMEM, VMEM, VMEM, part((width, cols), 0, 3)],
    )
    second, wide = call(add_kernel, (own, chunk), first, swap(terms, "head"))
    terms = call(
        feed_kernel,
        chunk,
        swap(wide, "head"), gains[2:3], late, late, late,
        specs=[VMEM, VMEM] + [part((width, ff), 0, i) for i in (1, 2, 3)],
    )
    return call(last_kernel, own, second, swap(terms, "head"))


def solution(mesh):
    in_specs = (
        P("ctx", None),
        P(None, "ctx", "head"),
        P("head", "ctx"),
        P(None, "ctx", "head"),
        P("head", "ctx"),
        P(None, "ctx", "head"),
        P("head", "ctx"),
        P(),
        P("ctx"),
        P(),
    )
    out_specs = P("ctx", "head")
    return jax.shard_map(body, mesh=mesh, in_specs=in_specs, out_specs=out_specs, check_vma=False)
```

```python
import jax
import jax.numpy as jnp
from jax import lax
from jax.experimental import pallas as pl
from jax.experimental.pallas import tpu as pltpu
from jax.sharding import PartitionSpec as P

HD = 128
epsilon = 1e-05
masked_score = -1e30
score_scale = HD ** (-0.5)
f32 = jnp.float32
bf16 = jnp.bfloat16
TAIL = 8
LATE = 55
VMEM = pl.BlockSpec(memory_space=pltpu.VMEM)
SMEM = pl.BlockSpec(memory_space=pltpu.SMEM)


def nt(a, b):
    return lax.dot_general(a, b, (((1,), (1,)), ((), ())), preferred_element_type=f32)


def nn(a, b):
    return jnp.dot(a, b, preferred_element_type=f32)


def call(kernel, out_shape, *args, specs=None, outs=None, grid=(1,), room=16):
    return pl.pallas_call(
        kernel,
        grid=grid,
        out_shape=out_shape,
        in_specs=specs if specs is not None else [VMEM] * len(args),
        out_specs=outs if outs is not None else jax.tree.map(lambda _: VMEM, out_shape),
        compiler_params=pltpu.CompilerParams(vmem_limit_bytes=room * 2**20),
    )(*args)


def part(shape, *index):
    return pl.BlockSpec(shape, lambda i: index)


def pack_kernel(attn_ref, out_w_ref, latent_ref, latent_out_ref, mlp_ref, down_ref, early_ref, late_ref):
    early_ref[:3] = attn_ref[...]
    early_ref[3] = out_w_ref[...]
    blocks = [latent_ref[i] for i in range(3)] + [latent_out_ref[...]]
    blocks += [mlp_ref[0], mlp_ref[1], down_ref[...]]
    at = 0
    for block in blocks:
        late_ref[:, at : at + block.shape[1]] = block
        at += block.shape[1]


def whole(x):
    return part(x.shape, *[0] * x.ndim)


def unit_rows(rows, gain):
    wide = rows.astype(f32)
    scale = lax.rsqrt(jnp.mean(wide * wide, axis=1, keepdims=True) + epsilon)
    return (wide * scale * gain).astype(bf16)


def by_parts(rows, w_ref):
    depth = w_ref.shape[2]
    total = nn(rows[:, :depth], w_ref[0, 0])
    for x in range(1, w_ref.shape[0]):
        total += nn(rows[:, x * depth : (x + 1) * depth], w_ref[x, 0])
    return total


def query_kernel(rows_ref, gain_ref, w_ref, out_ref):
    query = by_parts(unit_rows(rows_ref[...], gain_ref[...]), w_ref).astype(bf16)
    out_ref[...] = jnp.broadcast_to(query[None], out_ref.shape)


def keyval_kernel(rows_ref, gain_ref, k_w_ref, v_w_ref, key_ref, value_ref):
    rows = unit_rows(rows_ref[...], gain_ref[...])
    key_ref[...] = by_parts(rows, k_w_ref).astype(bf16)
    value_ref[...] = by_parts(rows, v_w_ref).T.astype(bf16)


def attend_kernel(info_ref, seen_ref, q_ref, k_ref, v_ref, out_ref):
    keys, cols = k_ref.shape
    count, rows = out_ref.shape[0], out_ref.shape[1] - TAIL
    step = 256
    chunks = step // rows
    key = lax.broadcasted_iota(jnp.int32, (keys, step), 0)
    inside = key < info_ref[0]
    position = key + info_ref[1]
    for t in range(count * rows // step):
        at = slice(t * step, (t + 1) * step)
        kept = inside & (position <= seen_ref[:, at])
        score = jnp.where(kept, nt(k_ref[...], q_ref[at, :]) * score_scale, masked_score)
        top = jnp.max(score, axis=0, keepdims=True)
        prob = jnp.where(kept, jnp.exp(score - top), 0.0)
        total = jnp.sum(prob, axis=0, keepdims=True)
        out = (nn(v_ref[...], prob.astype(bf16)) / total).T
        out = out.reshape(chunks, rows, cols)
        lse = top + jnp.log(total)
        high = lse.astype(bf16).astype(f32)
        middle = (lse - high).astype(bf16).astype(f32)
        low = lse - high - middle
        pieces = jnp.concatenate([high, middle, low, jnp.zeros((TAIL - 3, step), f32)])
        per = cols // rows
        for g in range(chunks):
            tail = pieces[:, g // per * cols : (g // per + 1) * cols]
            out_ref[t * chunks + g] = jnp.concatenate([out[g], tail]).astype(bf16)


def merge_kernel(info_ref, got_ref, w_ref, out_ref):
    count, height, cols = got_ref.shape
    rows = height - TAIL
    got = got_ref[...].astype(f32)
    lse = jnp.sum(got[:, rows:, :], axis=1)
    weight = jnp.exp(lse - jnp.max(lse, axis=0, keepdims=True))
    weight = (weight / jnp.sum(weight, axis=0, keepdims=True)).T
    own = jnp.zeros((rows, count), f32)
    for i in range(cols // rows):
        own = jnp.where(info_ref[0] == i, weight[i * rows : (i + 1) * rows, :], own)
    total = jnp.zeros((rows, cols), f32)
    for s in range(count):
        total += own[:, s : s + 1] * got[s, :rows, :]
    project(total.astype(bf16), lambda h: w_ref[h // 4, 0, h % 4 * cols : (h % 4 + 1) * cols, :], out_ref)


def project(acts, weight_rows, out_ref):
    for h in range(out_ref.shape[0]):
        out_ref[h] = nt(acts, weight_rows(h)).astype(bf16)


def add_kernel(base_ref, terms_ref, out_ref, wide_ref):
    total = base_ref[...].astype(f32) + jnp.sum(terms_ref[...].astype(f32), axis=0)
    out_ref[...] = total.astype(bf16)
    wide_ref[...] = jnp.broadcast_to(total.astype(bf16)[None], wide_ref.shape)


def last_kernel(base_ref, terms_ref, out_ref):
    total = base_ref[...].astype(f32) + jnp.sum(terms_ref[...].astype(f32), axis=0)
    out_ref[...] = total.astype(bf16)


def unit(all_ref, gain_ref):
    rows = jnp.concatenate([all_ref[h] for h in range(all_ref.shape[0])], axis=1)
    return unit_rows(rows, gain_ref[...])


def latent_kernel(all_ref, gain_ref, w_ref, q_ref, pair_ref):
    qkv = nn(unit(all_ref, gain_ref), w_ref[...]).astype(bf16)
    cols = q_ref.shape[1]
    q_ref[...] = qkv[:, :cols]
    pair_ref[...] = jnp.broadcast_to(qkv[:, cols:][None], pair_ref.shape)


def mix_kernel(own_ref, seen_ref, q_ref, pair_ref, w_ref, out_ref):
    cols = q_ref.shape[1]
    pair = pair_ref[...].reshape(-1, 2 * cols)
    seen = seen_ref[...] <= own_ref[...]
    score = jnp.where(seen, nt(q_ref[...], pair[:, :cols]) * score_scale, masked_score)
    prob = jnp.where(seen, jnp.exp(score - jnp.max(score, axis=1, keepdims=True)), 0.0)
    prob = (prob / jnp.sum(prob, axis=1, keepdims=True)).astype(bf16)
    mixed = nn(prob, pair[:, cols:]).astype(bf16)
    project(mixed, lambda h: w_ref[h * cols : (h + 1) * cols, :], out_ref)


def feed_kernel(all_ref, gain_ref, gate_ref, up_ref, down_ref, out_ref):
    acts = unit(all_ref, gain_ref)
    gate = nn(acts, gate_ref[...])
    hidden = (gate / (1.0 + jnp.exp(-gate)) * nn(acts, up_ref[...])).astype(bf16)
    cols = out_ref.shape[2]
    project(hidden, lambda h: down_ref[h * cols : (h + 1) * cols, :], out_ref)


def swap(x, axis):
    return lax.all_to_all(x, axis, 0, 0)


def body(
    context, w_attn, w_out, w_latent, w_latent_out, w_mlp, w_down, gains, valid_len, last_visible
):
    tokens, width = context.shape
    cols = w_attn.shape[2]
    ff = w_mlp.shape[2]
    latents = last_visible.shape[0]
    ctxs = lax.axis_size("ctx")
    heads = lax.axis_size("head")
    rows = latents // ctxs
    ctx_index = lax.axis_index("ctx")
    shape = jax.ShapeDtypeStruct
    ys = [[i * 8 + j for j in range(8)] for i in range(4)]
    xs = [[i * 8 + j for i in range(4)] for j in range(8)]

    piece = w_attn.shape[1]
    pieces = (w_attn, w_out.T, w_latent, w_latent_out.T, w_mlp, w_down.T)
    early, late = call(
        pack_kernel,
        (shape((4, piece, cols), bf16), shape((piece, 4 * cols + 3 * ff), bf16)),
        *pieces,
        specs=[whole(x) for x in pieces],
        outs=(VMEM, part((piece, 4 * cols + 3 * ff), 0, 0)),
        room=LATE,
    )
    late = lax.all_gather(late, "ctx", axis=0, tiled=True)

    near = lax.all_to_all(
        jnp.broadcast_to(early[None], (8,) + early.shape), "ctx", 0, 0, axis_index_groups=ys
    )
    near = near.transpose(1, 0, 2, 3).reshape(4, 8 * piece, cols)
    pick = jnp.clip(last_visible - (ctxs - 1) * tokens, 0, tokens - 1)
    mine = lax.dynamic_slice_in_dim(context, lax.axis_index("head") * cols, cols, 1)
    raw = jnp.take(mine, pick, axis=0, mode="clip").reshape(ctxs, rows, cols)
    near, raw = lax.optimization_barrier((near, raw))
    own_raw = swap(raw, "ctx")[ctxs - 1]
    near, own_raw = lax.optimization_barrier((near, own_raw))
    far = lax.all_to_all(
        jnp.broadcast_to(near[None], (4,) + near.shape), "ctx", 0, 0, axis_index_groups=xs
    )
    kind = (4, 1, 8 * piece, cols)
    raw_rows = lax.all_gather(own_raw, "head", axis=1, tiled=True)
    queries = call(
        query_kernel,
        shape((ctxs, rows, cols), bf16),
        raw_rows, gains[:1], far,
        specs=[VMEM, VMEM, part(kind, 0, 0, 0, 0)],
    )
    queries = swap(queries, "ctx")
    step = 256
    keys, values = call(
        keyval_kernel,
        (shape((tokens, cols), bf16), shape((cols, tokens), bf16)),
        context, gains[:1], far, far,
        specs=[
            pl.BlockSpec((step, width), lambda i: (i, 0)),
            part((1, width), 0, 0),
            part(kind, 0, 1, 0, 0),
            part(kind, 0, 2, 0, 0),
        ],
        outs=(
            pl.BlockSpec((step, cols), lambda i: (i, 0)),
            pl.BlockSpec((cols, step), lambda i: (0, i)),
        ),
        grid=(tokens // step,),
    )

    info = jnp.stack([valid_len[0], ctx_index * tokens])
    seen = last_visible.reshape(1, latents)
    sent = call(
        attend_kernel,
        shape((ctxs, rows + TAIL, cols), bf16),
        info, seen, queries.reshape(latents, cols), keys, values,
        specs=[SMEM, VMEM, VMEM, VMEM, VMEM],
    )
    got = swap(sent, "ctx")
    spot = lax.rem(ctx_index, cols // rows).reshape(1)
    chunk = shape((heads, rows, cols), bf16)
    own = shape((rows, cols), bf16)
    terms = call(
        merge_kernel, chunk, spot, got, far, specs=[SMEM, VMEM, part(kind, 0, 3, 0, 0)]
    )
    first, wide = call(add_kernel, (own, chunk), own_raw, swap(terms, "head"))
    query, pair = call(
        latent_kernel,
        (own, shape((ctxs, rows, 2 * cols), bf16)),
        swap(wide, "head"), gains[1:2], late,
        specs=[VMEM, VMEM, part((width, 3 * cols), 0, 0)],
        room=LATE,
    )
    place = lax.dynamic_slice_in_dim(last_visible, ctx_index * rows, rows, 0).reshape(rows, 1)
    terms = call(
        mix_kernel,
        chunk,
        place, seen, query, swap(pair, "ctx"), late,
        specs=[VMEM, VMEM, VMEM, VMEM, part((width, cols), 0, 3)],
        room=LATE,
    )
    second, wide = call(add_kernel, (own, chunk), first, swap(terms, "head"))
    terms = call(
        feed_kernel,
        chunk,
        swap(wide, "head"), gains[2:3], late, late, late,
        specs=[VMEM, VMEM] + [part((width, ff), 0, i) for i in (1, 2, 3)],
        room=LATE,
    )
    return call(last_kernel, own, second, swap(terms, "head"))


def solution(mesh):
    in_specs = (
        P("ctx", None),
        P(None, "ctx", "head"),
        P("head", "ctx"),
        P(None, "ctx", "head"),
        P("head", "ctx"),
        P(None, "ctx", "head"),
        P("head", "ctx"),
        P(),
        P("ctx"),
        P(),
    )
    out_specs = P("ctx", "head")
    return jax.shard_map(body, mesh=mesh, in_specs=in_specs, out_specs=out_specs, check_vma=False)
```

```python
import jax
import jax.numpy as jnp
from jax import lax
from jax.experimental import pallas as pl
from jax.experimental.pallas import tpu as pltpu
from jax.sharding import PartitionSpec as P

HD = 128
epsilon = 1e-05
masked_score = -1e30
score_scale = HD ** (-0.5)
f32 = jnp.float32
bf16 = jnp.bfloat16
TAIL = 8
LATE = 58
VMEM = pl.BlockSpec(memory_space=pltpu.VMEM)
SMEM = pl.BlockSpec(memory_space=pltpu.SMEM)


def nt(a, b):
    return lax.dot_general(a, b, (((1,), (1,)), ((), ())), preferred_element_type=f32)


def nn(a, b):
    return jnp.dot(a, b, preferred_element_type=f32)


def call(kernel, out_shape, *args, specs=None, outs=None, grid=(1,), room=16):
    return pl.pallas_call(
        kernel,
        grid=grid,
        out_shape=out_shape,
        in_specs=specs if specs is not None else [VMEM] * len(args),
        out_specs=outs if outs is not None else jax.tree.map(lambda _: VMEM, out_shape),
        compiler_params=pltpu.CompilerParams(vmem_limit_bytes=room * 2**20),
    )(*args)


def part(shape, *index):
    return pl.BlockSpec(shape, lambda i: index)


def pack_kernel(attn_ref, out_w_ref, latent_ref, latent_out_ref, mlp_ref, down_ref, early_ref, late_ref):
    blocks = [attn_ref[i] for i in range(3)] + [out_w_ref[...]] + [latent_ref[i] for i in range(3)]
    for i, block in enumerate(blocks):
        early_ref[:, i] = jnp.broadcast_to(block[None], (early_ref.shape[0],) + block.shape)
    at = 0
    for block in (mlp_ref[0], mlp_ref[1], down_ref[...], latent_out_ref[...]):
        late_ref[:, at : at + block.shape[1]] = block
        at += block.shape[1]


def whole(x):
    return part(x.shape, *[0] * x.ndim)


def unit_rows(rows, gain):
    wide = rows.astype(f32)
    scale = lax.rsqrt(jnp.mean(wide * wide, axis=1, keepdims=True) + epsilon)
    return (wide * scale * gain).astype(bf16)


def joined(w_ref):
    return w_ref[...].reshape(-1, w_ref.shape[-1])


def query_kernel(all_ref, gain_ref, w_ref, out_ref):
    query = nn(unit(all_ref, gain_ref), joined(w_ref)).astype(bf16)
    out_ref[...] = jnp.broadcast_to(query[None], out_ref.shape)


def keyval_kernel(rows_ref, gain_ref, k_w_ref, v_w_ref, key_ref, value_ref):
    rows = unit_rows(rows_ref[...], gain_ref[...])
    key_ref[...] = nn(rows, joined(k_w_ref)).astype(bf16)
    value_ref[...] = nn(rows, joined(v_w_ref)).T.astype(bf16)


def attend_kernel(info_ref, seen_ref, q_ref, k_ref, v_ref, out_ref):
    keys, cols = k_ref.shape
    count, rows = out_ref.shape[0], out_ref.shape[1] - TAIL
    step = 256
    chunks = step // rows
    key = lax.broadcasted_iota(jnp.int32, (keys, step), 0)
    inside = key < info_ref[0]
    position = key + info_ref[1]
    for t in range(count * rows // step):
        at = slice(t * step, (t + 1) * step)
        kept = inside & (position <= seen_ref[:, at])
        score = jnp.where(kept, nt(k_ref[...], q_ref[at, :]) * score_scale, masked_score)
        top = jnp.max(score, axis=0, keepdims=True)
        prob = jnp.where(kept, jnp.exp(score - top), 0.0)
        total = jnp.sum(prob, axis=0, keepdims=True)
        out = (nn(v_ref[...], prob.astype(bf16)) / total).T
        out = out.reshape(chunks, rows, cols)
        lse = top + jnp.log(total)
        high = lse.astype(bf16).astype(f32)
        middle = (lse - high).astype(bf16).astype(f32)
        low = lse - high - middle
        pieces = jnp.concatenate([high, middle, low, jnp.zeros((TAIL - 3, step), f32)])
        per = cols // rows
        for g in range(chunks):
            tail = pieces[:, g // per * cols : (g // per + 1) * cols]
            out_ref[t * chunks + g] = jnp.concatenate([out[g], tail]).astype(bf16)


def merge_kernel(info_ref, got_ref, w_ref, out_ref):
    count, height, cols = got_ref.shape
    rows = height - TAIL
    got = got_ref[...].astype(f32)
    lse = jnp.sum(got[:, rows:, :], axis=1)
    weight = jnp.exp(lse - jnp.max(lse, axis=0, keepdims=True))
    weight = (weight / jnp.sum(weight, axis=0, keepdims=True)).T
    own = jnp.zeros((rows, count), f32)
    for i in range(cols // rows):
        own = jnp.where(info_ref[0] == i, weight[i * rows : (i + 1) * rows, :], own)
    total = jnp.zeros((rows, cols), f32)
    for s in range(count):
        total += own[:, s : s + 1] * got[s, :rows, :]
    weight = joined(w_ref)
    project(total.astype(bf16), lambda h: weight[h * cols : (h + 1) * cols], out_ref)


def project(acts, weight_rows, out_ref):
    for h in range(out_ref.shape[0]):
        out_ref[h] = nt(acts, weight_rows(h)).astype(bf16)


def add_kernel(base_ref, terms_ref, out_ref, wide_ref):
    total = base_ref[...].astype(f32) + jnp.sum(terms_ref[...].astype(f32), axis=0)
    out_ref[...] = total.astype(bf16)
    wide_ref[...] = jnp.broadcast_to(total.astype(bf16)[None], wide_ref.shape)


def last_kernel(base_ref, terms_ref, out_ref):
    total = base_ref[...].astype(f32) + jnp.sum(terms_ref[...].astype(f32), axis=0)
    out_ref[...] = total.astype(bf16)


def unit(all_ref, gain_ref):
    rows = jnp.concatenate([all_ref[h] for h in range(all_ref.shape[0])], axis=1)
    return unit_rows(rows, gain_ref[...])


def latent_kernel(all_ref, gain_ref, q_w_ref, k_w_ref, v_w_ref, q_ref, pair_ref):
    rows = unit(all_ref, gain_ref)
    q_ref[...] = nn(rows, joined(q_w_ref)).astype(bf16)
    pair = [nn(rows, joined(w_ref)).astype(bf16) for w_ref in (k_w_ref, v_w_ref)]
    pair_ref[...] = jnp.broadcast_to(jnp.concatenate(pair, axis=1)[None], pair_ref.shape)


def mix_kernel(own_ref, seen_ref, q_ref, pair_ref, w_ref, out_ref):
    cols = q_ref.shape[1]
    pair = pair_ref[...].reshape(-1, 2 * cols)
    seen = seen_ref[...] <= own_ref[...]
    score = jnp.where(seen, nt(q_ref[...], pair[:, :cols]) * score_scale, masked_score)
    prob = jnp.where(seen, jnp.exp(score - jnp.max(score, axis=1, keepdims=True)), 0.0)
    prob = (prob / jnp.sum(prob, axis=1, keepdims=True)).astype(bf16)
    mixed = nn(prob, pair[:, cols:]).astype(bf16)
    project(mixed, lambda h: w_ref[h * cols : (h + 1) * cols, :], out_ref)


def feed_kernel(all_ref, gain_ref, gate_ref, up_ref, down_ref, out_ref):
    acts = unit(all_ref, gain_ref)
    gate = nn(acts, gate_ref[...])
    hidden = (gate / (1.0 + jnp.exp(-gate)) * nn(acts, up_ref[...])).astype(bf16)
    cols = out_ref.shape[2]
    project(hidden, lambda h: down_ref[h * cols : (h + 1) * cols, :], out_ref)


def swap(x, axis):
    return lax.all_to_all(x, axis, 0, 0)


def body(
    context, w_attn, w_out, w_latent, w_latent_out, w_mlp, w_down, gains, valid_len, last_visible
):
    tokens, width = context.shape
    cols = w_attn.shape[2]
    ff = w_mlp.shape[2]
    latents = last_visible.shape[0]
    ctxs = lax.axis_size("ctx")
    heads = lax.axis_size("head")
    rows = latents // ctxs
    ctx_index = lax.axis_index("ctx")
    shape = jax.ShapeDtypeStruct
    ys = [[i * 8 + j for j in range(8)] for i in range(4)]
    xs = [[i * 8 + j for i in range(4)] for j in range(8)]

    piece = w_attn.shape[1]
    pieces = (w_attn, w_out.T, w_latent, w_latent_out.T, w_mlp, w_down.T)
    early, late = call(
        pack_kernel,
        (shape((8, 7, piece, cols), bf16), shape((piece, cols + 3 * ff), bf16)),
        *pieces,
        specs=[whole(x) for x in pieces],
        outs=(VMEM, part((piece, cols + 3 * ff), 0, 0)),
        room=LATE,
    )
    near = lax.all_to_all(early, "ctx", 0, 0, axis_index_groups=ys)
    far = lax.all_gather(near, "ctx", axis_index_groups=xs)
    kinds = [part((4, 8, 1, piece, cols), 0, 0, i, 0, 0) for i in range(7)]

    pick = jnp.clip(last_visible - (ctxs - 1) * tokens, 0, tokens - 1)
    mine = lax.dynamic_slice_in_dim(context, lax.axis_index("head") * cols, cols, 1)
    raw = jnp.take(mine, pick, axis=0, mode="clip").reshape(ctxs, rows, cols)
    _, raw = lax.optimization_barrier((near, raw))
    own_raw = swap(raw, "ctx")[ctxs - 1]
    chunk = shape((heads, rows, cols), bf16)
    all_raw = swap(jnp.broadcast_to(own_raw[None], chunk.shape), "head")

    late, far, all_raw = lax.optimization_barrier((late, far, all_raw))
    late = lax.all_gather(late, "ctx", axis=0, tiled=True)

    queries = call(
        query_kernel,
        shape((ctxs, rows, cols), bf16),
        all_raw, gains[:1], far,
        specs=[VMEM, VMEM, kinds[0]],
        room=LATE,
    )
    queries = swap(queries, "ctx")
    step = 256
    keys, values = call(
        keyval_kernel,
        (shape((tokens, cols), bf16), shape((cols, tokens), bf16)),
        context, gains[:1], far, far,
        specs=[
            pl.BlockSpec((step, width), lambda i: (i, 0)),
            part((1, width), 0, 0),
            kinds[1],
            kinds[2],
        ],
        outs=(
            pl.BlockSpec((step, cols), lambda i: (i, 0)),
            pl.BlockSpec((cols, step), lambda i: (0, i)),
        ),
        grid=(tokens // step,),
    )

    info = jnp.stack([valid_len[0], ctx_index * tokens])
    seen = last_visible.reshape(1, latents)
    sent = call(
        attend_kernel,
        shape((ctxs, rows + TAIL, cols), bf16),
        info, seen, queries.reshape(latents, cols), keys, values,
        specs=[SMEM, VMEM, VMEM, VMEM, VMEM],
    )
    got = swap(sent, "ctx")
    spot = lax.rem(ctx_index, cols // rows).reshape(1)
    own = shape((rows, cols), bf16)
    terms = call(
        merge_kernel, chunk, spot, got, far, specs=[SMEM, VMEM, kinds[3]], room=LATE
    )
    first, wide = call(add_kernel, (own, chunk), own_raw, swap(terms, "head"))
    query, pair = call(
        latent_kernel,
        (own, shape((ctxs, rows, 2 * cols), bf16)),
        swap(wide, "head"), gains[1:2], far, far, far,
        specs=[VMEM, VMEM] + kinds[4:],
        room=LATE,
    )
    place = lax.dynamic_slice_in_dim(last_visible, ctx_index * rows, rows, 0).reshape(rows, 1)
    terms = call(
        mix_kernel,
        chunk,
        place, seen, query, swap(pair, "ctx"), late,
        specs=[VMEM, VMEM, VMEM, VMEM, part((width, cols), 0, 3 * ff // cols)],
        room=LATE,
    )
    second, wide = call(add_kernel, (own, chunk), first, swap(terms, "head"))
    terms = call(
        feed_kernel,
        chunk,
        swap(wide, "head"), gains[2:3], late, late, late,
        specs=[VMEM, VMEM] + [part((width, ff), 0, i) for i in range(3)],
        room=LATE,
    )
    return call(last_kernel, own, second, swap(terms, "head"))


def solution(mesh):
    in_specs = (
        P("ctx", None),
        P(None, "ctx", "head"),
        P("head", "ctx"),
        P(None, "ctx", "head"),
        P("head", "ctx"),
        P(None, "ctx", "head"),
        P("head", "ctx"),
        P(),
        P("ctx"),
        P(),
    )
    out_specs = P("ctx", "head")
    return jax.shard_map(body, mesh=mesh, in_specs=in_specs, out_specs=out_specs, check_vma=False)
```

```python
import jax
import jax.numpy as jnp
from jax import lax
from jax.experimental import pallas as pl
from jax.experimental.pallas import tpu as pltpu
from jax.sharding import PartitionSpec as P

HD = 128
epsilon = 1e-05
masked_score = -1e30
score_scale = HD ** (-0.5)
f32 = jnp.float32
bf16 = jnp.bfloat16
TAIL = 8
LATE = 58
VMEM = pl.BlockSpec(memory_space=pltpu.VMEM)
SMEM = pl.BlockSpec(memory_space=pltpu.SMEM)


def nt(a, b):
    return lax.dot_general(a, b, (((1,), (1,)), ((), ())), preferred_element_type=f32)


def nn(a, b):
    return jnp.dot(a, b, preferred_element_type=f32)


def call(kernel, out_shape, *args, specs=None, outs=None, grid=(1,), room=16):
    return pl.pallas_call(
        kernel,
        grid=grid,
        out_shape=out_shape,
        in_specs=specs if specs is not None else [VMEM] * len(args),
        out_specs=outs if outs is not None else jax.tree.map(lambda _: VMEM, out_shape),
        compiler_params=pltpu.CompilerParams(vmem_limit_bytes=room * 2**20),
    )(*args)


def part(shape, *index):
    return pl.BlockSpec(shape, lambda i: index)


def pack_kernel(attn_ref, out_w_ref, latent_ref, latent_out_ref, mlp_ref, down_ref, early_ref, mid_ref, late_ref):
    for i, block in enumerate([attn_ref[0], attn_ref[1], attn_ref[2], out_w_ref[...]]):
        early_ref[:, i] = jnp.broadcast_to(block[None], (early_ref.shape[0],) + block.shape)
    for ref, blocks in (
        (mid_ref, [latent_ref[0], latent_ref[1], latent_ref[2], latent_out_ref[...]]),
        (late_ref, [mlp_ref[0], mlp_ref[1], down_ref[...]]),
    ):
        size = blocks[0].shape[1]
        for i, block in enumerate(blocks):
            ref[:, i * size : (i + 1) * size] = block


def whole(x):
    return part(x.shape, *[0] * x.ndim)


def unit_rows(rows, gain):
    wide = rows.astype(f32)
    scale = lax.rsqrt(jnp.mean(wide * wide, axis=1, keepdims=True) + epsilon)
    return (wide * scale * gain).astype(bf16)


def joined(w_ref):
    return w_ref[...].reshape(-1, w_ref.shape[-1])


def query_kernel(rows_ref, gain_ref, w_ref, out_ref):
    query = nn(unit_rows(rows_ref[...], gain_ref[...]), joined(w_ref)).astype(bf16)
    out_ref[...] = jnp.broadcast_to(query[None], out_ref.shape)


def keyval_kernel(rows_ref, gain_ref, k_w_ref, v_w_ref, key_ref, value_ref):
    rows = unit_rows(rows_ref[...], gain_ref[...])
    key_ref[...] = nn(rows, joined(k_w_ref)).astype(bf16)
    value_ref[...] = nn(rows, joined(v_w_ref)).T.astype(bf16)


def attend_kernel(info_ref, seen_ref, q_ref, k_ref, v_ref, out_ref):
    keys, cols = k_ref.shape
    count, rows = out_ref.shape[0], out_ref.shape[1] - TAIL
    step = 256
    chunks = step // rows
    key = lax.broadcasted_iota(jnp.int32, (keys, step), 0)
    inside = key < info_ref[0]
    position = key + info_ref[1]
    for t in range(count * rows // step):
        at = slice(t * step, (t + 1) * step)
        kept = inside & (position <= seen_ref[:, at])
        score = jnp.where(kept, nt(k_ref[...], q_ref[at, :]) * score_scale, masked_score)
        top = jnp.max(score, axis=0, keepdims=True)
        prob = jnp.where(kept, jnp.exp(score - top), 0.0)
        total = jnp.sum(prob, axis=0, keepdims=True)
        out = (nn(v_ref[...], prob.astype(bf16)) / total).T
        out = out.reshape(chunks, rows, cols)
        lse = top + jnp.log(total)
        high = lse.astype(bf16).astype(f32)
        middle = (lse - high).astype(bf16).astype(f32)
        low = lse - high - middle
        pieces = jnp.concatenate([high, middle, low, jnp.zeros((TAIL - 3, step), f32)])
        per = cols // rows
        for g in range(chunks):
            tail = pieces[:, g // per * cols : (g // per + 1) * cols]
            out_ref[t * chunks + g] = jnp.concatenate([out[g], tail]).astype(bf16)


def merge_kernel(info_ref, got_ref, w_ref, out_ref):
    count, height, cols = got_ref.shape
    rows = height - TAIL
    got = got_ref[...].astype(f32)
    lse = jnp.sum(got[:, rows:, :], axis=1)
    weight = jnp.exp(lse - jnp.max(lse, axis=0, keepdims=True))
    weight = (weight / jnp.sum(weight, axis=0, keepdims=True)).T
    own = jnp.zeros((rows, count), f32)
    for i in range(cols // rows):
        own = jnp.where(info_ref[0] == i, weight[i * rows : (i + 1) * rows, :], own)
    total = jnp.zeros((rows, cols), f32)
    for s in range(count):
        total += own[:, s : s + 1] * got[s, :rows, :]
    weight = joined(w_ref)
    project(total.astype(bf16), lambda h: weight[h * cols : (h + 1) * cols], out_ref)


def project(acts, weight_rows, out_ref):
    for h in range(out_ref.shape[0]):
        out_ref[h] = nt(acts, weight_rows(h)).astype(bf16)


def add_kernel(base_ref, terms_ref, out_ref, wide_ref):
    total = base_ref[...].astype(f32) + jnp.sum(terms_ref[...].astype(f32), axis=0)
    out_ref[...] = total.astype(bf16)
    wide_ref[...] = jnp.broadcast_to(total.astype(bf16)[None], wide_ref.shape)


def last_kernel(base_ref, terms_ref, out_ref):
    total = base_ref[...].astype(f32) + jnp.sum(terms_ref[...].astype(f32), axis=0)
    out_ref[...] = total.astype(bf16)


def unit(all_ref, gain_ref):
    rows = jnp.concatenate([all_ref[h] for h in range(all_ref.shape[0])], axis=1)
    return unit_rows(rows, gain_ref[...])


def latent_kernel(all_ref, gain_ref, w_ref, q_ref, pair_ref):
    qkv = nn(unit(all_ref, gain_ref), w_ref[...]).astype(bf16)
    cols = q_ref.shape[1]
    q_ref[...] = qkv[:, :cols]
    pair_ref[...] = jnp.broadcast_to(qkv[:, cols:][None], pair_ref.shape)


def mix_kernel(own_ref, seen_ref, q_ref, pair_ref, w_ref, out_ref):
    cols = q_ref.shape[1]
    pair = pair_ref[...].reshape(-1, 2 * cols)
    seen = seen_ref[...] <= own_ref[...]
    score = jnp.where(seen, nt(q_ref[...], pair[:, :cols]) * score_scale, masked_score)
    prob = jnp.where(seen, jnp.exp(score - jnp.max(score, axis=1, keepdims=True)), 0.0)
    prob = (prob / jnp.sum(prob, axis=1, keepdims=True)).astype(bf16)
    mixed = nn(prob, pair[:, cols:]).astype(bf16)
    project(mixed, lambda h: w_ref[h * cols : (h + 1) * cols, :], out_ref)


def feed_kernel(all_ref, gain_ref, gate_ref, up_ref, down_ref, out_ref):
    acts = unit(all_ref, gain_ref)
    gate = nn(acts, gate_ref[...])
    hidden = (gate / (1.0 + jnp.exp(-gate)) * nn(acts, up_ref[...])).astype(bf16)
    cols = out_ref.shape[2]
    project(hidden, lambda h: down_ref[h * cols : (h + 1) * cols, :], out_ref)


def swap(x, axis):
    return lax.all_to_all(x, axis, 0, 0)


def body(
    context, w_attn, w_out, w_latent, w_latent_out, w_mlp, w_down, gains, valid_len, last_visible
):
    tokens, width = context.shape
    cols = w_attn.shape[2]
    ff = w_mlp.shape[2]
    latents = last_visible.shape[0]
    ctxs = lax.axis_size("ctx")
    heads = lax.axis_size("head")
    rows = latents // ctxs
    ctx_index = lax.axis_index("ctx")
    shape = jax.ShapeDtypeStruct
    ys = [[i * 8 + j for j in range(8)] for i in range(4)]
    xs = [[i * 8 + j for i in range(4)] for j in range(8)]

    piece = w_attn.shape[1]
    pieces = (w_attn, w_out.T, w_latent, w_latent_out.T, w_mlp, w_down.T)
    early, mid, late = call(
        pack_kernel,
        (
            shape((8, 4, piece, cols), bf16),
            shape((piece, 4 * cols), bf16),
            shape((piece, 3 * ff), bf16),
        ),
        *pieces,
        specs=[whole(x) for x in pieces],
        outs=(VMEM, part((piece, 4 * cols), 0, 0), part((piece, 3 * ff), 0, 0)),
        room=LATE,
    )
    mid = lax.all_gather(mid, "ctx", axis=0, tiled=True)

    near = lax.all_to_all(early, "ctx", 0, 0, axis_index_groups=ys)
    pick = jnp.clip(last_visible - (ctxs - 1) * tokens, 0, tokens - 1)
    mine = lax.dynamic_slice_in_dim(context, lax.axis_index("head") * cols, cols, 1)
    raw = jnp.take(mine, pick, axis=0, mode="clip").reshape(ctxs, rows, cols)
    near, late, raw = lax.optimization_barrier((near, late, raw))
    late = lax.all_gather(late, "ctx", axis=0, tiled=True)
    own_raw = swap(raw, "ctx")[ctxs - 1]
    near, own_raw = lax.optimization_barrier((near, own_raw))
    far = lax.all_to_all(
        jnp.broadcast_to(near[None], (4,) + near.shape), "ctx", 0, 0, axis_index_groups=xs
    )
    kinds = [part((4, 8, 1, piece, cols), 0, 0, i, 0, 0) for i in range(4)]
    raw_rows = lax.all_gather(own_raw, "head", axis=1, tiled=True)
    queries = call(
        query_kernel,
        shape((ctxs, rows, cols), bf16),
        raw_rows, gains[:1], far,
        specs=[VMEM, VMEM, kinds[0]],
    )
    queries = swap(queries, "ctx")
    step = 256
    keys, values = call(
        keyval_kernel,
        (shape((tokens, cols), bf16), shape((cols, tokens), bf16)),
        context, gains[:1], far, far,
        specs=[
            pl.BlockSpec((step, width), lambda i: (i, 0)),
            part((1, width), 0, 0),
            kinds[1],
            kinds[2],
        ],
        outs=(
            pl.BlockSpec((step, cols), lambda i: (i, 0)),
            pl.BlockSpec((cols, step), lambda i: (0, i)),
        ),
        grid=(tokens // step,),
    )

    info = jnp.stack([valid_len[0], ctx_index * tokens])
    seen = last_visible.reshape(1, latents)
    sent = call(
        attend_kernel,
        shape((ctxs, rows + TAIL, cols), bf16),
        info, seen, queries.reshape(latents, cols), keys, values,
        specs=[SMEM, VMEM, VMEM, VMEM, VMEM],
    )
    got = swap(sent, "ctx")
    spot = lax.rem(ctx_index, cols // rows).reshape(1)
    chunk = shape((heads, rows, cols), bf16)
    own = shape((rows, cols), bf16)
    terms = call(
        merge_kernel, chunk, spot, got, far, specs=[SMEM, VMEM, kinds[3]]
    )
    first, wide = call(add_kernel, (own, chunk), own_raw, swap(terms, "head"))
    query, pair = call(
        latent_kernel,
        (own, shape((ctxs, rows, 2 * cols), bf16)),
        swap(wide, "head"), gains[1:2], mid,
        specs=[VMEM, VMEM, part((width, 3 * cols), 0, 0)],
        room=LATE,
    )
    place = lax.dynamic_slice_in_dim(last_visible, ctx_index * rows, rows, 0).reshape(rows, 1)
    terms = call(
        mix_kernel,
        chunk,
        place, seen, query, swap(pair, "ctx"), mid,
        specs=[VMEM, VMEM, VMEM, VMEM, part((width, cols), 0, 3)],
        room=LATE,
    )
    second, wide = call(add_kernel, (own, chunk), first, swap(terms, "head"))
    terms = call(
        feed_kernel,
        chunk,
        swap(wide, "head"), gains[2:3], late, late, late,
        specs=[VMEM, VMEM] + [part((width, ff), 0, i) for i in range(3)],
        room=LATE,
    )
    return call(last_kernel, own, second, swap(terms, "head"))


def solution(mesh):
    in_specs = (
        P("ctx", None),
        P(None, "ctx", "head"),
        P("head", "ctx"),
        P(None, "ctx", "head"),
        P("head", "ctx"),
        P(None, "ctx", "head"),
        P("head", "ctx"),
        P(),
        P("ctx"),
        P(),
    )
    out_specs = P("ctx", "head")
    return jax.shard_map(body, mesh=mesh, in_specs=in_specs, out_specs=out_specs, check_vma=False)
```

```python
import jax
import jax.numpy as jnp
from jax import lax
from jax.experimental import pallas as pl
from jax.experimental.pallas import tpu as pltpu
from jax.sharding import PartitionSpec as P

HD = 128
epsilon = 1e-05
masked_score = -1e30
score_scale = HD ** (-0.5)
f32 = jnp.float32
bf16 = jnp.bfloat16
TAIL = 8
LATE = 58
VMEM = pl.BlockSpec(memory_space=pltpu.VMEM)
SMEM = pl.BlockSpec(memory_space=pltpu.SMEM)


def nt(a, b):
    return lax.dot_general(a, b, (((1,), (1,)), ((), ())), preferred_element_type=f32)


def nn(a, b):
    return jnp.dot(a, b, preferred_element_type=f32)


def call(kernel, out_shape, *args, specs=None, outs=None, grid=(1,), room=16):
    return pl.pallas_call(
        kernel,
        grid=grid,
        out_shape=out_shape,
        in_specs=specs if specs is not None else [VMEM] * len(args),
        out_specs=outs if outs is not None else jax.tree.map(lambda _: VMEM, out_shape),
        compiler_params=pltpu.CompilerParams(vmem_limit_bytes=room * 2**20),
    )(*args)


def part(shape, *index):
    return pl.BlockSpec(shape, lambda i: index)


def pack_kernel(attn_ref, out_w_ref, latent_ref, latent_out_ref, mlp_ref, down_ref, early_ref, mid_ref, late_ref):
    for i, block in enumerate([attn_ref[0], attn_ref[1], attn_ref[2]]):
        early_ref[:, i] = jnp.broadcast_to(block[None], (early_ref.shape[0],) + block.shape)
    for ref, blocks in (
        (mid_ref, [down_ref[...]] + [latent_ref[i] for i in range(3)] + [latent_out_ref[...], out_w_ref[...]]),
        (late_ref, [mlp_ref[0], mlp_ref[1]]),
    ):
        at = 0
        for block in blocks:
            ref[:, at : at + block.shape[1]] = block
            at += block.shape[1]


def whole(x):
    return part(x.shape, *[0] * x.ndim)


def unit_rows(rows, gain):
    wide = rows.astype(f32)
    scale = lax.rsqrt(jnp.mean(wide * wide, axis=1, keepdims=True) + epsilon)
    return (wide * scale * gain).astype(bf16)


def joined(w_ref):
    return w_ref[...].reshape(-1, w_ref.shape[-1])


def query_kernel(rows_ref, gain_ref, w_ref, out_ref):
    query = nn(unit_rows(rows_ref[...], gain_ref[...]), joined(w_ref)).astype(bf16)
    out_ref[...] = jnp.broadcast_to(query[None], out_ref.shape)


def keyval_kernel(rows_ref, gain_ref, k_w_ref, v_w_ref, key_ref, value_ref):
    rows = unit_rows(rows_ref[...], gain_ref[...])
    key_ref[...] = nn(rows, joined(k_w_ref)).astype(bf16)
    value_ref[...] = nn(rows, joined(v_w_ref)).T.astype(bf16)


def attend_kernel(info_ref, seen_ref, q_ref, k_ref, v_ref, out_ref):
    keys, cols = k_ref.shape
    count, rows = out_ref.shape[0], out_ref.shape[1] - TAIL
    step = 256
    chunks = step // rows
    key = lax.broadcasted_iota(jnp.int32, (keys, step), 0)
    inside = key < info_ref[0]
    position = key + info_ref[1]
    for t in range(count * rows // step):
        at = slice(t * step, (t + 1) * step)
        kept = inside & (position <= seen_ref[:, at])
        score = jnp.where(kept, nt(k_ref[...], q_ref[at, :]) * score_scale, masked_score)
        top = jnp.max(score, axis=0, keepdims=True)
        prob = jnp.where(kept, jnp.exp(score - top), 0.0)
        total = jnp.sum(prob, axis=0, keepdims=True)
        out = (nn(v_ref[...], prob.astype(bf16)) / total).T
        out = out.reshape(chunks, rows, cols)
        lse = top + jnp.log(total)
        high = lse.astype(bf16).astype(f32)
        middle = (lse - high).astype(bf16).astype(f32)
        low = lse - high - middle
        pieces = jnp.concatenate([high, middle, low, jnp.zeros((TAIL - 3, step), f32)])
        per = cols // rows
        for g in range(chunks):
            tail = pieces[:, g // per * cols : (g // per + 1) * cols]
            out_ref[t * chunks + g] = jnp.concatenate([out[g], tail]).astype(bf16)


def merge_kernel(info_ref, got_ref, w_ref, out_ref):
    count, height, cols = got_ref.shape
    rows = height - TAIL
    got = got_ref[...].astype(f32)
    lse = jnp.sum(got[:, rows:, :], axis=1)
    weight = jnp.exp(lse - jnp.max(lse, axis=0, keepdims=True))
    weight = (weight / jnp.sum(weight, axis=0, keepdims=True)).T
    own = jnp.zeros((rows, count), f32)
    for i in range(cols // rows):
        own = jnp.where(info_ref[0] == i, weight[i * rows : (i + 1) * rows, :], own)
    total = jnp.zeros((rows, cols), f32)
    for s in range(count):
        total += own[:, s : s + 1] * got[s, :rows, :]
    project(total.astype(bf16), lambda h: w_ref[h * cols : (h + 1) * cols, :], out_ref)


def project(acts, weight_rows, out_ref):
    for h in range(out_ref.shape[0]):
        out_ref[h] = nt(acts, weight_rows(h)).astype(bf16)


def add_kernel(base_ref, terms_ref, out_ref, wide_ref):
    total = base_ref[...].astype(f32) + jnp.sum(terms_ref[...].astype(f32), axis=0)
    out_ref[...] = total.astype(bf16)
    wide_ref[...] = jnp.broadcast_to(total.astype(bf16)[None], wide_ref.shape)


def last_kernel(base_ref, terms_ref, out_ref):
    total = base_ref[...].astype(f32) + jnp.sum(terms_ref[...].astype(f32), axis=0)
    out_ref[...] = total.astype(bf16)


def unit(all_ref, gain_ref):
    rows = jnp.concatenate([all_ref[h] for h in range(all_ref.shape[0])], axis=1)
    return unit_rows(rows, gain_ref[...])


def latent_kernel(all_ref, gain_ref, w_ref, q_ref, pair_ref):
    qkv = nn(unit(all_ref, gain_ref), w_ref[...]).astype(bf16)
    cols = q_ref.shape[1]
    q_ref[...] = qkv[:, :cols]
    pair_ref[...] = jnp.broadcast_to(qkv[:, cols:][None], pair_ref.shape)


def mix_kernel(own_ref, seen_ref, q_ref, pair_ref, w_ref, out_ref):
    cols = q_ref.shape[1]
    pair = pair_ref[...].reshape(-1, 2 * cols)
    seen = seen_ref[...] <= own_ref[...]
    score = jnp.where(seen, nt(q_ref[...], pair[:, :cols]) * score_scale, masked_score)
    prob = jnp.where(seen, jnp.exp(score - jnp.max(score, axis=1, keepdims=True)), 0.0)
    prob = (prob / jnp.sum(prob, axis=1, keepdims=True)).astype(bf16)
    mixed = nn(prob, pair[:, cols:]).astype(bf16)
    project(mixed, lambda h: w_ref[h * cols : (h + 1) * cols, :], out_ref)


def feed_kernel(all_ref, gain_ref, w_ref, down_ref, out_ref):
    acts = unit(all_ref, gain_ref)
    hidden = down_ref.shape[1]
    gate = nn(acts, w_ref[:, :hidden])
    hidden = (gate / (1.0 + jnp.exp(-gate)) * nn(acts, w_ref[:, hidden:])).astype(bf16)
    cols = out_ref.shape[2]
    project(hidden, lambda h: down_ref[h * cols : (h + 1) * cols, :], out_ref)


def swap(x, axis):
    return lax.all_to_all(x, axis, 0, 0)


def body(
    context, w_attn, w_out, w_latent, w_latent_out, w_mlp, w_down, gains, valid_len, last_visible
):
    tokens, width = context.shape
    cols = w_attn.shape[2]
    ff = w_mlp.shape[2]
    latents = last_visible.shape[0]
    ctxs = lax.axis_size("ctx")
    heads = lax.axis_size("head")
    rows = latents // ctxs
    ctx_index = lax.axis_index("ctx")
    shape = jax.ShapeDtypeStruct
    ys = [[i * 8 + j for j in range(8)] for i in range(4)]
    xs = [[i * 8 + j for i in range(4)] for j in range(8)]

    piece = w_attn.shape[1]
    mids = ff + 5 * cols
    pieces = (w_attn, w_out.T, w_latent, w_latent_out.T, w_mlp, w_down.T)
    early, mid, late = call(
        pack_kernel,
        (
            shape((8, 3, piece, cols), bf16),
            shape((piece, mids), bf16),
            shape((piece, 2 * ff), bf16),
        ),
        *pieces,
        specs=[whole(x) for x in pieces],
        outs=(VMEM, part((piece, mids), 0, 0), part((piece, 2 * ff), 0, 0)),
        room=LATE,
    )
    mid = lax.all_gather(mid, "ctx", axis=0, tiled=True)

    near = lax.all_to_all(early, "ctx", 0, 0, axis_index_groups=ys)
    pick = jnp.clip(last_visible - (ctxs - 1) * tokens, 0, tokens - 1)
    mine = lax.dynamic_slice_in_dim(context, lax.axis_index("head") * cols, cols, 1)
    raw = jnp.take(mine, pick, axis=0, mode="clip").reshape(ctxs, rows, cols)
    near, late, raw = lax.optimization_barrier((near, late, raw))
    late = lax.all_gather(late, "ctx", axis=0, tiled=True)
    own_raw = swap(raw, "ctx")[ctxs - 1]
    near = jnp.broadcast_to(near[None], (4,) + near.shape)
    near, own_raw = lax.optimization_barrier((near, own_raw))
    far = lax.all_to_all(near, "ctx", 0, 0, axis_index_groups=xs)
    kinds = [part((4, 8, 1, piece, cols), 0, 0, i, 0, 0) for i in range(3)]
    raw_rows = lax.all_gather(own_raw, "head", axis=1, tiled=True)
    queries = call(
        query_kernel,
        shape((ctxs, rows, cols), bf16),
        raw_rows, gains[:1], far,
        specs=[VMEM, VMEM, kinds[0]],
    )
    queries = swap(queries, "ctx")
    step = 256
    keys, values = call(
        keyval_kernel,
        (shape((tokens, cols), bf16), shape((cols, tokens), bf16)),
        context, gains[:1], far, far,
        specs=[
            pl.BlockSpec((step, width), lambda i: (i, 0)),
            part((1, width), 0, 0),
            kinds[1],
            kinds[2],
        ],
        outs=(
            pl.BlockSpec((step, cols), lambda i: (i, 0)),
            pl.BlockSpec((cols, step), lambda i: (0, i)),
        ),
        grid=(tokens // step,),
    )

    info = jnp.stack([valid_len[0], ctx_index * tokens])
    seen = last_visible.reshape(1, latents)
    sent = call(
        attend_kernel,
        shape((ctxs, rows + TAIL, cols), bf16),
        info, seen, queries.reshape(latents, cols), keys, values,
        specs=[SMEM, VMEM, VMEM, VMEM, VMEM],
    )
    sent, mid = lax.optimization_barrier((sent, mid))
    cut = [0, ff, ff + 3 * cols, ff + 4 * cols, mids]
    down, qkv_w, mix_w, out_w = [mid[:, i:j] for i, j in zip(cut, cut[1:])]
    got = swap(sent, "ctx")
    spot = lax.rem(ctx_index, cols // rows).reshape(1)
    chunk = shape((heads, rows, cols), bf16)
    own = shape((rows, cols), bf16)
    terms = call(
        merge_kernel, chunk, spot, got, out_w, specs=[SMEM, VMEM, VMEM]
    )
    first, wide = call(add_kernel, (own, chunk), own_raw, swap(terms, "head"))
    query, pair = call(
        latent_kernel,
        (own, shape((ctxs, rows, 2 * cols), bf16)),
        swap(wide, "head"), gains[1:2], qkv_w,
    )
    place = lax.dynamic_slice_in_dim(last_visible, ctx_index * rows, rows, 0).reshape(rows, 1)
    terms = call(
        mix_kernel,
        chunk,
        place, seen, query, swap(pair, "ctx"), mix_w,
    )
    second, wide = call(add_kernel, (own, chunk), first, swap(terms, "head"))
    terms = call(
        feed_kernel,
        chunk,
        swap(wide, "head"), gains[2:3], late, down,
    )
    return call(last_kernel, own, second, swap(terms, "head"))


def solution(mesh):
    in_specs = (
        P("ctx", None),
        P(None, "ctx", "head"),
        P("head", "ctx"),
        P(None, "ctx", "head"),
        P("head", "ctx"),
        P(None, "ctx", "head"),
        P("head", "ctx"),
        P(),
        P("ctx"),
        P(),
    )
    out_specs = P("ctx", "head")
    return jax.shard_map(body, mesh=mesh, in_specs=in_specs, out_specs=out_specs, check_vma=False)
```

```python
import jax
import jax.numpy as jnp
from jax import lax
from jax.experimental import pallas as pl
from jax.experimental.pallas import tpu as pltpu
from jax.sharding import PartitionSpec as P

HD = 128
epsilon = 1e-05
masked_score = -1e30
score_scale = HD ** (-0.5)
f32 = jnp.float32
bf16 = jnp.bfloat16
TAIL = 8
LATE = 58
VMEM = pl.BlockSpec(memory_space=pltpu.VMEM)
SMEM = pl.BlockSpec(memory_space=pltpu.SMEM)


def nt(a, b):
    return lax.dot_general(a, b, (((1,), (1,)), ((), ())), preferred_element_type=f32)


def nn(a, b):
    return jnp.dot(a, b, preferred_element_type=f32)


def call(kernel, out_shape, *args, specs=None, outs=None, grid=(1,), room=16):
    return pl.pallas_call(
        kernel,
        grid=grid,
        out_shape=out_shape,
        in_specs=specs if specs is not None else [VMEM] * len(args),
        out_specs=outs if outs is not None else jax.tree.map(lambda _: VMEM, out_shape),
        compiler_params=pltpu.CompilerParams(vmem_limit_bytes=room * 2**20),
    )(*args)


def part(shape, *index):
    return pl.BlockSpec(shape, lambda i: index)


def pack_kernel(attn_ref, out_w_ref, latent_ref, latent_out_ref, mlp_ref, down_ref, early_ref, late_ref):
    for i, block in enumerate([attn_ref[0], attn_ref[1], attn_ref[2], out_w_ref[...]]):
        early_ref[:, i] = jnp.broadcast_to(block[None], (early_ref.shape[0],) + block.shape)
    at = 0
    for block in [latent_ref[0], latent_ref[1], latent_ref[2], latent_out_ref[...], mlp_ref[0], mlp_ref[1], down_ref[...]]:
        late_ref[:, at : at + block.shape[1]] = block
        at += block.shape[1]


def whole(x):
    return part(x.shape, *[0] * x.ndim)


def unit_rows(rows, gain):
    wide = rows.astype(f32)
    scale = lax.rsqrt(jnp.mean(wide * wide, axis=1, keepdims=True) + epsilon)
    return (wide * scale * gain).astype(bf16)


def joined(w_ref):
    return w_ref[...].reshape(-1, w_ref.shape[-1])


def query_kernel(rows_ref, gain_ref, w_ref, out_ref):
    query = nn(unit_rows(rows_ref[...], gain_ref[...]), joined(w_ref)).astype(bf16)
    out_ref[...] = jnp.broadcast_to(query[None], out_ref.shape)


def keyval_kernel(rows_ref, gain_ref, k_w_ref, v_w_ref, key_ref, value_ref):
    rows = unit_rows(rows_ref[...], gain_ref[...])
    key_ref[...] = nn(rows, joined(k_w_ref)).astype(bf16)
    value_ref[...] = nn(rows, joined(v_w_ref)).T.astype(bf16)


def attend_kernel(info_ref, seen_ref, q_ref, k_ref, v_ref, out_ref):
    keys, cols = k_ref.shape
    count, rows = out_ref.shape[0], out_ref.shape[1] - TAIL
    step = 256
    chunks = step // rows
    key = lax.broadcasted_iota(jnp.int32, (keys, step), 0)
    inside = key < info_ref[0]
    position = key + info_ref[1]
    for t in range(count * rows // step):
        at = slice(t * step, (t + 1) * step)
        kept = inside & (position <= seen_ref[:, at])
        score = jnp.where(kept, nt(k_ref[...], q_ref[at, :]) * score_scale, masked_score)
        top = jnp.max(score, axis=0, keepdims=True)
        prob = jnp.where(kept, jnp.exp(score - top), 0.0)
        total = jnp.sum(prob, axis=0, keepdims=True)
        out = (nn(v_ref[...], prob.astype(bf16)) / total).T
        out = out.reshape(chunks, rows, cols)
        lse = top + jnp.log(total)
        high = lse.astype(bf16).astype(f32)
        middle = (lse - high).astype(bf16).astype(f32)
        low = lse - high - middle
        pieces = jnp.concatenate([high, middle, low, jnp.zeros((TAIL - 3, step), f32)])
        per = cols // rows
        for g in range(chunks):
            tail = pieces[:, g // per * cols : (g // per + 1) * cols]
            out_ref[t * chunks + g] = jnp.concatenate([out[g], tail]).astype(bf16)


def merge_kernel(info_ref, got_ref, w_ref, out_ref):
    count, height, cols = got_ref.shape
    rows = height - TAIL
    got = got_ref[...].astype(f32)
    lse = jnp.sum(got[:, rows:, :], axis=1)
    weight = jnp.exp(lse - jnp.max(lse, axis=0, keepdims=True))
    weight = (weight / jnp.sum(weight, axis=0, keepdims=True)).T
    own = jnp.zeros((rows, count), f32)
    for i in range(cols // rows):
        own = jnp.where(info_ref[0] == i, weight[i * rows : (i + 1) * rows, :], own)
    total = jnp.zeros((rows, cols), f32)
    for s in range(count):
        total += own[:, s : s + 1] * got[s, :rows, :]
    project(total.astype(bf16), lambda h: w_ref[h * cols : (h + 1) * cols, :], out_ref)


def project(acts, weight_rows, out_ref):
    for h in range(out_ref.shape[0]):
        out_ref[h] = nt(acts, weight_rows(h)).astype(bf16)


def add_kernel(base_ref, terms_ref, out_ref, wide_ref):
    total = base_ref[...].astype(f32) + jnp.sum(terms_ref[...].astype(f32), axis=0)
    out_ref[...] = total.astype(bf16)
    wide_ref[...] = jnp.broadcast_to(total.astype(bf16)[None], wide_ref.shape)


def last_kernel(base_ref, terms_ref, out_ref):
    total = base_ref[...].astype(f32) + jnp.sum(terms_ref[...].astype(f32), axis=0)
    out_ref[...] = total.astype(bf16)


def unit(all_ref, gain_ref):
    rows = jnp.concatenate([all_ref[h] for h in range(all_ref.shape[0])], axis=1)
    return unit_rows(rows, gain_ref[...])


def latent_kernel(all_ref, gain_ref, w_ref, q_ref, pair_ref):
    qkv = nn(unit(all_ref, gain_ref), w_ref[...]).astype(bf16)
    cols = q_ref.shape[1]
    q_ref[...] = qkv[:, :cols]
    pair_ref[...] = jnp.broadcast_to(qkv[:, cols:][None], pair_ref.shape)


def mix_kernel(own_ref, seen_ref, q_ref, pair_ref, w_ref, out_ref):
    cols = q_ref.shape[1]
    pair = pair_ref[...].reshape(-1, 2 * cols)
    seen = seen_ref[...] <= own_ref[...]
    score = jnp.where(seen, nt(q_ref[...], pair[:, :cols]) * score_scale, masked_score)
    prob = jnp.where(seen, jnp.exp(score - jnp.max(score, axis=1, keepdims=True)), 0.0)
    prob = (prob / jnp.sum(prob, axis=1, keepdims=True)).astype(bf16)
    mixed = nn(prob, pair[:, cols:]).astype(bf16)
    project(mixed, lambda h: w_ref[h * cols : (h + 1) * cols, :], out_ref)


def feed_kernel(all_ref, gain_ref, gate_ref, up_ref, down_ref, out_ref):
    acts = unit(all_ref, gain_ref)
    gate = nn(acts, gate_ref[...])
    hidden = (gate / (1.0 + jnp.exp(-gate)) * nn(acts, up_ref[...])).astype(bf16)
    cols = out_ref.shape[2]
    project(hidden, lambda h: down_ref[h * cols : (h + 1) * cols, :], out_ref)


def swap(x, axis):
    return lax.all_to_all(x, axis, 0, 0)


def body(
    context, w_attn, w_out, w_latent, w_latent_out, w_mlp, w_down, gains, valid_len, last_visible
):
    tokens, width = context.shape
    cols = w_attn.shape[2]
    ff = w_mlp.shape[2]
    latents = last_visible.shape[0]
    ctxs = lax.axis_size("ctx")
    heads = lax.axis_size("head")
    rows = latents // ctxs
    ctx_index = lax.axis_index("ctx")
    shape = jax.ShapeDtypeStruct
    ys = [[i * 8 + j for j in range(8)] for i in range(4)]
    xs = [[i * 8 + j for i in range(4)] for j in range(8)]

    piece = w_attn.shape[1]
    lates = 4 * cols + 3 * ff
    pieces = (w_attn, w_out.T, w_latent, w_latent_out.T, w_mlp, w_down.T)
    early, late = call(
        pack_kernel,
        (shape((8, 4, piece, cols), bf16), shape((piece, lates), bf16)),
        *pieces,
        specs=[whole(x) for x in pieces],
        outs=(VMEM, part((piece, lates), 0, 0)),
        room=LATE,
    )

    near = lax.all_to_all(early, "ctx", 0, 0, axis_index_groups=ys)
    pick = jnp.clip(last_visible - (ctxs - 1) * tokens, 0, tokens - 1)
    mine = lax.dynamic_slice_in_dim(context, lax.axis_index("head") * cols, cols, 1)
    raw = jnp.take(mine, pick, axis=0, mode="clip").reshape(ctxs, rows, cols)
    near, late, raw = lax.optimization_barrier((near, late, raw))
    late = lax.all_gather(late, "ctx", axis=0, tiled=True)
    own_raw = swap(raw, "ctx")[ctxs - 1]
    near_out = near[:, 3].reshape(8 * piece, cols)
    near = near[:, :3]
    near = jnp.broadcast_to(near[None], (4,) + near.shape)
    near, own_raw = lax.optimization_barrier((near, own_raw))
    far = lax.all_to_all(near, "ctx", 0, 0, axis_index_groups=xs)
    kinds = [part((4, 8, 1, piece, cols), 0, 0, i, 0, 0) for i in range(3)]
    raw_rows = lax.all_gather(own_raw, "head", axis=1, tiled=True)
    queries = call(
        query_kernel,
        shape((ctxs, rows, cols), bf16),
        raw_rows, gains[:1], far,
        specs=[VMEM, VMEM, kinds[0]],
    )
    queries, near_out = lax.optimization_barrier((queries, near_out))
    queries = swap(queries, "ctx")
    out_w = lax.all_gather(near_out, "ctx", axis=0, tiled=True, axis_index_groups=xs)
    step = 256
    keys, values = call(
        keyval_kernel,
        (shape((tokens, cols), bf16), shape((cols, tokens), bf16)),
        context, gains[:1], far, far,
        specs=[
            pl.BlockSpec((step, width), lambda i: (i, 0)),
            part((1, width), 0, 0),
            kinds[1],
            kinds[2],
        ],
        outs=(
            pl.BlockSpec((step, cols), lambda i: (i, 0)),
            pl.BlockSpec((cols, step), lambda i: (0, i)),
        ),
        grid=(tokens // step,),
    )

    info = jnp.stack([valid_len[0], ctx_index * tokens])
    seen = last_visible.reshape(1, latents)
    sent = call(
        attend_kernel,
        shape((ctxs, rows + TAIL, cols), bf16),
        info, seen, queries.reshape(latents, cols), keys, values,
        specs=[SMEM, VMEM, VMEM, VMEM, VMEM],
    )
    at = [0, 3 * cols, 4 * cols, 4 * cols + ff, 4 * cols + 2 * ff, lates]
    qkv_w, mix_w, gate_w = [late[:, at[i] : at[i + 1]] for i in range(3)]
    got = swap(sent, "ctx")
    spot = lax.rem(ctx_index, cols // rows).reshape(1)
    chunk = shape((heads, rows, cols), bf16)
    own = shape((rows, cols), bf16)
    terms = call(
        merge_kernel, chunk, spot, got, out_w, specs=[SMEM, VMEM, VMEM]
    )
    first, wide = call(add_kernel, (own, chunk), own_raw, swap(terms, "head"))
    query, pair = call(
        latent_kernel,
        (own, shape((ctxs, rows, 2 * cols), bf16)),
        swap(wide, "head"), gains[1:2], qkv_w,
    )
    place = lax.dynamic_slice_in_dim(last_visible, ctx_index * rows, rows, 0).reshape(rows, 1)
    pair, late = lax.optimization_barrier((swap(pair, "ctx"), late))
    up_w = late[:, at[3] : at[4]]
    terms = call(mix_kernel, chunk, place, seen, query, pair, mix_w)
    second, wide = call(add_kernel, (own, chunk), first, swap(terms, "head"))
    wide, late = lax.optimization_barrier((wide, late))
    down_w = late[:, at[4] :]
    terms = call(
        feed_kernel, chunk, swap(wide, "head"), gains[2:3], gate_w, up_w, down_w
    )
    return call(last_kernel, own, second, swap(terms, "head"))


def solution(mesh):
    in_specs = (
        P("ctx", None),
        P(None, "ctx", "head"),
        P("head", "ctx"),
        P(None, "ctx", "head"),
        P("head", "ctx"),
        P(None, "ctx", "head"),
        P("head", "ctx"),
        P(),
        P("ctx"),
        P(),
    )
    out_specs = P("ctx", "head")
    return jax.shard_map(body, mesh=mesh, in_specs=in_specs, out_specs=out_specs, check_vma=False)
```

```python
import jax
import jax.numpy as jnp
from jax import lax
from jax.experimental import pallas as pl
from jax.experimental.pallas import tpu as pltpu
from jax.sharding import PartitionSpec as P

HD = 128
epsilon = 1e-05
masked_score = -1e30
score_scale = HD ** (-0.5)
f32 = jnp.float32
bf16 = jnp.bfloat16
TAIL = 8
LATE = 58
LOG2E = 1.4426950408889634
VMEM = pl.BlockSpec(memory_space=pltpu.VMEM)
SMEM = pl.BlockSpec(memory_space=pltpu.SMEM)


def nt(a, b):
    return lax.dot_general(a, b, (((1,), (1,)), ((), ())), preferred_element_type=f32)


def nn(a, b):
    return jnp.dot(a, b, preferred_element_type=f32)


def call(kernel, out_shape, *args, specs=None, outs=None, grid=(1,), room=16, scratch=()):
    return pl.pallas_call(
        kernel,
        grid=grid,
        out_shape=out_shape,
        in_specs=specs if specs is not None else [VMEM] * len(args),
        out_specs=outs if outs is not None else jax.tree.map(lambda _: VMEM, out_shape),
        scratch_shapes=scratch,
        compiler_params=pltpu.CompilerParams(vmem_limit_bytes=room * 2**20),
    )(*args)


def part(shape, *index):
    return pl.BlockSpec(shape, lambda i: index)


def pack_kernel(attn_ref, out_w_ref, latent_ref, latent_out_ref, mlp_ref, down_ref, early_ref, late_ref):
    for i, block in enumerate([attn_ref[0], attn_ref[1], attn_ref[2], out_w_ref[...]]):
        early_ref[:, i] = jnp.broadcast_to(block[None], (early_ref.shape[0],) + block.shape)
    at = 0
    for block in [latent_ref[0], latent_ref[1], latent_ref[2], latent_out_ref[...], mlp_ref[0], mlp_ref[1], down_ref[...]]:
        late_ref[:, at : at + block.shape[1]] = block
        at += block.shape[1]


def whole(x):
    return part(x.shape, *[0] * x.ndim)


def unit_rows(rows, gain):
    wide = rows.astype(f32)
    scale = lax.rsqrt(jnp.mean(wide * wide, axis=1, keepdims=True) + epsilon)
    return (wide * scale * gain).astype(bf16)


def joined(w_ref):
    return w_ref[...].reshape(-1, w_ref.shape[-1])


def query_kernel(rows_ref, gain_ref, w_ref, out_ref):
    query = nn(unit_rows(rows_ref[...], gain_ref[...]), joined(w_ref)).astype(bf16)
    out_ref[...] = jnp.broadcast_to(query[None], out_ref.shape)


def keyval_kernel(rows_ref, gain_ref, k_w_ref, v_w_ref, key_ref, value_ref):
    rows = unit_rows(rows_ref[...], gain_ref[...])
    key_ref[...] = nn(rows, joined(k_w_ref)).astype(bf16)
    value_ref[...] = nn(rows, joined(v_w_ref)).T.astype(bf16)


def attend_kernel(info_ref, *refs):
    is_last = info_ref[2] == 1
    pl.when(is_last)(lambda: attend(True, info_ref, *refs))
    pl.when(jnp.logical_not(is_last))(lambda: attend(False, info_ref, *refs))


def attend(last, info_ref, seen_ref, q_ref, k_ref, v_ref, out_ref):
    keys, cols = k_ref.shape
    count, rows = out_ref.shape[0], out_ref.shape[1] - TAIL
    step = 256
    chunks = step // rows
    bias = jnp.where(
        lax.broadcasted_iota(jnp.int32, (keys, 1), 0) < info_ref[0], 0.0, masked_score
    )
    for t in range(count * rows // step):
        at = slice(t * step, (t + 1) * step)
        score = nt(k_ref[...], q_ref[at, :]) + bias
        if last:
            position = lax.broadcasted_iota(jnp.int32, (keys, step), 0) + info_ref[1]
            score = jnp.where(position <= seen_ref[:, at], score, masked_score)
        top = jnp.max(score, axis=0, keepdims=True)
        prob = jnp.exp2((score - top) * (score_scale * LOG2E))
        total = jnp.sum(prob, axis=0, keepdims=True)
        out = (nn(v_ref[...], prob.astype(bf16)) / total).T
        out = out.reshape(chunks, rows, cols)
        lse = top * score_scale + jnp.log(total)
        high = lse.astype(bf16).astype(f32)
        middle = (lse - high).astype(bf16).astype(f32)
        low = lse - high - middle
        pieces = jnp.concatenate([high, middle, low, jnp.zeros((TAIL - 3, step), f32)])
        per = cols // rows
        for g in range(chunks):
            tail = pieces[:, g // per * cols : (g // per + 1) * cols]
            out_ref[t * chunks + g] = jnp.concatenate([out[g], tail]).astype(bf16)


def merge_kernel(info_ref, got_ref, w_ref, out_ref):
    count, height, cols = got_ref.shape
    rows = height - TAIL
    got = got_ref[...].astype(f32)
    lse = jnp.sum(got[:, rows:, :], axis=1)
    weight = jnp.exp(lse - jnp.max(lse, axis=0, keepdims=True))
    weight = (weight / jnp.sum(weight, axis=0, keepdims=True)).T
    own = jnp.zeros((rows, count), f32)
    for i in range(cols // rows):
        own = jnp.where(info_ref[0] == i, weight[i * rows : (i + 1) * rows, :], own)
    total = jnp.zeros((rows, cols), f32)
    for s in range(count):
        total += own[:, s : s + 1] * got[s, :rows, :]
    project(total.astype(bf16), lambda h: w_ref[h * cols : (h + 1) * cols, :], out_ref)


def project(acts, weight_rows, out_ref):
    for h in range(out_ref.shape[0]):
        out_ref[h] = nt(acts, weight_rows(h)).astype(bf16)


def add_kernel(base_ref, terms_ref, out_ref, wide_ref):
    total = base_ref[...].astype(f32) + jnp.sum(terms_ref[...].astype(f32), axis=0)
    out_ref[...] = total.astype(bf16)
    wide_ref[...] = jnp.broadcast_to(total.astype(bf16)[None], wide_ref.shape)


def last_kernel(base_ref, terms_ref, out_ref):
    total = base_ref[...].astype(f32) + jnp.sum(terms_ref[...].astype(f32), axis=0)
    out_ref[...] = total.astype(bf16)


def unit(all_ref, gain_ref):
    rows = jnp.concatenate([all_ref[h] for h in range(all_ref.shape[0])], axis=1)
    return unit_rows(rows, gain_ref[...])


def latent_kernel(all_ref, gain_ref, w_ref, q_ref, pair_ref):
    qkv = nn(unit(all_ref, gain_ref), w_ref[...]).astype(bf16)
    cols = q_ref.shape[1]
    q_ref[...] = qkv[:, :cols]
    pair_ref[...] = jnp.broadcast_to(qkv[:, cols:][None], pair_ref.shape)


def mix_kernel(own_ref, seen_ref, q_ref, pair_ref, w_ref, out_ref):
    cols = q_ref.shape[1]
    pair = pair_ref[...].reshape(-1, 2 * cols)
    seen = seen_ref[...] <= own_ref[...]
    score = jnp.where(seen, nt(q_ref[...], pair[:, :cols]) * score_scale, masked_score)
    prob = jnp.where(seen, jnp.exp(score - jnp.max(score, axis=1, keepdims=True)), 0.0)
    prob = (prob / jnp.sum(prob, axis=1, keepdims=True)).astype(bf16)
    mixed = nn(prob, pair[:, cols:]).astype(bf16)
    project(mixed, lambda h: w_ref[h * cols : (h + 1) * cols, :], out_ref)


def feed_kernel(all_ref, gain_ref, gate_ref, up_ref, down_ref, out_ref, acts_ref, sum_ref):
    step = pl.program_id(0)
    cols = out_ref.shape[2]

    @pl.when(step == 0)
    def _():
        acts_ref[...] = unit(all_ref, gain_ref)
        sum_ref[...] = jnp.zeros_like(sum_ref)

    acts = acts_ref[...]
    gate = nn(acts, gate_ref[...])
    hidden = (gate / (1.0 + jnp.exp(-gate)) * nn(acts, up_ref[...])).astype(bf16)
    for h in range(out_ref.shape[0]):
        sum_ref[h] += nt(hidden, down_ref[h * cols : (h + 1) * cols, :])

    @pl.when(step == pl.num_programs(0) - 1)
    def _():
        out_ref[...] = sum_ref[...].astype(bf16)


def swap(x, axis):
    return lax.all_to_all(x, axis, 0, 0)


def body(
    context, w_attn, w_out, w_latent, w_latent_out, w_mlp, w_down, gains, valid_len, last_visible
):
    tokens, width = context.shape
    cols = w_attn.shape[2]
    ff = w_mlp.shape[2]
    latents = last_visible.shape[0]
    ctxs = lax.axis_size("ctx")
    heads = lax.axis_size("head")
    rows = latents // ctxs
    ctx_index = lax.axis_index("ctx")
    shape = jax.ShapeDtypeStruct
    ys = [[i * 8 + j for j in range(8)] for i in range(4)]
    xs = [[i * 8 + j for i in range(4)] for j in range(8)]

    piece = w_attn.shape[1]
    lates = 4 * cols + 3 * ff
    pieces = (w_attn, w_out.T, w_latent, w_latent_out.T, w_mlp, w_down.T)
    early, late = call(
        pack_kernel,
        (shape((8, 4, piece, cols), bf16), shape((piece, lates), bf16)),
        *pieces,
        specs=[whole(x) for x in pieces],
        outs=(VMEM, part((piece, lates), 0, 0)),
        room=LATE,
    )

    near = lax.all_to_all(early, "ctx", 0, 0, axis_index_groups=ys)
    pick = jnp.clip(last_visible - (ctxs - 1) * tokens, 0, tokens - 1)
    mine = lax.dynamic_slice_in_dim(context, lax.axis_index("head") * cols, cols, 1)
    raw = jnp.take(mine, pick, axis=0, mode="clip").reshape(ctxs, rows, cols)
    near, late, raw = lax.optimization_barrier((near, late, raw))
    late = lax.all_gather(late, "ctx", axis=0, tiled=True)
    own_raw = swap(raw, "ctx")[ctxs - 1]
    out_w = lax.all_gather(
        near[:, 3].reshape(8 * piece, cols), "ctx", axis=0, tiled=True, axis_index_groups=xs
    )
    near = near[:, :3]
    near = jnp.broadcast_to(near[None], (4,) + near.shape)
    near, own_raw, out_w = lax.optimization_barrier((near, own_raw, out_w))
    far = lax.all_to_all(near, "ctx", 0, 0, axis_index_groups=xs)
    kinds = [part((4, 8, 1, piece, cols), 0, 0, i, 0, 0) for i in range(3)]
    raw_rows = lax.all_gather(own_raw, "head", axis=1, tiled=True)
    queries = call(
        query_kernel,
        shape((ctxs, rows, cols), bf16),
        raw_rows, gains[:1], far,
        specs=[VMEM, VMEM, kinds[0]],
    )
    queries = swap(queries, "ctx")
    step = 256
    keys, values = call(
        keyval_kernel,
        (shape((tokens, cols), bf16), shape((cols, tokens), bf16)),
        context, gains[:1], far, far,
        specs=[
            pl.BlockSpec((step, width), lambda i: (i, 0)),
            part((1, width), 0, 0),
            kinds[1],
            kinds[2],
        ],
        outs=(
            pl.BlockSpec((step, cols), lambda i: (i, 0)),
            pl.BlockSpec((cols, step), lambda i: (0, i)),
        ),
        grid=(tokens // step,),
    )

    is_last = (ctx_index == ctxs - 1).astype(jnp.int32)
    info = jnp.stack([valid_len[0], ctx_index * tokens, is_last])
    seen = last_visible.reshape(1, latents)
    sent = call(
        attend_kernel,
        shape((ctxs, rows + TAIL, cols), bf16),
        info, seen, queries.reshape(latents, cols), keys, values,
        specs=[SMEM, VMEM, VMEM, VMEM, VMEM],
    )
    qkv_w, mix_w = late[:, : 3 * cols], late[:, 3 * cols : 4 * cols]
    got = swap(sent, "ctx")
    spot = lax.rem(ctx_index, cols // rows).reshape(1)
    chunk = shape((heads, rows, cols), bf16)
    own = shape((rows, cols), bf16)
    terms = call(
        merge_kernel, chunk, spot, got, out_w, specs=[SMEM, VMEM, VMEM]
    )
    first, wide = call(add_kernel, (own, chunk), own_raw, swap(terms, "head"))
    query, pair = call(
        latent_kernel,
        (own, shape((ctxs, rows, 2 * cols), bf16)),
        swap(wide, "head"), gains[1:2], qkv_w,
    )
    place = lax.dynamic_slice_in_dim(last_visible, ctx_index * rows, rows, 0).reshape(rows, 1)
    terms = call(mix_kernel, chunk, place, seen, query, swap(pair, "ctx"), mix_w)
    second, wide = call(add_kernel, (own, chunk), first, swap(terms, "head"))
    steps = ff // cols
    terms = call(
        feed_kernel,
        chunk,
        swap(wide, "head"), gains[2:3], late, late, late,
        specs=[VMEM, VMEM]
        + [
            pl.BlockSpec((width, cols), lambda i, first=4 + n * steps: (0, first + i))
            for n in range(3)
        ],
        grid=(steps,),
        room=LATE,
        scratch=[pltpu.VMEM((rows, width), bf16), pltpu.VMEM(chunk.shape, f32)],
    )
    return call(last_kernel, own, second, swap(terms, "head"))


def solution(mesh):
    in_specs = (
        P("ctx", None),
        P(None, "ctx", "head"),
        P("head", "ctx"),
        P(None, "ctx", "head"),
        P("head", "ctx"),
        P(None, "ctx", "head"),
        P("head", "ctx"),
        P(),
        P("ctx"),
        P(),
    )
    out_specs = P("ctx", "head")
    return jax.shard_map(body, mesh=mesh, in_specs=in_specs, out_specs=out_specs, check_vma=False)
```

```python
import jax
import jax.numpy as jnp
from jax import lax
from jax.experimental import pallas as pl
from jax.experimental.pallas import tpu as pltpu
from jax.sharding import PartitionSpec as P

HD = 128
epsilon = 1e-05
masked_score = -1e30
score_scale = HD ** (-0.5)
f32 = jnp.float32
bf16 = jnp.bfloat16
TAIL = 8
LATE = 58
LOG2E = 1.4426950408889634
VMEM = pl.BlockSpec(memory_space=pltpu.VMEM)
SMEM = pl.BlockSpec(memory_space=pltpu.SMEM)


def nt(a, b):
    return lax.dot_general(a, b, (((1,), (1,)), ((), ())), preferred_element_type=f32)


def nn(a, b):
    return jnp.dot(a, b, preferred_element_type=f32)


def call(kernel, out_shape, *args, specs=None, outs=None, grid=(1,), room=16):
    return pl.pallas_call(
        kernel,
        grid=grid,
        out_shape=out_shape,
        in_specs=specs if specs is not None else [VMEM] * len(args),
        out_specs=outs if outs is not None else jax.tree.map(lambda _: VMEM, out_shape),
        compiler_params=pltpu.CompilerParams(vmem_limit_bytes=room * 2**20),
    )(*args)


def part(shape, *index):
    return pl.BlockSpec(shape, lambda i: index)


def pack_kernel(
    spot_ref, seen_ref, rows_ref, attn_ref, out_w_ref, latent_ref, latent_out_ref, mlp_ref, down_ref,
    early_ref, late_ref,
):
    blocks = [attn_ref[0], attn_ref[1], attn_ref[2], out_w_ref[...]]
    piece, cols = blocks[0].shape
    ways = early_ref.shape[0]
    for i, block in enumerate(blocks):
        early_ref[:, i * piece : (i + 1) * piece, :] = jnp.broadcast_to(
            block[None], (ways,) + block.shape
        )
    at = 0
    for block in [latent_ref[0], latent_ref[1], latent_ref[2], latent_out_ref[...], mlp_ref[0], mlp_ref[1], down_ref[...]]:
        late_ref[:, at : at + block.shape[1]] = block
        at += block.shape[1]
    tokens = rows_ref.shape[0]
    turned = rows_ref[...].astype(f32).T.astype(bf16)
    step = 256
    rows = step // ways
    behind = len(blocks) * piece
    position = lax.broadcasted_iota(jnp.int32, (tokens, step), 0)
    for t in range(seen_ref.shape[1] // step):
        pick = seen_ref[:, t * step : (t + 1) * step] - spot_ref[1]
        chosen = jnp.where(position == pick, 1.0, 0.0).astype(bf16)
        picked = nn(turned, chosen).T.astype(bf16)
        early_ref[:, behind + t * rows : behind + (t + 1) * rows, :] = picked.reshape(
            ways, rows, cols
        )


def whole(x):
    return part(x.shape, *[0] * x.ndim)


def unit_rows(rows, gain):
    wide = rows.astype(f32)
    scale = lax.rsqrt(jnp.mean(wide * wide, axis=1, keepdims=True) + epsilon)
    return (wide * scale * gain).astype(bf16)


def joined(w_ref):
    return w_ref[...].reshape(-1, w_ref.shape[-1])


def query_kernel(rows_ref, gain_ref, w_ref, out_ref):
    query = nn(unit_rows(rows_ref[...], gain_ref[...]), joined(w_ref)).astype(bf16)
    out_ref[...] = jnp.broadcast_to(query[None], out_ref.shape)


def keyval_kernel(rows_ref, gain_ref, k_w_ref, v_w_ref, key_ref, value_ref):
    rows = unit_rows(rows_ref[...], gain_ref[...])
    key_ref[...] = nn(rows, joined(k_w_ref)).astype(bf16)
    value_ref[...] = nn(rows, joined(v_w_ref)).T.astype(bf16)


def attend_kernel(info_ref, *refs):
    is_last = info_ref[2] == 1
    pl.when(is_last)(lambda: attend(True, info_ref, *refs))
    pl.when(jnp.logical_not(is_last))(lambda: attend(False, info_ref, *refs))


def attend(last, info_ref, seen_ref, q_ref, k_ref, v_ref, out_ref):
    keys, cols = k_ref.shape
    count, rows = out_ref.shape[0], out_ref.shape[1] - TAIL
    step = 256
    chunks = step // rows
    bias = jnp.where(
        lax.broadcasted_iota(jnp.int32, (keys, 1), 0) < info_ref[0], 0.0, masked_score
    )
    for t in range(count * rows // step):
        at = slice(t * step, (t + 1) * step)
        score = nt(k_ref[...], q_ref[at, :]) + bias
        if last:
            position = lax.broadcasted_iota(jnp.int32, (keys, step), 0) + info_ref[1]
            score = jnp.where(position <= seen_ref[:, at], score, masked_score)
        top = jnp.max(score, axis=0, keepdims=True)
        prob = jnp.exp2((score - top) * (score_scale * LOG2E))
        total = jnp.sum(prob, axis=0, keepdims=True)
        out = (nn(v_ref[...], prob.astype(bf16)) / total).T
        out = out.reshape(chunks, rows, cols)
        lse = top * score_scale + jnp.log(total)
        high = lse.astype(bf16).astype(f32)
        middle = (lse - high).astype(bf16).astype(f32)
        low = lse - high - middle
        pieces = jnp.concatenate([high, middle, low, jnp.zeros((TAIL - 3, step), f32)])
        per = cols // rows
        for g in range(chunks):
            tail = pieces[:, g // per * cols : (g // per + 1) * cols]
            out_ref[t * chunks + g] = jnp.concatenate([out[g], tail]).astype(bf16)


def merge_kernel(info_ref, got_ref, w_ref, out_ref):
    count, height, cols = got_ref.shape
    rows = height - TAIL
    got = got_ref[...].astype(f32)
    lse = jnp.sum(got[:, rows:, :], axis=1)
    weight = jnp.exp(lse - jnp.max(lse, axis=0, keepdims=True))
    weight = (weight / jnp.sum(weight, axis=0, keepdims=True)).T
    own = jnp.zeros((rows, count), f32)
    for i in range(cols // rows):
        own = jnp.where(info_ref[0] == i, weight[i * rows : (i + 1) * rows, :], own)
    total = jnp.zeros((rows, cols), f32)
    for s in range(count):
        total += own[:, s : s + 1] * got[s, :rows, :]
    weight = joined(w_ref)
    project(total.astype(bf16), lambda h: weight[h * cols : (h + 1) * cols], out_ref)


def project(acts, weight_rows, out_ref):
    for h in range(out_ref.shape[0]):
        out_ref[h] = nt(acts, weight_rows(h)).astype(bf16)


def add_kernel(base_ref, terms_ref, out_ref, wide_ref):
    total = base_ref[...].astype(f32) + jnp.sum(terms_ref[...].astype(f32), axis=0)
    out_ref[...] = total.astype(bf16)
    wide_ref[...] = jnp.broadcast_to(total.astype(bf16)[None], wide_ref.shape)


def last_kernel(base_ref, terms_ref, out_ref):
    total = base_ref[...].astype(f32) + jnp.sum(terms_ref[...].astype(f32), axis=0)
    out_ref[...] = total.astype(bf16)


def unit(all_ref, gain_ref):
    rows = jnp.concatenate([all_ref[h] for h in range(all_ref.shape[0])], axis=1)
    return unit_rows(rows, gain_ref[...])


def latent_kernel(all_ref, gain_ref, w_ref, q_ref, pair_ref):
    qkv = nn(unit(all_ref, gain_ref), w_ref[...]).astype(bf16)
    cols = q_ref.shape[1]
    q_ref[...] = qkv[:, :cols]
    pair_ref[...] = jnp.broadcast_to(qkv[:, cols:][None], pair_ref.shape)


def mix_kernel(own_ref, seen_ref, q_ref, pair_ref, w_ref, out_ref):
    cols = q_ref.shape[1]
    pair = pair_ref[...].reshape(-1, 2 * cols)
    seen = seen_ref[...] <= own_ref[...]
    score = jnp.where(seen, nt(q_ref[...], pair[:, :cols]) * score_scale, masked_score)
    prob = jnp.where(seen, jnp.exp(score - jnp.max(score, axis=1, keepdims=True)), 0.0)
    prob = (prob / jnp.sum(prob, axis=1, keepdims=True)).astype(bf16)
    mixed = nn(prob, pair[:, cols:]).astype(bf16)
    project(mixed, lambda h: w_ref[h * cols : (h + 1) * cols, :], out_ref)


def feed_kernel(all_ref, gain_ref, gate_ref, up_ref, down_ref, out_ref):
    acts = unit(all_ref, gain_ref)
    gate = nn(acts, gate_ref[...])
    hidden = (gate / (1.0 + jnp.exp(-gate)) * nn(acts, up_ref[...])).astype(bf16)
    cols = out_ref.shape[2]
    project(hidden, lambda h: down_ref[h * cols : (h + 1) * cols, :], out_ref)


def swap(x, axis):
    return lax.all_to_all(x, axis, 0, 0)


def body(
    context, w_attn, w_out, w_latent, w_latent_out, w_mlp, w_down, gains, valid_len, last_visible
):
    tokens, width = context.shape
    cols = w_attn.shape[2]
    ff = w_mlp.shape[2]
    latents = last_visible.shape[0]
    ctxs = lax.axis_size("ctx")
    heads = lax.axis_size("head")
    rows = latents // ctxs
    ctx_index = lax.axis_index("ctx")
    shape = jax.ShapeDtypeStruct
    ys = [[i * 8 + j for j in range(8)] for i in range(4)]
    xs = [[i * 8 + j for i in range(4)] for j in range(8)]

    piece = w_attn.shape[1]
    lates = 4 * cols + 3 * ff
    pieces = (w_attn, w_out.T, w_latent, w_latent_out.T, w_mlp, w_down.T)
    seen = last_visible.reshape(1, latents)
    head = lax.axis_index("head")
    height = 4 * piece + latents // 8
    early, late = pl.pallas_call(
        pack_kernel,
        grid_spec=pltpu.PrefetchScalarGridSpec(
            num_scalar_prefetch=1,
            grid=(1,),
            in_specs=[
                pl.BlockSpec((1, latents), lambda i, spot: (0, 0)),
                pl.BlockSpec((tokens, cols), lambda i, spot: (0, spot[0])),
            ]
            + [pl.BlockSpec(x.shape, lambda i, spot, n=x.ndim: (0,) * n) for x in pieces],
            out_specs=[
                pl.BlockSpec((8, height, cols), lambda i, spot: (0, 0, 0)),
                pl.BlockSpec((piece, lates), lambda i, spot: (0, 0)),
            ],
        ),
        out_shape=(shape((8, height, cols), bf16), shape((piece, lates), bf16)),
        compiler_params=pltpu.CompilerParams(vmem_limit_bytes=LATE * 2**20),
    )(jnp.stack([head, jnp.int32((ctxs - 1) * tokens)]), seen, context, *pieces)
    late = lax.all_gather(late, "ctx", axis=0, tiled=True)

    near = lax.all_to_all(early, "ctx", 0, 0, axis_index_groups=ys)
    raw = near[7, 4 * piece :].reshape(4, rows, cols)
    near = jnp.broadcast_to(near[None, :, : 4 * piece], (4, 8, 4 * piece, cols))
    own_raw = lax.all_to_all(raw, "ctx", 0, 0, axis_index_groups=xs)[3]
    near, own_raw = lax.optimization_barrier((near, own_raw))
    far = lax.all_to_all(near, "ctx", 0, 0, axis_index_groups=xs)
    kinds = [part((4, 8, piece, cols), 0, 0, i, 0) for i in range(4)]
    raw_rows = lax.all_gather(own_raw, "head", axis=1, tiled=True)
    queries = call(
        query_kernel,
        shape((ctxs, rows, cols), bf16),
        raw_rows, gains[:1], far,
        specs=[VMEM, VMEM, kinds[0]],
    )
    queries = swap(queries, "ctx")
    step = 256
    keys, values = call(
        keyval_kernel,
        (shape((tokens, cols), bf16), shape((cols, tokens), bf16)),
        context, gains[:1], far, far,
        specs=[
            pl.BlockSpec((step, width), lambda i: (i, 0)),
            part((1, width), 0, 0),
            kinds[1],
            kinds[2],
        ],
        outs=(
            pl.BlockSpec((step, cols), lambda i: (i, 0)),
            pl.BlockSpec((cols, step), lambda i: (0, i)),
        ),
        grid=(tokens // step,),
    )

    is_last = (ctx_index == ctxs - 1).astype(jnp.int32)
    info = jnp.stack([valid_len[0], ctx_index * tokens, is_last])
    sent = call(
        attend_kernel,
        shape((ctxs, rows + TAIL, cols), bf16),
        info, seen, queries.reshape(latents, cols), keys, values,
        specs=[SMEM, VMEM, VMEM, VMEM, VMEM],
    )
    at = [0, 3 * cols, 4 * cols, 4 * cols + ff, 4 * cols + 2 * ff, lates]
    qkv_w, mix_w, gate_w, up_w, down_w = [late[:, i:j] for i, j in zip(at, at[1:])]
    got = swap(sent, "ctx")
    spot = lax.rem(ctx_index, cols // rows).reshape(1)
    chunk = shape((heads, rows, cols), bf16)
    own = shape((rows, cols), bf16)
    terms = call(
        merge_kernel, chunk, spot, got, far, specs=[SMEM, VMEM, kinds[3]]
    )
    first, wide = call(add_kernel, (own, chunk), own_raw, swap(terms, "head"))
    query, pair = call(
        latent_kernel,
        (own, shape((ctxs, rows, 2 * cols), bf16)),
        swap(wide, "head"), gains[1:2], qkv_w,
    )
    place = lax.dynamic_slice_in_dim(last_visible, ctx_index * rows, rows, 0).reshape(rows, 1)
    pair, gate_w = lax.optimization_barrier((swap(pair, "ctx"), gate_w))
    terms = call(mix_kernel, chunk, place, seen, query, pair, mix_w)
    terms, up_w = lax.optimization_barrier((swap(terms, "head"), up_w))
    second, wide = call(add_kernel, (own, chunk), first, terms)
    terms = call(
        feed_kernel, chunk, swap(wide, "head"), gains[2:3], gate_w, up_w, down_w
    )
    return call(last_kernel, own, second, swap(terms, "head"))


def solution(mesh):
    in_specs = (
        P("ctx", None),
        P(None, "ctx", "head"),
        P("head", "ctx"),
        P(None, "ctx", "head"),
        P("head", "ctx"),
        P(None, "ctx", "head"),
        P("head", "ctx"),
        P(),
        P("ctx"),
        P(),
    )
    out_specs = P("ctx", "head")
    return jax.shard_map(body, mesh=mesh, in_specs=in_specs, out_specs=out_specs, check_vma=False)
```

```python
import jax
import jax.numpy as jnp
from jax import lax
from jax.experimental import pallas as pl
from jax.experimental.pallas import tpu as pltpu
from jax.sharding import PartitionSpec as P

HD = 128
epsilon = 1e-05
masked_score = -1e30
score_scale = HD ** (-0.5)
f32 = jnp.float32
bf16 = jnp.bfloat16
TAIL = 8
LATE = 58
LOG2E = 1.4426950408889634
VMEM = pl.BlockSpec(memory_space=pltpu.VMEM)
SMEM = pl.BlockSpec(memory_space=pltpu.SMEM)


def nt(a, b):
    return lax.dot_general(a, b, (((1,), (1,)), ((), ())), preferred_element_type=f32)


def nn(a, b):
    return jnp.dot(a, b, preferred_element_type=f32)


def call(kernel, out_shape, *args, specs=None, outs=None, grid=(1,), room=16):
    return pl.pallas_call(
        kernel,
        grid=grid,
        out_shape=out_shape,
        in_specs=specs if specs is not None else [VMEM] * len(args),
        out_specs=outs if outs is not None else jax.tree.map(lambda _: VMEM, out_shape),
        compiler_params=pltpu.CompilerParams(vmem_limit_bytes=room * 2**20),
    )(*args)


def part(shape, *index):
    return pl.BlockSpec(shape, lambda i: index)


def pack_kernel(attn_ref, out_w_ref, latent_ref, latent_out_ref, mlp_ref, down_ref, early_ref, mid_ref, late_ref):
    for i, block in enumerate([attn_ref[0], attn_ref[1], attn_ref[2]]):
        early_ref[:, i] = jnp.broadcast_to(block[None], (early_ref.shape[0],) + block.shape)
    for ref, blocks in (
        (mid_ref, [down_ref[...]] + [latent_ref[i] for i in range(3)] + [latent_out_ref[...], out_w_ref[...]]),
        (late_ref, [mlp_ref[0], mlp_ref[1]]),
    ):
        at = 0
        for block in blocks:
            ref[:, at : at + block.shape[1]] = block
            at += block.shape[1]


def whole(x):
    return part(x.shape, *[0] * x.ndim)


def unit_rows(rows, gain):
    wide = rows.astype(f32)
    scale = lax.rsqrt(jnp.mean(wide * wide, axis=1, keepdims=True) + epsilon)
    return (wide * scale * gain).astype(bf16)


def joined(w_ref):
    return w_ref[...].reshape(-1, w_ref.shape[-1])


def query_kernel(rows_ref, gain_ref, w_ref, out_ref):
    query = nn(unit_rows(rows_ref[...], gain_ref[...]), joined(w_ref)).astype(bf16)
    out_ref[...] = jnp.broadcast_to(query[None], out_ref.shape)


def keyval_kernel(rows_ref, gain_ref, k_w_ref, v_w_ref, key_ref, value_ref):
    rows = unit_rows(rows_ref[...], gain_ref[...])
    key_ref[...] = nn(rows, joined(k_w_ref)).astype(bf16)
    value_ref[...] = nn(rows, joined(v_w_ref)).T.astype(bf16)


def attend_kernel(info_ref, *refs):
    is_last = info_ref[2] == 1
    pl.when(is_last)(lambda: attend(True, info_ref, *refs))
    pl.when(jnp.logical_not(is_last))(lambda: attend(False, info_ref, *refs))


def attend(last, info_ref, seen_ref, q_ref, k_ref, v_ref, out_ref):
    keys, cols = k_ref.shape
    count, rows = out_ref.shape[0], out_ref.shape[1] - TAIL
    step = 256
    chunks = step // rows
    bias = jnp.where(
        lax.broadcasted_iota(jnp.int32, (keys, 1), 0) < info_ref[0], 0.0, masked_score
    )
    for t in range(count * rows // step):
        at = slice(t * step, (t + 1) * step)
        score = nt(k_ref[...], q_ref[at, :]) + bias
        if last:
            position = lax.broadcasted_iota(jnp.int32, (keys, step), 0) + info_ref[1]
            score = jnp.where(position <= seen_ref[:, at], score, masked_score)
        top = jnp.max(score, axis=0, keepdims=True)
        prob = jnp.exp2((score - top) * (score_scale * LOG2E))
        total = jnp.sum(prob, axis=0, keepdims=True)
        out = (nn(v_ref[...], prob.astype(bf16)) / total).T
        out = out.reshape(chunks, rows, cols)
        lse = top * score_scale + jnp.log(total)
        high = lse.astype(bf16).astype(f32)
        middle = (lse - high).astype(bf16).astype(f32)
        low = lse - high - middle
        pieces = jnp.concatenate([high, middle, low, jnp.zeros((TAIL - 3, step), f32)])
        per = cols // rows
        for g in range(chunks):
            tail = pieces[:, g // per * cols : (g // per + 1) * cols]
            out_ref[t * chunks + g] = jnp.concatenate([out[g], tail]).astype(bf16)


def merge_kernel(info_ref, got_ref, w_ref, out_ref):
    count, height, cols = got_ref.shape
    rows = height - TAIL
    got = got_ref[...].astype(f32)
    lse = jnp.sum(got[:, rows:, :], axis=1)
    weight = jnp.exp(lse - jnp.max(lse, axis=0, keepdims=True))
    weight = (weight / jnp.sum(weight, axis=0, keepdims=True)).T
    own = jnp.zeros((rows, count), f32)
    for i in range(cols // rows):
        own = jnp.where(info_ref[0] == i, weight[i * rows : (i + 1) * rows, :], own)
    total = jnp.zeros((rows, cols), f32)
    for s in range(count):
        total += own[:, s : s + 1] * got[s, :rows, :]
    project(total.astype(bf16), lambda h: w_ref[h * cols : (h + 1) * cols, :], out_ref)


def project(acts, weight_rows, out_ref):
    for h in range(out_ref.shape[0]):
        out_ref[h] = nt(acts, weight_rows(h)).astype(bf16)


def add_kernel(base_ref, terms_ref, out_ref, wide_ref):
    total = base_ref[...].astype(f32) + jnp.sum(terms_ref[...].astype(f32), axis=0)
    out_ref[...] = total.astype(bf16)
    wide_ref[...] = jnp.broadcast_to(total.astype(bf16)[None], wide_ref.shape)


def last_kernel(base_ref, terms_ref, out_ref):
    total = base_ref[...].astype(f32) + jnp.sum(terms_ref[...].astype(f32), axis=0)
    out_ref[...] = total.astype(bf16)


def unit(all_ref, gain_ref):
    rows = jnp.concatenate([all_ref[h] for h in range(all_ref.shape[0])], axis=1)
    return unit_rows(rows, gain_ref[...])


def latent_kernel(all_ref, gain_ref, w_ref, q_ref, pair_ref):
    qkv = nn(unit(all_ref, gain_ref), w_ref[...]).astype(bf16)
    cols = q_ref.shape[1]
    q_ref[...] = qkv[:, :cols]
    pair_ref[...] = jnp.broadcast_to(qkv[:, cols:][None], pair_ref.shape)


def mix_kernel(own_ref, seen_ref, q_ref, pair_ref, w_ref, out_ref):
    cols = q_ref.shape[1]
    pair = pair_ref[...].reshape(-1, 2 * cols)
    seen = seen_ref[...] <= own_ref[...]
    score = jnp.where(seen, nt(q_ref[...], pair[:, :cols]) * score_scale, masked_score)
    prob = jnp.where(seen, jnp.exp(score - jnp.max(score, axis=1, keepdims=True)), 0.0)
    prob = (prob / jnp.sum(prob, axis=1, keepdims=True)).astype(bf16)
    mixed = nn(prob, pair[:, cols:]).astype(bf16)
    project(mixed, lambda h: w_ref[h * cols : (h + 1) * cols, :], out_ref)


def feed_kernel(all_ref, gain_ref, w_ref, down_ref, out_ref):
    acts = unit(all_ref, gain_ref)
    hidden = down_ref.shape[1]
    gate = nn(acts, w_ref[:, :hidden])
    hidden = (gate / (1.0 + jnp.exp(-gate)) * nn(acts, w_ref[:, hidden:])).astype(bf16)
    cols = out_ref.shape[2]
    project(hidden, lambda h: down_ref[h * cols : (h + 1) * cols, :], out_ref)


def swap(x, axis):
    return lax.all_to_all(x, axis, 0, 0)


def body(
    context, w_attn, w_out, w_latent, w_latent_out, w_mlp, w_down, gains, valid_len, last_visible
):
    tokens, width = context.shape
    cols = w_attn.shape[2]
    ff = w_mlp.shape[2]
    latents = last_visible.shape[0]
    ctxs = lax.axis_size("ctx")
    heads = lax.axis_size("head")
    rows = latents // ctxs
    ctx_index = lax.axis_index("ctx")
    shape = jax.ShapeDtypeStruct
    ys = [[i * 8 + j for j in range(8)] for i in range(4)]
    xs = [[i * 8 + j for i in range(4)] for j in range(8)]

    piece = w_attn.shape[1]
    mids = ff + 5 * cols
    pieces = (w_attn, w_out.T, w_latent, w_latent_out.T, w_mlp, w_down.T)
    early, mid, late = call(
        pack_kernel,
        (
            shape((8, 3, piece, cols), bf16),
            shape((piece, mids), bf16),
            shape((piece, 2 * ff), bf16),
        ),
        *pieces,
        specs=[whole(x) for x in pieces],
        outs=(VMEM, part((piece, mids), 0, 0), part((piece, 2 * ff), 0, 0)),
        room=LATE,
    )
    mid = lax.all_gather(mid, "ctx", axis=0, tiled=True)

    near = lax.all_to_all(early, "ctx", 0, 0, axis_index_groups=ys)
    pick = jnp.clip(last_visible - (ctxs - 1) * tokens, 0, tokens - 1)
    mine = lax.dynamic_slice_in_dim(context, lax.axis_index("head") * cols, cols, 1)
    raw = jnp.take(mine, pick, axis=0, mode="clip").reshape(ctxs, rows, cols)
    near, late, raw = lax.optimization_barrier((near, late, raw))
    late = lax.all_gather(late, "ctx", axis=0, tiled=True)
    own_raw = swap(raw, "ctx")[ctxs - 1]
    near = jnp.broadcast_to(near[None], (4,) + near.shape)
    near, own_raw = lax.optimization_barrier((near, own_raw))
    far = lax.all_to_all(near, "ctx", 0, 0, axis_index_groups=xs)
    kinds = [part((4, 8, 1, piece, cols), 0, 0, i, 0, 0) for i in range(3)]
    raw_rows = lax.all_gather(own_raw, "head", axis=1, tiled=True)
    queries = call(
        query_kernel,
        shape((ctxs, rows, cols), bf16),
        raw_rows, gains[:1], far,
        specs=[VMEM, VMEM, kinds[0]],
    )
    queries = swap(queries, "ctx")
    step = 256
    keys, values = call(
        keyval_kernel,
        (shape((tokens, cols), bf16), shape((cols, tokens), bf16)),
        context, gains[:1], far, far,
        specs=[
            pl.BlockSpec((step, width), lambda i: (i, 0)),
            part((1, width), 0, 0),
            kinds[1],
            kinds[2],
        ],
        outs=(
            pl.BlockSpec((step, cols), lambda i: (i, 0)),
            pl.BlockSpec((cols, step), lambda i: (0, i)),
        ),
        grid=(tokens // step,),
    )

    is_last = (ctx_index == ctxs - 1).astype(jnp.int32)
    info = jnp.stack([valid_len[0], ctx_index * tokens, is_last])
    seen = last_visible.reshape(1, latents)
    sent = call(
        attend_kernel,
        shape((ctxs, rows + TAIL, cols), bf16),
        info, seen, queries.reshape(latents, cols), keys, values,
        specs=[SMEM, VMEM, VMEM, VMEM, VMEM],
    )
    got = swap(sent, "ctx")
    cut = [0, ff, ff + 3 * cols, ff + 4 * cols, mids]
    down, qkv_w, mix_w, out_w = [mid[:, i:j] for i, j in zip(cut, cut[1:])]
    spot = lax.rem(ctx_index, cols // rows).reshape(1)
    chunk = shape((heads, rows, cols), bf16)
    own = shape((rows, cols), bf16)
    terms = call(
        merge_kernel, chunk, spot, got, out_w, specs=[SMEM, VMEM, VMEM]
    )
    first, wide = call(add_kernel, (own, chunk), own_raw, swap(terms, "head"))
    query, pair = call(
        latent_kernel,
        (own, shape((ctxs, rows, 2 * cols), bf16)),
        swap(wide, "head"), gains[1:2], qkv_w,
    )
    place = lax.dynamic_slice_in_dim(last_visible, ctx_index * rows, rows, 0).reshape(rows, 1)
    terms = call(
        mix_kernel,
        chunk,
        place, seen, query, swap(pair, "ctx"), mix_w,
    )
    second, wide = call(add_kernel, (own, chunk), first, swap(terms, "head"))
    terms = call(
        feed_kernel,
        chunk,
        swap(wide, "head"), gains[2:3], late, down,
    )
    return call(last_kernel, own, second, swap(terms, "head"))


def solution(mesh):
    in_specs = (
        P("ctx", None),
        P(None, "ctx", "head"),
        P("head", "ctx"),
        P(None, "ctx", "head"),
        P("head", "ctx"),
        P(None, "ctx", "head"),
        P("head", "ctx"),
        P(),
        P("ctx"),
        P(),
    )
    out_specs = P("ctx", "head")
    return jax.shard_map(body, mesh=mesh, in_specs=in_specs, out_specs=out_specs, check_vma=False)
```

```python
import jax
import jax.numpy as jnp
from jax import lax
from jax.experimental import pallas as pl
from jax.experimental.pallas import tpu as pltpu
from jax.sharding import PartitionSpec as P

HD = 128
epsilon = 1e-05
masked_score = -1e30
score_scale = HD ** (-0.5)
f32 = jnp.float32
bf16 = jnp.bfloat16
TAIL = 8
LATE = 58
LOG2E = 1.4426950408889634
VMEM = pl.BlockSpec(memory_space=pltpu.VMEM)
SMEM = pl.BlockSpec(memory_space=pltpu.SMEM)


def nt(a, b):
    return lax.dot_general(a, b, (((1,), (1,)), ((), ())), preferred_element_type=f32)


def nn(a, b):
    return jnp.dot(a, b, preferred_element_type=f32)


def call(kernel, out_shape, *args, specs=None, outs=None, grid=(1,), room=16):
    return pl.pallas_call(
        kernel,
        grid=grid,
        out_shape=out_shape,
        in_specs=specs if specs is not None else [VMEM] * len(args),
        out_specs=outs if outs is not None else jax.tree.map(lambda _: VMEM, out_shape),
        compiler_params=pltpu.CompilerParams(vmem_limit_bytes=room * 2**20),
    )(*args)


def part(shape, *index):
    return pl.BlockSpec(shape, lambda i: index)


def pack_kernel(attn_ref, out_w_ref, latent_ref, latent_out_ref, mlp_ref, down_ref, early_ref, mid_ref, late_ref):
    for i, block in enumerate([attn_ref[0], attn_ref[1], attn_ref[2]]):
        early_ref[:, i] = jnp.broadcast_to(block[None], (early_ref.shape[0],) + block.shape)
    for ref, blocks in (
        (
            mid_ref,
            [mlp_ref[0], mlp_ref[1]]
            + [latent_ref[i] for i in range(3)]
            + [latent_out_ref[...], out_w_ref[...]],
        ),
        (late_ref, [down_ref[...]]),
    ):
        at = 0
        for block in blocks:
            ref[:, at : at + block.shape[1]] = block
            at += block.shape[1]


def whole(x):
    return part(x.shape, *[0] * x.ndim)


def unit_rows(rows, gain):
    wide = rows.astype(f32)
    scale = lax.rsqrt(jnp.mean(wide * wide, axis=1, keepdims=True) + epsilon)
    return (wide * scale * gain).astype(bf16)


def joined(w_ref):
    return w_ref[...].reshape(-1, w_ref.shape[-1])


def query_kernel(rows_ref, gain_ref, w_ref, out_ref):
    query = nn(unit_rows(rows_ref[...], gain_ref[...]), joined(w_ref)).astype(bf16)
    out_ref[...] = jnp.broadcast_to(query[None], out_ref.shape)


def keyval_kernel(rows_ref, gain_ref, k_w_ref, v_w_ref, key_ref, value_ref):
    rows = unit_rows(rows_ref[...], gain_ref[...])
    key_ref[...] = nn(rows, joined(k_w_ref)).astype(bf16)
    value_ref[...] = nn(rows, joined(v_w_ref)).T.astype(bf16)


def attend_kernel(info_ref, *refs):
    is_last = info_ref[2] == 1
    pl.when(is_last)(lambda: attend(True, info_ref, *refs))
    pl.when(jnp.logical_not(is_last))(lambda: attend(False, info_ref, *refs))


def attend(last, info_ref, seen_ref, q_ref, k_ref, v_ref, out_ref):
    keys, cols = k_ref.shape
    count, rows = out_ref.shape[0], out_ref.shape[1] - TAIL
    step = 256
    chunks = step // rows
    bias = jnp.where(
        lax.broadcasted_iota(jnp.int32, (keys, 1), 0) < info_ref[0], 0.0, masked_score
    )
    for t in range(count * rows // step):
        at = slice(t * step, (t + 1) * step)
        score = nt(k_ref[...], q_ref[at, :]) + bias
        if last:
            position = lax.broadcasted_iota(jnp.int32, (keys, step), 0) + info_ref[1]
            score = jnp.where(position <= seen_ref[:, at], score, masked_score)
        top = jnp.max(score, axis=0, keepdims=True)
        prob = jnp.exp2((score - top) * (score_scale * LOG2E))
        total = jnp.sum(prob, axis=0, keepdims=True)
        out = (nn(v_ref[...], prob.astype(bf16)) / total).T
        out = out.reshape(chunks, rows, cols)
        lse = top * score_scale + jnp.log(total)
        high = lse.astype(bf16).astype(f32)
        middle = (lse - high).astype(bf16).astype(f32)
        low = lse - high - middle
        pieces = jnp.concatenate([high, middle, low, jnp.zeros((TAIL - 3, step), f32)])
        per = cols // rows
        for g in range(chunks):
            tail = pieces[:, g // per * cols : (g // per + 1) * cols]
            out_ref[t * chunks + g] = jnp.concatenate([out[g], tail]).astype(bf16)


def merge_kernel(info_ref, got_ref, w_ref, out_ref):
    count, height, cols = got_ref.shape
    rows = height - TAIL
    got = got_ref[...].astype(f32)
    lse = jnp.sum(got[:, rows:, :], axis=1)
    weight = jnp.exp(lse - jnp.max(lse, axis=0, keepdims=True))
    weight = (weight / jnp.sum(weight, axis=0, keepdims=True)).T
    own = jnp.zeros((rows, count), f32)
    for i in range(cols // rows):
        own = jnp.where(info_ref[0] == i, weight[i * rows : (i + 1) * rows, :], own)
    total = jnp.zeros((rows, cols), f32)
    for s in range(count):
        total += own[:, s : s + 1] * got[s, :rows, :]
    project(total.astype(bf16), lambda h: w_ref[h * cols : (h + 1) * cols, :], out_ref)


def project(acts, weight_rows, out_ref):
    for h in range(out_ref.shape[0]):
        out_ref[h] = nt(acts, weight_rows(h)).astype(bf16)


def add_kernel(base_ref, terms_ref, out_ref, wide_ref):
    total = base_ref[...].astype(f32) + jnp.sum(terms_ref[...].astype(f32), axis=0)
    out_ref[...] = total.astype(bf16)
    wide_ref[...] = jnp.broadcast_to(total.astype(bf16)[None], wide_ref.shape)


def last_kernel(base_ref, terms_ref, out_ref):
    total = base_ref[...].astype(f32) + jnp.sum(terms_ref[...].astype(f32), axis=0)
    out_ref[...] = total.astype(bf16)


def unit(all_ref, gain_ref):
    rows = jnp.concatenate([all_ref[h] for h in range(all_ref.shape[0])], axis=1)
    return unit_rows(rows, gain_ref[...])


def latent_kernel(all_ref, gain_ref, w_ref, q_ref, pair_ref):
    qkv = nn(unit(all_ref, gain_ref), w_ref[...]).astype(bf16)
    cols = q_ref.shape[1]
    q_ref[...] = qkv[:, :cols]
    pair_ref[...] = jnp.broadcast_to(qkv[:, cols:][None], pair_ref.shape)


def mix_kernel(own_ref, seen_ref, q_ref, pair_ref, w_ref, out_ref):
    cols = q_ref.shape[1]
    pair = pair_ref[...].reshape(-1, 2 * cols)
    seen = seen_ref[...] <= own_ref[...]
    score = jnp.where(seen, nt(q_ref[...], pair[:, :cols]) * score_scale, masked_score)
    prob = jnp.where(seen, jnp.exp(score - jnp.max(score, axis=1, keepdims=True)), 0.0)
    prob = (prob / jnp.sum(prob, axis=1, keepdims=True)).astype(bf16)
    mixed = nn(prob, pair[:, cols:]).astype(bf16)
    project(mixed, lambda h: w_ref[h * cols : (h + 1) * cols, :], out_ref)


def hidden_kernel(all_ref, gain_ref, gate_ref, up_ref, out_ref):
    acts = unit(all_ref, gain_ref)
    gate = nn(acts, gate_ref[...])
    out_ref[...] = (gate / (1.0 + jnp.exp(-gate)) * nn(acts, up_ref[...])).astype(bf16)


def down_kernel(acts_ref, w_ref, out_ref):
    cols = out_ref.shape[2]
    project(acts_ref[...], lambda h: w_ref[h * cols : (h + 1) * cols, :], out_ref)


def swap(x, axis):
    return lax.all_to_all(x, axis, 0, 0)


def body(
    context, w_attn, w_out, w_latent, w_latent_out, w_mlp, w_down, gains, valid_len, last_visible
):
    tokens, width = context.shape
    cols = w_attn.shape[2]
    ff = w_mlp.shape[2]
    latents = last_visible.shape[0]
    ctxs = lax.axis_size("ctx")
    heads = lax.axis_size("head")
    rows = latents // ctxs
    ctx_index = lax.axis_index("ctx")
    shape = jax.ShapeDtypeStruct
    ys = [[i * 8 + j for j in range(8)] for i in range(4)]
    xs = [[i * 8 + j for i in range(4)] for j in range(8)]

    piece = w_attn.shape[1]
    mids = 2 * ff + 5 * cols
    pieces = (w_attn, w_out.T, w_latent, w_latent_out.T, w_mlp, w_down.T)
    early, mid, late = call(
        pack_kernel,
        (
            shape((8, 3, piece, cols), bf16),
            shape((piece, mids), bf16),
            shape((piece, ff), bf16),
        ),
        *pieces,
        specs=[whole(x) for x in pieces],
        outs=(VMEM, part((piece, mids), 0, 0), part((piece, ff), 0, 0)),
        room=LATE,
    )
    mid = lax.all_gather(mid, "ctx", axis=0, tiled=True)

    near = lax.all_to_all(early, "ctx", 0, 0, axis_index_groups=ys)
    pick = jnp.clip(last_visible - (ctxs - 1) * tokens, 0, tokens - 1)
    mine = lax.dynamic_slice_in_dim(context, lax.axis_index("head") * cols, cols, 1)
    raw = jnp.take(mine, pick, axis=0, mode="clip").reshape(ctxs, rows, cols)
    near, late, raw = lax.optimization_barrier((near, late, raw))
    late = lax.all_gather(late, "ctx", axis=0, tiled=True)
    own_raw = swap(raw, "ctx")[ctxs - 1]
    near = jnp.broadcast_to(near[None], (4,) + near.shape)
    near, own_raw = lax.optimization_barrier((near, own_raw))
    far = lax.all_to_all(near, "ctx", 0, 0, axis_index_groups=xs)
    kinds = [part((4, 8, 1, piece, cols), 0, 0, i, 0, 0) for i in range(3)]
    raw_rows = lax.all_gather(own_raw, "head", axis=1, tiled=True)
    queries = call(
        query_kernel,
        shape((ctxs, rows, cols), bf16),
        raw_rows, gains[:1], far,
        specs=[VMEM, VMEM, kinds[0]],
    )
    queries = swap(queries, "ctx")
    step = 256
    keys, values = call(
        keyval_kernel,
        (shape((tokens, cols), bf16), shape((cols, tokens), bf16)),
        context, gains[:1], far, far,
        specs=[
            pl.BlockSpec((step, width), lambda i: (i, 0)),
            part((1, width), 0, 0),
            kinds[1],
            kinds[2],
        ],
        outs=(
            pl.BlockSpec((step, cols), lambda i: (i, 0)),
            pl.BlockSpec((cols, step), lambda i: (0, i)),
        ),
        grid=(tokens // step,),
    )

    is_last = (ctx_index == ctxs - 1).astype(jnp.int32)
    info = jnp.stack([valid_len[0], ctx_index * tokens, is_last])
    seen = last_visible.reshape(1, latents)
    sent = call(
        attend_kernel,
        shape((ctxs, rows + TAIL, cols), bf16),
        info, seen, queries.reshape(latents, cols), keys, values,
        specs=[SMEM, VMEM, VMEM, VMEM, VMEM],
    )
    got = swap(sent, "ctx")
    cut = [0, ff, 2 * ff, 2 * ff + 3 * cols, 2 * ff + 4 * cols, mids]
    gate_w, up_w, qkv_w, mix_w, out_w = [mid[:, i:j] for i, j in zip(cut, cut[1:])]
    spot = lax.rem(ctx_index, cols // rows).reshape(1)
    chunk = shape((heads, rows, cols), bf16)
    own = shape((rows, cols), bf16)
    terms = call(
        merge_kernel, chunk, spot, got, out_w, specs=[SMEM, VMEM, VMEM]
    )
    first, wide = call(add_kernel, (own, chunk), own_raw, swap(terms, "head"))
    query, pair = call(
        latent_kernel,
        (own, shape((ctxs, rows, 2 * cols), bf16)),
        swap(wide, "head"), gains[1:2], qkv_w,
    )
    place = lax.dynamic_slice_in_dim(last_visible, ctx_index * rows, rows, 0).reshape(rows, 1)
    terms = call(
        mix_kernel,
        chunk,
        place, seen, query, swap(pair, "ctx"), mix_w,
    )
    second, wide = call(add_kernel, (own, chunk), first, swap(terms, "head"))
    wide = swap(wide, "head")
    hidden = call(
        hidden_kernel, shape((rows, ff), bf16), wide, gains[2:3], gate_w, up_w
    )
    terms = call(down_kernel, chunk, hidden, late)
    return call(last_kernel, own, second, swap(terms, "head"))


def solution(mesh):
    in_specs = (
        P("ctx", None),
        P(None, "ctx", "head"),
        P("head", "ctx"),
        P(None, "ctx", "head"),
        P("head", "ctx"),
        P(None, "ctx", "head"),
        P("head", "ctx"),
        P(),
        P("ctx"),
        P(),
    )
    out_specs = P("ctx", "head")
    return jax.shard_map(body, mesh=mesh, in_specs=in_specs, out_specs=out_specs, check_vma=False)
```

```python
import jax
import jax.numpy as jnp
from jax import lax
from jax.experimental import pallas as pl
from jax.experimental.pallas import tpu as pltpu
from jax.sharding import PartitionSpec as P

HD = 128
epsilon = 1e-05
masked_score = -1e30
score_scale = HD ** (-0.5)
f32 = jnp.float32
bf16 = jnp.bfloat16
TAIL = 8
LATE = 58
LOG2E = 1.4426950408889634
VMEM = pl.BlockSpec(memory_space=pltpu.VMEM)
SMEM = pl.BlockSpec(memory_space=pltpu.SMEM)


def nt(a, b):
    return lax.dot_general(a, b, (((1,), (1,)), ((), ())), preferred_element_type=f32)


def nn(a, b):
    return jnp.dot(a, b, preferred_element_type=f32)


def call(kernel, out_shape, *args, specs=None, outs=None, grid=(1,), room=16, scratch=()):
    return pl.pallas_call(
        kernel,
        grid=grid,
        out_shape=out_shape,
        in_specs=specs if specs is not None else [VMEM] * len(args),
        out_specs=outs if outs is not None else jax.tree.map(lambda _: VMEM, out_shape),
        scratch_shapes=scratch,
        compiler_params=pltpu.CompilerParams(vmem_limit_bytes=room * 2**20),
    )(*args)


def part(shape, *index):
    return pl.BlockSpec(shape, lambda i: index)


def pack_kernel(attn_ref, out_w_ref, latent_ref, latent_out_ref, mlp_ref, down_ref, early_ref, mid_ref, late_ref):
    for i, block in enumerate([attn_ref[0], attn_ref[1], attn_ref[2]]):
        early_ref[:, i] = jnp.broadcast_to(block[None], (early_ref.shape[0],) + block.shape)
    for ref, blocks in (
        (mid_ref, [down_ref[...]] + [latent_ref[i] for i in range(3)] + [latent_out_ref[...], out_w_ref[...]]),
        (late_ref, [mlp_ref[0], mlp_ref[1]]),
    ):
        at = 0
        for block in blocks:
            ref[:, at : at + block.shape[1]] = block
            at += block.shape[1]


def whole(x):
    return part(x.shape, *[0] * x.ndim)


def unit_rows(rows, gain):
    wide = rows.astype(f32)
    scale = lax.rsqrt(jnp.mean(wide * wide, axis=1, keepdims=True) + epsilon)
    return (wide * scale * gain).astype(bf16)


def joined(w_ref):
    return w_ref[...].reshape(-1, w_ref.shape[-1])


def query_kernel(rows_ref, gain_ref, w_ref, out_ref):
    query = nn(unit_rows(rows_ref[...], gain_ref[...]), joined(w_ref)).astype(bf16)
    out_ref[...] = jnp.broadcast_to(query[None], out_ref.shape)


def keyval_kernel(rows_ref, gain_ref, k_w_ref, v_w_ref, key_ref, value_ref):
    rows = unit_rows(rows_ref[...], gain_ref[...])
    key_ref[...] = nn(rows, joined(k_w_ref)).astype(bf16)
    value_ref[...] = nn(rows, joined(v_w_ref)).T.astype(bf16)


def attend_kernel(info_ref, *refs):
    is_last = info_ref[2] == 1
    pl.when(is_last)(lambda: attend(True, info_ref, *refs))
    pl.when(jnp.logical_not(is_last))(lambda: attend(False, info_ref, *refs))


def attend(last, info_ref, seen_ref, q_ref, k_ref, v_ref, out_ref):
    keys, cols = k_ref.shape
    count, rows = out_ref.shape[0], out_ref.shape[1] - TAIL
    step = 256
    chunks = step // rows
    bias = jnp.where(
        lax.broadcasted_iota(jnp.int32, (keys, 1), 0) < info_ref[0], 0.0, masked_score
    )
    for t in range(count * rows // step):
        at = slice(t * step, (t + 1) * step)
        score = nt(k_ref[...], q_ref[at, :]) + bias
        if last:
            position = lax.broadcasted_iota(jnp.int32, (keys, step), 0) + info_ref[1]
            score = jnp.where(position <= seen_ref[:, at], score, masked_score)
        top = jnp.max(score, axis=0, keepdims=True)
        prob = jnp.exp2((score - top) * (score_scale * LOG2E))
        total = jnp.sum(prob, axis=0, keepdims=True)
        out = (nn(v_ref[...], prob.astype(bf16)) / total).T
        out = out.reshape(chunks, rows, cols)
        lse = top * score_scale + jnp.log(total)
        high = lse.astype(bf16).astype(f32)
        middle = (lse - high).astype(bf16).astype(f32)
        low = lse - high - middle
        pieces = jnp.concatenate([high, middle, low, jnp.zeros((TAIL - 3, step), f32)])
        per = cols // rows
        for g in range(chunks):
            tail = pieces[:, g // per * cols : (g // per + 1) * cols]
            out_ref[t * chunks + g] = jnp.concatenate([out[g], tail]).astype(bf16)


def merge_kernel(info_ref, got_ref, w_ref, out_ref):
    count, height, cols = got_ref.shape
    rows = height - TAIL
    got = got_ref[...].astype(f32)
    lse = jnp.sum(got[:, rows:, :], axis=1)
    weight = jnp.exp(lse - jnp.max(lse, axis=0, keepdims=True))
    weight = (weight / jnp.sum(weight, axis=0, keepdims=True)).T
    own = jnp.zeros((rows, count), f32)
    for i in range(cols // rows):
        own = jnp.where(info_ref[0] == i, weight[i * rows : (i + 1) * rows, :], own)
    total = jnp.zeros((rows, cols), f32)
    for s in range(count):
        total += own[:, s : s + 1] * got[s, :rows, :]
    project(total.astype(bf16), lambda h: w_ref[h * cols : (h + 1) * cols, :], out_ref)


def project(acts, weight_rows, out_ref):
    for h in range(out_ref.shape[0]):
        out_ref[h] = nt(acts, weight_rows(h)).astype(bf16)


def add_kernel(base_ref, terms_ref, out_ref, wide_ref):
    total = base_ref[...].astype(f32) + jnp.sum(terms_ref[...].astype(f32), axis=0)
    out_ref[...] = total.astype(bf16)
    wide_ref[...] = jnp.broadcast_to(total.astype(bf16)[None], wide_ref.shape)


def last_kernel(base_ref, terms_ref, out_ref):
    total = base_ref[...].astype(f32) + jnp.sum(terms_ref[...].astype(f32), axis=0)
    out_ref[...] = total.astype(bf16)


def unit(all_ref, gain_ref):
    rows = jnp.concatenate([all_ref[h] for h in range(all_ref.shape[0])], axis=1)
    return unit_rows(rows, gain_ref[...])


def latent_kernel(all_ref, gain_ref, w_ref, q_ref, pair_ref):
    qkv = nn(unit(all_ref, gain_ref), w_ref[...]).astype(bf16)
    cols = q_ref.shape[1]
    q_ref[...] = qkv[:, :cols]
    pair_ref[...] = jnp.broadcast_to(qkv[:, cols:][None], pair_ref.shape)


def mix_kernel(own_ref, seen_ref, q_ref, pair_ref, w_ref, out_ref):
    cols = q_ref.shape[1]
    pair = pair_ref[...].reshape(-1, 2 * cols)
    seen = seen_ref[...] <= own_ref[...]
    score = jnp.where(seen, nt(q_ref[...], pair[:, :cols]) * score_scale, masked_score)
    prob = jnp.where(seen, jnp.exp(score - jnp.max(score, axis=1, keepdims=True)), 0.0)
    prob = (prob / jnp.sum(prob, axis=1, keepdims=True)).astype(bf16)
    mixed = nn(prob, pair[:, cols:]).astype(bf16)
    project(mixed, lambda h: w_ref[h * cols : (h + 1) * cols, :], out_ref)


def feed_kernel(all_ref, gain_ref, w_ref, down_ref, out_ref, acts_ref, sum_ref, hidden_ref):
    step = pl.program_id(0)
    blocks, _, size = acts_ref.shape
    cols = out_ref.shape[2]

    @pl.when(step == 0)
    def _():
        acts = unit(all_ref, gain_ref)
        for i in range(blocks):
            acts_ref[i] = acts[:, i * size : (i + 1) * size]
        sum_ref[...] = nn(acts_ref[0], w_ref[...])

    @pl.when((step > 0) & (step < blocks))
    def _():
        sum_ref[...] += nn(acts_ref[step], w_ref[...])

    @pl.when(step == blocks - 1)
    def _():
        gate, up = jnp.split(sum_ref[...], 2, axis=1)
        hidden_ref[...] = (gate / (1.0 + jnp.exp(-gate)) * up).astype(bf16)

    @pl.when(step >= blocks)
    def _():
        hidden = hidden_ref[...]
        per = down_ref.shape[0] // cols
        for h in range(per):
            term = nt(hidden, down_ref[h * cols : (h + 1) * cols, :]).astype(bf16)
            out_ref[(step - blocks) * per + h] = term


def swap(x, axis):
    return lax.all_to_all(x, axis, 0, 0)


def body(
    context, w_attn, w_out, w_latent, w_latent_out, w_mlp, w_down, gains, valid_len, last_visible
):
    tokens, width = context.shape
    cols = w_attn.shape[2]
    ff = w_mlp.shape[2]
    latents = last_visible.shape[0]
    ctxs = lax.axis_size("ctx")
    heads = lax.axis_size("head")
    rows = latents // ctxs
    ctx_index = lax.axis_index("ctx")
    shape = jax.ShapeDtypeStruct
    ys = [[i * 8 + j for j in range(8)] for i in range(4)]
    xs = [[i * 8 + j for i in range(4)] for j in range(8)]

    piece = w_attn.shape[1]
    mids = ff + 5 * cols
    pieces = (w_attn, w_out.T, w_latent, w_latent_out.T, w_mlp, w_down.T)
    early, mid, late = call(
        pack_kernel,
        (
            shape((8, 3, piece, cols), bf16),
            shape((piece, mids), bf16),
            shape((piece, 2 * ff), bf16),
        ),
        *pieces,
        specs=[whole(x) for x in pieces],
        outs=(VMEM, part((piece, mids), 0, 0), part((piece, 2 * ff), 0, 0)),
        room=LATE,
    )
    mid = lax.all_gather(mid, "ctx", axis=0, tiled=True)

    near = lax.all_to_all(early, "ctx", 0, 0, axis_index_groups=ys)
    pick = jnp.clip(last_visible - (ctxs - 1) * tokens, 0, tokens - 1)
    mine = lax.dynamic_slice_in_dim(context, lax.axis_index("head") * cols, cols, 1)
    raw = jnp.take(mine, pick, axis=0, mode="clip").reshape(ctxs, rows, cols)
    near, late, raw = lax.optimization_barrier((near, late, raw))
    late = lax.all_gather(late, "ctx", axis=0, tiled=True)
    own_raw = swap(raw, "ctx")[ctxs - 1]
    near = jnp.broadcast_to(near[None], (4,) + near.shape)
    near, own_raw = lax.optimization_barrier((near, own_raw))
    far = lax.all_to_all(near, "ctx", 0, 0, axis_index_groups=xs)
    kinds = [part((4, 8, 1, piece, cols), 0, 0, i, 0, 0) for i in range(3)]
    raw_rows = lax.all_gather(own_raw, "head", axis=1, tiled=True)
    queries = call(
        query_kernel,
        shape((ctxs, rows, cols), bf16),
        raw_rows, gains[:1], far,
        specs=[VMEM, VMEM, kinds[0]],
    )
    queries = swap(queries, "ctx")
    step = 256
    keys, values = call(
        keyval_kernel,
        (shape((tokens, cols), bf16), shape((cols, tokens), bf16)),
        context, gains[:1], far, far,
        specs=[
            pl.BlockSpec((step, width), lambda i: (i, 0)),
            part((1, width), 0, 0),
            kinds[1],
            kinds[2],
        ],
        outs=(
            pl.BlockSpec((step, cols), lambda i: (i, 0)),
            pl.BlockSpec((cols, step), lambda i: (0, i)),
        ),
        grid=(tokens // step,),
    )

    is_last = (ctx_index == ctxs - 1).astype(jnp.int32)
    info = jnp.stack([valid_len[0], ctx_index * tokens, is_last])
    seen = last_visible.reshape(1, latents)
    sent = call(
        attend_kernel,
        shape((ctxs, rows + TAIL, cols), bf16),
        info, seen, queries.reshape(latents, cols), keys, values,
        specs=[SMEM, VMEM, VMEM, VMEM, VMEM],
    )
    got = swap(sent, "ctx")
    cut = [0, ff, ff + 3 * cols, ff + 4 * cols, mids]
    _, qkv_w, mix_w, out_w = [mid[:, i:j] for i, j in zip(cut, cut[1:])]
    spot = lax.rem(ctx_index, cols // rows).reshape(1)
    chunk = shape((heads, rows, cols), bf16)
    own = shape((rows, cols), bf16)
    terms = call(
        merge_kernel, chunk, spot, got, out_w, specs=[SMEM, VMEM, VMEM]
    )
    first, wide = call(add_kernel, (own, chunk), own_raw, swap(terms, "head"))
    query, pair = call(
        latent_kernel,
        (own, shape((ctxs, rows, 2 * cols), bf16)),
        swap(wide, "head"), gains[1:2], qkv_w,
    )
    place = lax.dynamic_slice_in_dim(last_visible, ctx_index * rows, rows, 0).reshape(rows, 1)
    terms = call(
        mix_kernel,
        chunk,
        place, seen, query, swap(pair, "ctx"), mix_w,
    )
    second, wide = call(add_kernel, (own, chunk), first, swap(terms, "head"))
    terms = call(
        feed_kernel,
        chunk,
        swap(wide, "head"), gains[2:3], late, mid,
        specs=[
            VMEM,
            VMEM,
            pl.BlockSpec((width // 4, 2 * ff), lambda i: (jnp.minimum(i, 3), 0)),
            pl.BlockSpec((width // 4, ff), lambda i: (jnp.maximum(i - 4, 0), 0)),
        ],
        grid=(8,),
        room=LATE,
        scratch=[
            pltpu.VMEM((4, rows, width // 4), bf16),
            pltpu.VMEM((rows, 2 * ff), f32),
            pltpu.VMEM((rows, ff), bf16),
        ],
    )
    return call(last_kernel, own, second, swap(terms, "head"))


def solution(mesh):
    in_specs = (
        P("ctx", None),
        P(None, "ctx", "head"),
        P("head", "ctx"),
        P(None, "ctx", "head"),
        P("head", "ctx"),
        P(None, "ctx", "head"),
        P("head", "ctx"),
        P(),
        P("ctx"),
        P(),
    )
    out_specs = P("ctx", "head")
    return jax.shard_map(body, mesh=mesh, in_specs=in_specs, out_specs=out_specs, check_vma=False)
```

```python
import jax
import jax.numpy as jnp
from jax import lax
from jax.experimental import pallas as pl
from jax.experimental.pallas import tpu as pltpu
from jax.sharding import PartitionSpec as P

HD = 128
epsilon = 1e-05
masked_score = -1e30
score_scale = HD ** (-0.5)
f32 = jnp.float32
bf16 = jnp.bfloat16
TAIL = 8
LATE = 58
LOG2E = 1.4426950408889634
VMEM = pl.BlockSpec(memory_space=pltpu.VMEM)
SMEM = pl.BlockSpec(memory_space=pltpu.SMEM)


def nt(a, b):
    return lax.dot_general(a, b, (((1,), (1,)), ((), ())), preferred_element_type=f32)


def nn(a, b):
    return jnp.dot(a, b, preferred_element_type=f32)


def call(kernel, out_shape, *args, specs=None, outs=None, grid=(1,), room=16):
    return pl.pallas_call(
        kernel,
        grid=grid,
        out_shape=out_shape,
        in_specs=specs if specs is not None else [VMEM] * len(args),
        out_specs=outs if outs is not None else jax.tree.map(lambda _: VMEM, out_shape),
        compiler_params=pltpu.CompilerParams(vmem_limit_bytes=room * 2**20),
    )(*args)


def part(shape, *index):
    return pl.BlockSpec(shape, lambda i: index)


def pack_kernel(attn_ref, out_w_ref, latent_ref, latent_out_ref, mlp_ref, down_ref, early_ref, mid_ref, late_ref):
    for i, block in enumerate([attn_ref[0], attn_ref[1], attn_ref[2]]):
        early_ref[:, i] = jnp.broadcast_to(block[None], (early_ref.shape[0],) + block.shape)
    for ref, blocks in (
        (mid_ref, [down_ref[...]] + [latent_ref[i] for i in range(3)] + [latent_out_ref[...], out_w_ref[...]]),
        (late_ref, [mlp_ref[0], mlp_ref[1]]),
    ):
        at = 0
        for block in blocks:
            ref[:, at : at + block.shape[1]] = block
            at += block.shape[1]
    late_ref[:, at:] = jnp.zeros_like(late_ref[:, at:])


def whole(x):
    return part(x.shape, *[0] * x.ndim)


def unit_rows(rows, gain):
    wide = rows.astype(f32)
    scale = lax.rsqrt(jnp.mean(wide * wide, axis=1, keepdims=True) + epsilon)
    return (wide * scale * gain).astype(bf16)


def joined(w_ref):
    return w_ref[...].reshape(-1, w_ref.shape[-1])


def query_kernel(rows_ref, gain_ref, w_ref, out_ref):
    query = nn(unit_rows(rows_ref[...], gain_ref[...]), joined(w_ref)).astype(bf16)
    out_ref[...] = jnp.broadcast_to(query[None], out_ref.shape)


def keyval_kernel(rows_ref, gain_ref, k_w_ref, v_w_ref, key_ref, value_ref):
    rows = unit_rows(rows_ref[...], gain_ref[...])
    key_ref[...] = nn(rows, joined(k_w_ref)).astype(bf16)
    value_ref[...] = nn(rows, joined(v_w_ref)).T.astype(bf16)


def attend_kernel(info_ref, *refs):
    is_last = info_ref[2] == 1
    pl.when(is_last)(lambda: attend(True, info_ref, *refs))
    pl.when(jnp.logical_not(is_last))(lambda: attend(False, info_ref, *refs))


def attend(last, info_ref, seen_ref, q_ref, k_ref, v_ref, out_ref):
    keys, cols = k_ref.shape
    count, rows = out_ref.shape[0], out_ref.shape[1] - TAIL
    step = 256
    chunks = step // rows
    bias = jnp.where(
        lax.broadcasted_iota(jnp.int32, (keys, 1), 0) < info_ref[0], 0.0, masked_score
    )
    for t in range(count * rows // step):
        at = slice(t * step, (t + 1) * step)
        score = nt(k_ref[...], q_ref[at, :]) + bias
        if last:
            position = lax.broadcasted_iota(jnp.int32, (keys, step), 0) + info_ref[1]
            score = jnp.where(position <= seen_ref[:, at], score, masked_score)
        top = jnp.max(score, axis=0, keepdims=True)
        prob = jnp.exp2((score - top) * (score_scale * LOG2E))
        total = jnp.sum(prob, axis=0, keepdims=True)
        out = (nn(v_ref[...], prob.astype(bf16)) / total).T
        out = out.reshape(chunks, rows, cols)
        lse = top * score_scale + jnp.log(total)
        high = lse.astype(bf16).astype(f32)
        middle = (lse - high).astype(bf16).astype(f32)
        low = lse - high - middle
        pieces = jnp.concatenate([high, middle, low, jnp.zeros((TAIL - 3, step), f32)])
        per = cols // rows
        for g in range(chunks):
            tail = pieces[:, g // per * cols : (g // per + 1) * cols]
            out_ref[t * chunks + g] = jnp.concatenate([out[g], tail]).astype(bf16)


def merge_kernel(info_ref, got_ref, w_ref, out_ref):
    count, height, cols = got_ref.shape
    rows = height - TAIL
    got = got_ref[...].astype(f32)
    lse = jnp.sum(got[:, rows:, :], axis=1)
    weight = jnp.exp(lse - jnp.max(lse, axis=0, keepdims=True))
    weight = (weight / jnp.sum(weight, axis=0, keepdims=True)).T
    own = jnp.zeros((rows, count), f32)
    for i in range(cols // rows):
        own = jnp.where(info_ref[0] == i, weight[i * rows : (i + 1) * rows, :], own)
    total = jnp.zeros((rows, cols), f32)
    for s in range(count):
        total += own[:, s : s + 1] * got[s, :rows, :]
    project(total.astype(bf16), lambda h: w_ref[h * cols : (h + 1) * cols, :], out_ref)


def project(acts, weight_rows, out_ref):
    for h in range(out_ref.shape[0]):
        out_ref[h] = nt(acts, weight_rows(h)).astype(bf16)


def add_kernel(base_ref, terms_ref, out_ref, wide_ref):
    total = base_ref[...].astype(f32) + jnp.sum(terms_ref[...].astype(f32), axis=0)
    out_ref[...] = total.astype(bf16)
    wide_ref[...] = jnp.broadcast_to(total.astype(bf16)[None], wide_ref.shape)


def last_kernel(base_ref, terms_ref, out_ref):
    total = base_ref[...].astype(f32) + jnp.sum(terms_ref[...].astype(f32), axis=0)
    out_ref[...] = total.astype(bf16)


def unit(all_ref, gain_ref):
    rows = jnp.concatenate([all_ref[h] for h in range(all_ref.shape[0])], axis=1)
    return unit_rows(rows, gain_ref[...])


def latent_kernel(all_ref, gain_ref, w_ref, q_ref, pair_ref):
    qkv = nn(unit(all_ref, gain_ref), w_ref[...]).astype(bf16)
    cols = q_ref.shape[1]
    q_ref[...] = qkv[:, :cols]
    pair_ref[...] = jnp.broadcast_to(qkv[:, cols:][None], pair_ref.shape)


def mix_kernel(own_ref, seen_ref, q_ref, pair_ref, w_ref, out_ref):
    cols = q_ref.shape[1]
    pair = pair_ref[...].reshape(-1, 2 * cols)
    seen = seen_ref[...] <= own_ref[...]
    score = jnp.where(seen, nt(q_ref[...], pair[:, :cols]) * score_scale, masked_score)
    prob = jnp.where(seen, jnp.exp(score - jnp.max(score, axis=1, keepdims=True)), 0.0)
    prob = (prob / jnp.sum(prob, axis=1, keepdims=True)).astype(bf16)
    mixed = nn(prob, pair[:, cols:]).astype(bf16)
    project(mixed, lambda h: w_ref[h * cols : (h + 1) * cols, :], out_ref)


def feed_kernel(all_ref, gain_ref, w_ref, down_ref, out_ref):
    acts = unit(all_ref, gain_ref)
    ff = down_ref.shape[1]
    gate = nn(acts, w_ref[:, :ff])
    hidden = (gate / (1.0 + jnp.exp(-gate)) * nn(acts, w_ref[:, ff : 2 * ff])).astype(bf16)
    cols = out_ref.shape[2]
    project(hidden, lambda h: down_ref[h * cols : (h + 1) * cols, :], out_ref)


def swap(x, axis):
    return lax.all_to_all(x, axis, 0, 0)


def body(
    context, w_attn, w_out, w_latent, w_latent_out, w_mlp, w_down, gains, valid_len, last_visible
):
    tokens, width = context.shape
    cols = w_attn.shape[2]
    ff = w_mlp.shape[2]
    latents = last_visible.shape[0]
    ctxs = lax.axis_size("ctx")
    heads = lax.axis_size("head")
    rows = latents // ctxs
    ctx_index = lax.axis_index("ctx")
    shape = jax.ShapeDtypeStruct
    ys = [[i * 8 + j for j in range(8)] for i in range(4)]
    xs = [[i * 8 + j for i in range(4)] for j in range(8)]

    piece = w_attn.shape[1]
    mids = ff + 5 * cols
    pieces = (w_attn, w_out.T, w_latent, w_latent_out.T, w_mlp, w_down.T)
    early, mid, late = call(
        pack_kernel,
        (
            shape((8, 3, piece, cols), bf16),
            shape((piece, mids), bf16),
            shape((piece, mids), bf16),
        ),
        *pieces,
        specs=[whole(x) for x in pieces],
        outs=(VMEM, part((piece, mids), 0, 0), part((piece, mids), 0, 0)),
        room=LATE,
    )
    mid = lax.all_gather(mid, "ctx", axis=0, tiled=True)

    near = lax.all_to_all(early, "ctx", 0, 0, axis_index_groups=ys)
    pick = jnp.clip(last_visible - (ctxs - 1) * tokens, 0, tokens - 1)
    mine = lax.dynamic_slice_in_dim(context, lax.axis_index("head") * cols, cols, 1)
    raw = jnp.take(mine, pick, axis=0, mode="clip").reshape(ctxs, rows, cols)
    near, late, raw = lax.optimization_barrier((near, late, raw))
    late = lax.all_gather(late, "ctx", axis=0, tiled=True)
    own_raw = swap(raw, "ctx")[ctxs - 1]
    near = jnp.broadcast_to(near[None], (4,) + near.shape)
    near, own_raw = lax.optimization_barrier((near, own_raw))
    far = lax.all_to_all(near, "ctx", 0, 0, axis_index_groups=xs)
    kinds = [part((4, 8, 1, piece, cols), 0, 0, i, 0, 0) for i in range(3)]
    raw_rows = lax.all_gather(own_raw, "head", axis=1, tiled=True)
    queries = call(
        query_kernel,
        shape((ctxs, rows, cols), bf16),
        raw_rows, gains[:1], far,
        specs=[VMEM, VMEM, kinds[0]],
    )
    queries = swap(queries, "ctx")
    step = 256
    keys, values = call(
        keyval_kernel,
        (shape((tokens, cols), bf16), shape((cols, tokens), bf16)),
        context, gains[:1], far, far,
        specs=[
            pl.BlockSpec((step, width), lambda i: (i, 0)),
            part((1, width), 0, 0),
            kinds[1],
            kinds[2],
        ],
        outs=(
            pl.BlockSpec((step, cols), lambda i: (i, 0)),
            pl.BlockSpec((cols, step), lambda i: (0, i)),
        ),
        grid=(tokens // step,),
    )

    is_last = (ctx_index == ctxs - 1).astype(jnp.int32)
    info = jnp.stack([valid_len[0], ctx_index * tokens, is_last])
    seen = last_visible.reshape(1, latents)
    sent = call(
        attend_kernel,
        shape((ctxs, rows + TAIL, cols), bf16),
        info, seen, queries.reshape(latents, cols), keys, values,
        specs=[SMEM, VMEM, VMEM, VMEM, VMEM],
    )
    got = swap(sent, "ctx")
    cut = [0, ff, ff + 3 * cols, ff + 4 * cols, mids]
    down, qkv_w, mix_w, out_w = [mid[:, i:j] for i, j in zip(cut, cut[1:])]
    spot = lax.rem(ctx_index, cols // rows).reshape(1)
    chunk = shape((heads, rows, cols), bf16)
    own = shape((rows, cols), bf16)
    terms = call(
        merge_kernel, chunk, spot, got, out_w, specs=[SMEM, VMEM, VMEM]
    )
    first, wide = call(add_kernel, (own, chunk), own_raw, swap(terms, "head"))
    query, pair = call(
        latent_kernel,
        (own, shape((ctxs, rows, 2 * cols), bf16)),
        swap(wide, "head"), gains[1:2], qkv_w,
    )
    place = lax.dynamic_slice_in_dim(last_visible, ctx_index * rows, rows, 0).reshape(rows, 1)
    terms = call(
        mix_kernel,
        chunk,
        place, seen, query, swap(pair, "ctx"), mix_w,
    )
    second, wide = call(add_kernel, (own, chunk), first, swap(terms, "head"))
    terms = call(
        feed_kernel,
        chunk,
        swap(wide, "head"), gains[2:3], late, down,
    )
    return call(last_kernel, own, second, swap(terms, "head"))


def solution(mesh):
    in_specs = (
        P("ctx", None),
        P(None, "ctx", "head"),
        P("head", "ctx"),
        P(None, "ctx", "head"),
        P("head", "ctx"),
        P(None, "ctx", "head"),
        P("head", "ctx"),
        P(),
        P("ctx"),
        P(),
    )
    out_specs = P("ctx", "head")
    return jax.shard_map(body, mesh=mesh, in_specs=in_specs, out_specs=out_specs, check_vma=False)
```

```python
import jax
import jax.numpy as jnp
from jax import lax
from jax.experimental import pallas as pl
from jax.experimental.pallas import tpu as pltpu
from jax.sharding import PartitionSpec as P

HD = 128
epsilon = 1e-05
masked_score = -1e30
score_scale = HD ** (-0.5)
f32 = jnp.float32
bf16 = jnp.bfloat16
TAIL = 8
LATE = 58
LOG2E = 1.4426950408889634
VMEM = pl.BlockSpec(memory_space=pltpu.VMEM)
SMEM = pl.BlockSpec(memory_space=pltpu.SMEM)


def nt(a, b):
    return lax.dot_general(a, b, (((1,), (1,)), ((), ())), preferred_element_type=f32)


def nn(a, b):
    return jnp.dot(a, b, preferred_element_type=f32)


def call(kernel, out_shape, *args, specs=None, outs=None, grid=(1,), room=16):
    return pl.pallas_call(
        kernel,
        grid=grid,
        out_shape=out_shape,
        in_specs=specs if specs is not None else [VMEM] * len(args),
        out_specs=outs if outs is not None else jax.tree.map(lambda _: VMEM, out_shape),
        compiler_params=pltpu.CompilerParams(vmem_limit_bytes=room * 2**20),
    )(*args)


def part(shape, *index):
    return pl.BlockSpec(shape, lambda i: index)


def pack_kernel(attn_ref, out_w_ref, latent_ref, latent_out_ref, mlp_ref, down_ref, early_ref, late_ref):
    for i, block in enumerate([attn_ref[0], attn_ref[1], attn_ref[2], out_w_ref[...]]):
        early_ref[:, i] = jnp.broadcast_to(block[None], (early_ref.shape[0],) + block.shape)
    at = 0
    for block in [latent_ref[0], latent_ref[1], latent_ref[2], latent_out_ref[...], mlp_ref[0], mlp_ref[1], down_ref[...]]:
        late_ref[:, at : at + block.shape[1]] = block
        at += block.shape[1]


def whole(x):
    return part(x.shape, *[0] * x.ndim)


def unit_rows(rows, gain):
    wide = rows.astype(f32)
    scale = lax.rsqrt(jnp.mean(wide * wide, axis=1, keepdims=True) + epsilon)
    return (wide * scale * gain).astype(bf16)


def joined(w_ref):
    return w_ref[...].reshape(-1, w_ref.shape[-1])


def query_kernel(rows_ref, gain_ref, w_ref, out_ref):
    query = nn(unit_rows(rows_ref[...], gain_ref[...]), joined(w_ref)).astype(bf16)
    out_ref[...] = jnp.broadcast_to(query[None], out_ref.shape)


def keyval_kernel(rows_ref, gain_ref, k_w_ref, v_w_ref, key_ref, value_ref):
    rows = unit_rows(rows_ref[...], gain_ref[...])
    key_ref[...] = nn(rows, joined(k_w_ref)).astype(bf16)
    value_ref[...] = nn(rows, joined(v_w_ref)).T.astype(bf16)


def attend_kernel(info_ref, *refs):
    is_last = info_ref[2] == 1
    pl.when(is_last)(lambda: attend(True, info_ref, *refs))
    pl.when(jnp.logical_not(is_last))(lambda: attend(False, info_ref, *refs))


def attend(last, info_ref, seen_ref, q_ref, k_ref, v_ref, out_ref):
    keys, cols = k_ref.shape
    count, rows = out_ref.shape[0], out_ref.shape[1] - TAIL
    step = 256
    chunks = step // rows
    bias = jnp.where(
        lax.broadcasted_iota(jnp.int32, (keys, 1), 0) < info_ref[0], 0.0, masked_score
    )
    for t in range(count * rows // step):
        at = slice(t * step, (t + 1) * step)
        score = nt(k_ref[...], q_ref[at, :]) + bias
        if last:
            position = lax.broadcasted_iota(jnp.int32, (keys, step), 0) + info_ref[1]
            score = jnp.where(position <= seen_ref[:, at], score, masked_score)
        top = jnp.max(score, axis=0, keepdims=True)
        prob = jnp.exp2((score - top) * (score_scale * LOG2E))
        total = jnp.sum(prob, axis=0, keepdims=True)
        out = (nn(v_ref[...], prob.astype(bf16)) / total).T
        out = out.reshape(chunks, rows, cols)
        lse = top * score_scale + jnp.log(total)
        high = lse.astype(bf16).astype(f32)
        middle = (lse - high).astype(bf16).astype(f32)
        low = lse - high - middle
        pieces = jnp.concatenate([high, middle, low, jnp.zeros((TAIL - 3, step), f32)])
        per = cols // rows
        for g in range(chunks):
            tail = pieces[:, g // per * cols : (g // per + 1) * cols]
            out_ref[t * chunks + g] = jnp.concatenate([out[g], tail]).astype(bf16)


def merge_kernel(info_ref, got_ref, w_ref, out_ref):
    count, height, cols = got_ref.shape
    rows = height - TAIL
    got = got_ref[...].astype(f32)
    lse = jnp.sum(got[:, rows:, :], axis=1)
    weight = jnp.exp(lse - jnp.max(lse, axis=0, keepdims=True))
    weight = (weight / jnp.sum(weight, axis=0, keepdims=True)).T
    own = jnp.zeros((rows, count), f32)
    for i in range(cols // rows):
        own = jnp.where(info_ref[0] == i, weight[i * rows : (i + 1) * rows, :], own)
    total = jnp.zeros((rows, cols), f32)
    for s in range(count):
        total += own[:, s : s + 1] * got[s, :rows, :]
    project(total.astype(bf16), lambda h: w_ref[h * cols : (h + 1) * cols, :], out_ref)


def project(acts, weight_rows, out_ref):
    for h in range(out_ref.shape[0]):
        out_ref[h] = nt(acts, weight_rows(h)).astype(bf16)


def add_kernel(base_ref, terms_ref, out_ref, wide_ref):
    total = base_ref[...].astype(f32) + jnp.sum(terms_ref[...].astype(f32), axis=0)
    out_ref[...] = total.astype(bf16)
    wide_ref[...] = jnp.broadcast_to(total.astype(bf16)[None], wide_ref.shape)


def last_kernel(base_ref, terms_ref, out_ref):
    total = base_ref[...].astype(f32) + jnp.sum(terms_ref[...].astype(f32), axis=0)
    out_ref[...] = total.astype(bf16)


def unit(all_ref, gain_ref):
    rows = jnp.concatenate([all_ref[h] for h in range(all_ref.shape[0])], axis=1)
    return unit_rows(rows, gain_ref[...])


def latent_kernel(all_ref, gain_ref, w_ref, q_ref, pair_ref):
    qkv = nn(unit(all_ref, gain_ref), w_ref[...]).astype(bf16)
    cols = q_ref.shape[1]
    q_ref[...] = qkv[:, :cols]
    pair_ref[...] = jnp.broadcast_to(qkv[:, cols:][None], pair_ref.shape)


def mix_kernel(own_ref, seen_ref, q_ref, pair_ref, w_ref, out_ref):
    cols = q_ref.shape[1]
    pair = pair_ref[...].reshape(-1, 2 * cols)
    seen = seen_ref[...] <= own_ref[...]
    score = jnp.where(seen, nt(q_ref[...], pair[:, :cols]) * score_scale, masked_score)
    prob = jnp.where(seen, jnp.exp(score - jnp.max(score, axis=1, keepdims=True)), 0.0)
    prob = (prob / jnp.sum(prob, axis=1, keepdims=True)).astype(bf16)
    mixed = nn(prob, pair[:, cols:]).astype(bf16)
    project(mixed, lambda h: w_ref[h * cols : (h + 1) * cols, :], out_ref)


def feed_kernel(all_ref, gain_ref, w_ref, down_ref, out_ref):
    acts = unit(all_ref, gain_ref)
    hidden = down_ref.shape[1]
    gate = nn(acts, w_ref[:, :hidden])
    hidden = (gate / (1.0 + jnp.exp(-gate)) * nn(acts, w_ref[:, hidden:])).astype(bf16)
    cols = out_ref.shape[2]
    project(hidden, lambda h: down_ref[h * cols : (h + 1) * cols, :], out_ref)


def swap(x, axis):
    return lax.all_to_all(x, axis, 0, 0)


def body(
    context, w_attn, w_out, w_latent, w_latent_out, w_mlp, w_down, gains, valid_len, last_visible
):
    tokens, width = context.shape
    cols = w_attn.shape[2]
    ff = w_mlp.shape[2]
    latents = last_visible.shape[0]
    ctxs = lax.axis_size("ctx")
    heads = lax.axis_size("head")
    rows = latents // ctxs
    ctx_index = lax.axis_index("ctx")
    shape = jax.ShapeDtypeStruct
    ys = [[i * 8 + j for j in range(8)] for i in range(4)]
    xs = [[i * 8 + j for i in range(4)] for j in range(8)]

    piece = w_attn.shape[1]
    lates = 4 * cols + 3 * ff
    pieces = (w_attn, w_out.T, w_latent, w_latent_out.T, w_mlp, w_down.T)
    early, late = call(
        pack_kernel,
        (shape((8, 4, piece, cols), bf16), shape((piece, lates), bf16)),
        *pieces,
        specs=[whole(x) for x in pieces],
        outs=(VMEM, part((piece, lates), 0, 0)),
        room=LATE,
    )

    pick = jnp.clip(last_visible - (ctxs - 1) * tokens, 0, tokens - 1)
    near = lax.all_to_all(early, "ctx", 0, 0, axis_index_groups=ys)
    mine = lax.dynamic_slice_in_dim(context, lax.axis_index("head") * cols, cols, 1)
    raw = jnp.take(mine, pick, axis=0, mode="clip").reshape(ctxs, rows, cols)
    near, late, raw = lax.optimization_barrier((near, late, raw))
    late = lax.all_gather(late, "ctx", axis=0, tiled=True)
    own_raw = swap(raw, "ctx")[ctxs - 1]
    near_out = near[:, 3].reshape(8 * piece, cols)
    near = near[:, :3]
    near = jnp.broadcast_to(near[None], (4,) + near.shape)
    near, own_raw = lax.optimization_barrier((near, own_raw))
    far = lax.all_to_all(near, "ctx", 0, 0, axis_index_groups=xs)
    kinds = [part((4, 8, 1, piece, cols), 0, 0, i, 0, 0) for i in range(3)]
    raw_rows = lax.all_gather(own_raw, "head", axis=1, tiled=True)
    queries = call(
        query_kernel,
        shape((ctxs, rows, cols), bf16),
        raw_rows, gains[:1], far,
        specs=[VMEM, VMEM, kinds[0]],
    )
    queries, near_out = lax.optimization_barrier((queries, near_out))
    queries = swap(queries, "ctx")
    out_w = lax.all_gather(near_out, "ctx", axis=0, tiled=True, axis_index_groups=xs)
    step = 256
    keys, values = call(
        keyval_kernel,
        (shape((tokens, cols), bf16), shape((cols, tokens), bf16)),
        context, gains[:1], far, far,
        specs=[
            pl.BlockSpec((step, width), lambda i: (i, 0)),
            part((1, width), 0, 0),
            kinds[1],
            kinds[2],
        ],
        outs=(
            pl.BlockSpec((step, cols), lambda i: (i, 0)),
            pl.BlockSpec((cols, step), lambda i: (0, i)),
        ),
        grid=(tokens // step,),
    )

    is_last = (ctx_index == ctxs - 1).astype(jnp.int32)
    info = jnp.stack([valid_len[0], ctx_index * tokens, is_last])
    seen = last_visible.reshape(1, latents)
    sent = call(
        attend_kernel,
        shape((ctxs, rows + TAIL, cols), bf16),
        info, seen, queries.reshape(latents, cols), keys, values,
        specs=[SMEM, VMEM, VMEM, VMEM, VMEM],
    )
    got = swap(sent, "ctx")
    cut = [0, 3 * cols, 4 * cols, 4 * cols + 2 * ff, lates]
    qkv_w, mix_w, up_w, down_w = [late[:, i:j] for i, j in zip(cut, cut[1:])]
    spot = lax.rem(ctx_index, cols // rows).reshape(1)
    chunk = shape((heads, rows, cols), bf16)
    own = shape((rows, cols), bf16)
    terms = call(
        merge_kernel, chunk, spot, got, out_w, specs=[SMEM, VMEM, VMEM]
    )
    first, wide = call(add_kernel, (own, chunk), own_raw, swap(terms, "head"))
    query, pair = call(
        latent_kernel,
        (own, shape((ctxs, rows, 2 * cols), bf16)),
        swap(wide, "head"), gains[1:2], qkv_w,
    )
    place = lax.dynamic_slice_in_dim(last_visible, ctx_index * rows, rows, 0).reshape(rows, 1)
    pair, up_w = lax.optimization_barrier((swap(pair, "ctx"), up_w))
    terms = call(mix_kernel, chunk, place, seen, query, pair, mix_w)
    second, wide = call(add_kernel, (own, chunk), first, swap(terms, "head"))
    terms = call(feed_kernel, chunk, swap(wide, "head"), gains[2:3], up_w, down_w)
    return call(last_kernel, own, second, swap(terms, "head"))


def solution(mesh):
    in_specs = (
        P("ctx", None),
        P(None, "ctx", "head"),
        P("head", "ctx"),
        P(None, "ctx", "head"),
        P("head", "ctx"),
        P(None, "ctx", "head"),
        P("head", "ctx"),
        P(),
        P("ctx"),
        P(),
    )
    out_specs = P("ctx", "head")
    return jax.shard_map(body, mesh=mesh, in_specs=in_specs, out_specs=out_specs, check_vma=False)
```

```python
import jax
import jax.numpy as jnp
from jax import lax
from jax.experimental import pallas as pl
from jax.experimental.pallas import tpu as pltpu
from jax.sharding import PartitionSpec as P

HD = 128
epsilon = 1e-05
masked_score = -1e30
score_scale = HD ** (-0.5)
f32 = jnp.float32
bf16 = jnp.bfloat16
TAIL = 8
LATE = 58
LOG2E = 1.4426950408889634
VMEM = pl.BlockSpec(memory_space=pltpu.VMEM)
SMEM = pl.BlockSpec(memory_space=pltpu.SMEM)


def nt(a, b):
    return lax.dot_general(a, b, (((1,), (1,)), ((), ())), preferred_element_type=f32)


def nn(a, b):
    return jnp.dot(a, b, preferred_element_type=f32)


def call(kernel, out_shape, *args, specs=None, outs=None, grid=(1,), room=16):
    return pl.pallas_call(
        kernel,
        grid=grid,
        out_shape=out_shape,
        in_specs=specs if specs is not None else [VMEM] * len(args),
        out_specs=outs if outs is not None else jax.tree.map(lambda _: VMEM, out_shape),
        compiler_params=pltpu.CompilerParams(vmem_limit_bytes=room * 2**20),
    )(*args)


def part(shape, *index):
    return pl.BlockSpec(shape, lambda i: index)


def pack_kernel(attn_ref, out_w_ref, latent_ref, latent_out_ref, mlp_ref, down_ref, early_ref, mid_ref, late_ref):
    cols = out_w_ref.shape[1]
    for i, block in enumerate([attn_ref[0], attn_ref[1], attn_ref[2]]):
        early_ref[:, i] = jnp.broadcast_to(block[None], (early_ref.shape[0],) + block.shape)
    for ref, blocks in (
        (
            mid_ref,
            [down_ref[:, cols:]]
            + [latent_ref[i] for i in range(3)]
            + [latent_out_ref[...], out_w_ref[...]],
        ),
        (late_ref, [mlp_ref[0], mlp_ref[1], down_ref[:, :cols]]),
    ):
        at = 0
        for block in blocks:
            ref[:, at : at + block.shape[1]] = block
            at += block.shape[1]


def whole(x):
    return part(x.shape, *[0] * x.ndim)


def unit_rows(rows, gain):
    wide = rows.astype(f32)
    scale = lax.rsqrt(jnp.mean(wide * wide, axis=1, keepdims=True) + epsilon)
    return (wide * scale * gain).astype(bf16)


def joined(w_ref):
    return w_ref[...].reshape(-1, w_ref.shape[-1])


def query_kernel(rows_ref, gain_ref, w_ref, out_ref):
    query = nn(unit_rows(rows_ref[...], gain_ref[...]), joined(w_ref)).astype(bf16)
    out_ref[...] = jnp.broadcast_to(query[None], out_ref.shape)


def keyval_kernel(rows_ref, gain_ref, k_w_ref, v_w_ref, key_ref, value_ref):
    rows = unit_rows(rows_ref[...], gain_ref[...])
    key_ref[...] = nn(rows, joined(k_w_ref)).astype(bf16)
    value_ref[...] = nn(rows, joined(v_w_ref)).T.astype(bf16)


def attend_kernel(info_ref, *refs):
    is_last = info_ref[2] == 1
    pl.when(is_last)(lambda: attend(True, info_ref, *refs))
    pl.when(jnp.logical_not(is_last))(lambda: attend(False, info_ref, *refs))


def attend(last, info_ref, seen_ref, q_ref, k_ref, v_ref, out_ref):
    keys, cols = k_ref.shape
    count, rows = out_ref.shape[0], out_ref.shape[1] - TAIL
    step = 256
    chunks = step // rows
    bias = jnp.where(
        lax.broadcasted_iota(jnp.int32, (keys, 1), 0) < info_ref[0], 0.0, masked_score
    )
    for t in range(count * rows // step):
        at = slice(t * step, (t + 1) * step)
        score = nt(k_ref[...], q_ref[at, :]) + bias
        if last:
            position = lax.broadcasted_iota(jnp.int32, (keys, step), 0) + info_ref[1]
            score = jnp.where(position <= seen_ref[:, at], score, masked_score)
        top = jnp.max(score, axis=0, keepdims=True)
        prob = jnp.exp2((score - top) * (score_scale * LOG2E))
        total = jnp.sum(prob, axis=0, keepdims=True)
        out = (nn(v_ref[...], prob.astype(bf16)) / total).T
        out = out.reshape(chunks, rows, cols)
        lse = top * score_scale + jnp.log(total)
        high = lse.astype(bf16).astype(f32)
        middle = (lse - high).astype(bf16).astype(f32)
        low = lse - high - middle
        pieces = jnp.concatenate([high, middle, low, jnp.zeros((TAIL - 3, step), f32)])
        per = cols // rows
        for g in range(chunks):
            tail = pieces[:, g // per * cols : (g // per + 1) * cols]
            out_ref[t * chunks + g] = jnp.concatenate([out[g], tail]).astype(bf16)


def merge_kernel(info_ref, got_ref, w_ref, out_ref):
    count, height, cols = got_ref.shape
    rows = height - TAIL
    got = got_ref[...].astype(f32)
    lse = jnp.sum(got[:, rows:, :], axis=1)
    weight = jnp.exp(lse - jnp.max(lse, axis=0, keepdims=True))
    weight = (weight / jnp.sum(weight, axis=0, keepdims=True)).T
    own = jnp.zeros((rows, count), f32)
    for i in range(cols // rows):
        own = jnp.where(info_ref[0] == i, weight[i * rows : (i + 1) * rows, :], own)
    total = jnp.zeros((rows, cols), f32)
    for s in range(count):
        total += own[:, s : s + 1] * got[s, :rows, :]
    project(total.astype(bf16), lambda h: w_ref[h * cols : (h + 1) * cols, :], out_ref)


def project(acts, weight_rows, out_ref):
    for h in range(out_ref.shape[0]):
        out_ref[h] = nt(acts, weight_rows(h)).astype(bf16)


def add_kernel(base_ref, terms_ref, out_ref, wide_ref):
    total = base_ref[...].astype(f32) + jnp.sum(terms_ref[...].astype(f32), axis=0)
    out_ref[...] = total.astype(bf16)
    wide_ref[...] = jnp.broadcast_to(total.astype(bf16)[None], wide_ref.shape)


def last_kernel(base_ref, terms_ref, out_ref):
    total = base_ref[...].astype(f32) + jnp.sum(terms_ref[...].astype(f32), axis=0)
    out_ref[...] = total.astype(bf16)


def unit(all_ref, gain_ref):
    rows = jnp.concatenate([all_ref[h] for h in range(all_ref.shape[0])], axis=1)
    return unit_rows(rows, gain_ref[...])


def latent_kernel(all_ref, gain_ref, w_ref, q_ref, pair_ref):
    qkv = nn(unit(all_ref, gain_ref), w_ref[...]).astype(bf16)
    cols = q_ref.shape[1]
    q_ref[...] = qkv[:, :cols]
    pair_ref[...] = jnp.broadcast_to(qkv[:, cols:][None], pair_ref.shape)


def mix_kernel(own_ref, seen_ref, q_ref, pair_ref, w_ref, out_ref):
    cols = q_ref.shape[1]
    pair = pair_ref[...].reshape(-1, 2 * cols)
    seen = seen_ref[...] <= own_ref[...]
    score = jnp.where(seen, nt(q_ref[...], pair[:, :cols]) * score_scale, masked_score)
    prob = jnp.where(seen, jnp.exp(score - jnp.max(score, axis=1, keepdims=True)), 0.0)
    prob = (prob / jnp.sum(prob, axis=1, keepdims=True)).astype(bf16)
    mixed = nn(prob, pair[:, cols:]).astype(bf16)
    project(mixed, lambda h: w_ref[h * cols : (h + 1) * cols, :], out_ref)


def feed_kernel(all_ref, gain_ref, w_ref, down_ref, out_ref):
    acts = unit(all_ref, gain_ref)
    cols = out_ref.shape[2]
    ff = down_ref.shape[1] + cols
    gate = nn(acts, w_ref[:, :ff])
    hidden = (gate / (1.0 + jnp.exp(-gate)) * nn(acts, w_ref[:, ff : 2 * ff])).astype(bf16)
    for h in range(out_ref.shape[0]):
        at = slice(h * cols, (h + 1) * cols)
        term = nt(hidden[:, :cols], w_ref[at, 2 * ff :]) + nt(hidden[:, cols:], down_ref[at, :])
        out_ref[h] = term.astype(bf16)


def swap(x, axis):
    return lax.all_to_all(x, axis, 0, 0)


def body(
    context, w_attn, w_out, w_latent, w_latent_out, w_mlp, w_down, gains, valid_len, last_visible
):
    tokens, width = context.shape
    cols = w_attn.shape[2]
    ff = w_mlp.shape[2]
    latents = last_visible.shape[0]
    ctxs = lax.axis_size("ctx")
    heads = lax.axis_size("head")
    rows = latents // ctxs
    ctx_index = lax.axis_index("ctx")
    shape = jax.ShapeDtypeStruct
    ys = [[i * 8 + j for j in range(8)] for i in range(4)]
    xs = [[i * 8 + j for i in range(4)] for j in range(8)]

    piece = w_attn.shape[1]
    mids = ff + 4 * cols
    lates = 2 * ff + cols
    pieces = (w_attn, w_out.T, w_latent, w_latent_out.T, w_mlp, w_down.T)
    early, mid, late = call(
        pack_kernel,
        (
            shape((8, 3, piece, cols), bf16),
            shape((piece, mids), bf16),
            shape((piece, lates), bf16),
        ),
        *pieces,
        specs=[whole(x) for x in pieces],
        outs=(VMEM, part((piece, mids), 0, 0), part((piece, lates), 0, 0)),
        room=LATE,
    )
    mid = lax.all_gather(mid, "ctx", axis=0, tiled=True)

    near = lax.all_to_all(early, "ctx", 0, 0, axis_index_groups=ys)
    pick = jnp.clip(last_visible - (ctxs - 1) * tokens, 0, tokens - 1)
    mine = lax.dynamic_slice_in_dim(context, lax.axis_index("head") * cols, cols, 1)
    raw = jnp.take(mine, pick, axis=0, mode="clip").reshape(ctxs, rows, cols)
    near, late, raw = lax.optimization_barrier((near, late, raw))
    late = lax.all_gather(late, "ctx", axis=0, tiled=True)
    own_raw = swap(raw, "ctx")[ctxs - 1]
    near = jnp.broadcast_to(near[None], (4,) + near.shape)
    near, own_raw = lax.optimization_barrier((near, own_raw))
    far = lax.all_to_all(near, "ctx", 0, 0, axis_index_groups=xs)
    kinds = [part((4, 8, 1, piece, cols), 0, 0, i, 0, 0) for i in range(3)]
    raw_rows = lax.all_gather(own_raw, "head", axis=1, tiled=True)
    queries = call(
        query_kernel,
        shape((ctxs, rows, cols), bf16),
        raw_rows, gains[:1], far,
        specs=[VMEM, VMEM, kinds[0]],
    )
    queries = swap(queries, "ctx")
    step = 256
    keys, values = call(
        keyval_kernel,
        (shape((tokens, cols), bf16), shape((cols, tokens), bf16)),
        context, gains[:1], far, far,
        specs=[
            pl.BlockSpec((step, width), lambda i: (i, 0)),
            part((1, width), 0, 0),
            kinds[1],
            kinds[2],
        ],
        outs=(
            pl.BlockSpec((step, cols), lambda i: (i, 0)),
            pl.BlockSpec((cols, step), lambda i: (0, i)),
        ),
        grid=(tokens // step,),
    )

    is_last = (ctx_index == ctxs - 1).astype(jnp.int32)
    info = jnp.stack([valid_len[0], ctx_index * tokens, is_last])
    seen = last_visible.reshape(1, latents)
    sent = call(
        attend_kernel,
        shape((ctxs, rows + TAIL, cols), bf16),
        info, seen, queries.reshape(latents, cols), keys, values,
        specs=[SMEM, VMEM, VMEM, VMEM, VMEM],
    )
    got = swap(sent, "ctx")
    cut = [0, ff - cols, ff + 2 * cols, ff + 3 * cols, mids]
    down, qkv_w, mix_w, out_w = [mid[:, i:j] for i, j in zip(cut, cut[1:])]
    spot = lax.rem(ctx_index, cols // rows).reshape(1)
    chunk = shape((heads, rows, cols), bf16)
    own = shape((rows, cols), bf16)
    terms = call(
        merge_kernel, chunk, spot, got, out_w, specs=[SMEM, VMEM, VMEM]
    )
    first, wide = call(add_kernel, (own, chunk), own_raw, swap(terms, "head"))
    query, pair = call(
        latent_kernel,
        (own, shape((ctxs, rows, 2 * cols), bf16)),
        swap(wide, "head"), gains[1:2], qkv_w,
    )
    place = lax.dynamic_slice_in_dim(last_visible, ctx_index * rows, rows, 0).reshape(rows, 1)
    terms = call(
        mix_kernel,
        chunk,
        place, seen, query, swap(pair, "ctx"), mix_w,
    )
    second, wide = call(add_kernel, (own, chunk), first, swap(terms, "head"))
    terms = call(
        feed_kernel,
        chunk,
        swap(wide, "head"), gains[2:3], late, down,
    )
    return call(last_kernel, own, second, swap(terms, "head"))


def solution(mesh):
    in_specs = (
        P("ctx", None),
        P(None, "ctx", "head"),
        P("head", "ctx"),
        P(None, "ctx", "head"),
        P("head", "ctx"),
        P(None, "ctx", "head"),
        P("head", "ctx"),
        P(),
        P("ctx"),
        P(),
    )
    out_specs = P("ctx", "head")
    return jax.shard_map(body, mesh=mesh, in_specs=in_specs, out_specs=out_specs, check_vma=False)
```

```python
import jax
import jax.numpy as jnp
from jax import lax
from jax.experimental import pallas as pl
from jax.experimental.pallas import tpu as pltpu
from jax.sharding import PartitionSpec as P

HD = 128
epsilon = 1e-05
masked_score = -1e30
score_scale = HD ** (-0.5)
f32 = jnp.float32
bf16 = jnp.bfloat16
TAIL = 8
LATE = 58
LOG2E = 1.4426950408889634
VMEM = pl.BlockSpec(memory_space=pltpu.VMEM)
SMEM = pl.BlockSpec(memory_space=pltpu.SMEM)


def nt(a, b):
    return lax.dot_general(a, b, (((1,), (1,)), ((), ())), preferred_element_type=f32)


def nn(a, b):
    return jnp.dot(a, b, preferred_element_type=f32)


def call(kernel, out_shape, *args, specs=None, outs=None, grid=(1,), room=16):
    return pl.pallas_call(
        kernel,
        grid=grid,
        out_shape=out_shape,
        in_specs=specs if specs is not None else [VMEM] * len(args),
        out_specs=outs if outs is not None else jax.tree.map(lambda _: VMEM, out_shape),
        compiler_params=pltpu.CompilerParams(vmem_limit_bytes=room * 2**20),
    )(*args)


def part(shape, *index):
    return pl.BlockSpec(shape, lambda i: index)


def pack_kernel(attn_ref, out_w_ref, latent_ref, latent_out_ref, mlp_ref, down_ref, early_ref, mid_ref, late_ref):
    for i, block in enumerate([attn_ref[0], attn_ref[1], attn_ref[2]]):
        early_ref[:, i] = jnp.broadcast_to(block[None], (early_ref.shape[0],) + block.shape)
    for ref, blocks in (
        (mid_ref, [mlp_ref[0]] + [latent_ref[i] for i in range(3)] + [latent_out_ref[...], out_w_ref[...]]),
        (late_ref, [mlp_ref[1], down_ref[...]]),
    ):
        at = 0
        for block in blocks:
            ref[:, at : at + block.shape[1]] = block
            at += block.shape[1]


def whole(x):
    return part(x.shape, *[0] * x.ndim)


def unit_rows(rows, gain):
    wide = rows.astype(f32)
    scale = lax.rsqrt(jnp.mean(wide * wide, axis=1, keepdims=True) + epsilon)
    return (wide * scale * gain).astype(bf16)


def joined(w_ref):
    return w_ref[...].reshape(-1, w_ref.shape[-1])


def query_kernel(rows_ref, gain_ref, w_ref, out_ref):
    query = nn(unit_rows(rows_ref[...], gain_ref[...]), joined(w_ref)).astype(bf16)
    out_ref[...] = jnp.broadcast_to(query[None], out_ref.shape)


def keyval_kernel(rows_ref, gain_ref, k_w_ref, v_w_ref, key_ref, value_ref):
    rows = unit_rows(rows_ref[...], gain_ref[...])
    key_ref[...] = nn(rows, joined(k_w_ref)).astype(bf16)
    value_ref[...] = nn(rows, joined(v_w_ref)).T.astype(bf16)


def attend_kernel(info_ref, *refs):
    is_last = info_ref[2] == 1
    pl.when(is_last)(lambda: attend(True, info_ref, *refs))
    pl.when(jnp.logical_not(is_last))(lambda: attend(False, info_ref, *refs))


def attend(last, info_ref, seen_ref, q_ref, k_ref, v_ref, out_ref):
    keys, cols = k_ref.shape
    count, rows = out_ref.shape[0], out_ref.shape[1] - TAIL
    step = 256
    chunks = step // rows
    bias = jnp.where(
        lax.broadcasted_iota(jnp.int32, (keys, 1), 0) < info_ref[0], 0.0, masked_score
    )
    for t in range(count * rows // step):
        at = slice(t * step, (t + 1) * step)
        score = nt(k_ref[...], q_ref[at, :]) + bias
        if last:
            position = lax.broadcasted_iota(jnp.int32, (keys, step), 0) + info_ref[1]
            score = jnp.where(position <= seen_ref[:, at], score, masked_score)
        top = jnp.max(score, axis=0, keepdims=True)
        prob = jnp.exp2((score - top) * (score_scale * LOG2E))
        total = jnp.sum(prob, axis=0, keepdims=True)
        out = (nn(v_ref[...], prob.astype(bf16)) / total).T
        out = out.reshape(chunks, rows, cols)
        lse = top * score_scale + jnp.log(total)
        high = lse.astype(bf16).astype(f32)
        middle = (lse - high).astype(bf16).astype(f32)
        low = lse - high - middle
        pieces = jnp.concatenate([high, middle, low, jnp.zeros((TAIL - 3, step), f32)])
        per = cols // rows
        for g in range(chunks):
            tail = pieces[:, g // per * cols : (g // per + 1) * cols]
            out_ref[t * chunks + g] = jnp.concatenate([out[g], tail]).astype(bf16)


def merge_kernel(info_ref, got_ref, w_ref, out_ref):
    count, height, cols = got_ref.shape
    rows = height - TAIL
    got = got_ref[...].astype(f32)
    lse = jnp.sum(got[:, rows:, :], axis=1)
    weight = jnp.exp(lse - jnp.max(lse, axis=0, keepdims=True))
    weight = (weight / jnp.sum(weight, axis=0, keepdims=True)).T
    own = jnp.zeros((rows, count), f32)
    for i in range(cols // rows):
        own = jnp.where(info_ref[0] == i, weight[i * rows : (i + 1) * rows, :], own)
    total = jnp.zeros((rows, cols), f32)
    for s in range(count):
        total += own[:, s : s + 1] * got[s, :rows, :]
    project(total.astype(bf16), lambda h: w_ref[h * cols : (h + 1) * cols, :], out_ref)


def project(acts, weight_rows, out_ref):
    for h in range(out_ref.shape[0]):
        out_ref[h] = nt(acts, weight_rows(h)).astype(bf16)


def add_kernel(base_ref, terms_ref, out_ref, wide_ref):
    total = base_ref[...].astype(f32) + jnp.sum(terms_ref[...].astype(f32), axis=0)
    out_ref[...] = total.astype(bf16)
    wide_ref[...] = jnp.broadcast_to(total.astype(bf16)[None], wide_ref.shape)


def last_kernel(base_ref, terms_ref, out_ref):
    total = base_ref[...].astype(f32) + jnp.sum(terms_ref[...].astype(f32), axis=0)
    out_ref[...] = total.astype(bf16)


def unit(all_ref, gain_ref):
    rows = jnp.concatenate([all_ref[h] for h in range(all_ref.shape[0])], axis=1)
    return unit_rows(rows, gain_ref[...])


def latent_kernel(all_ref, gain_ref, w_ref, q_ref, pair_ref):
    qkv = nn(unit(all_ref, gain_ref), w_ref[...]).astype(bf16)
    cols = q_ref.shape[1]
    q_ref[...] = qkv[:, :cols]
    pair_ref[...] = jnp.broadcast_to(qkv[:, cols:][None], pair_ref.shape)


def mix_kernel(own_ref, seen_ref, q_ref, pair_ref, w_ref, out_ref):
    cols = q_ref.shape[1]
    pair = pair_ref[...].reshape(-1, 2 * cols)
    seen = seen_ref[...] <= own_ref[...]
    score = jnp.where(seen, nt(q_ref[...], pair[:, :cols]) * score_scale, masked_score)
    prob = jnp.where(seen, jnp.exp(score - jnp.max(score, axis=1, keepdims=True)), 0.0)
    prob = (prob / jnp.sum(prob, axis=1, keepdims=True)).astype(bf16)
    mixed = nn(prob, pair[:, cols:]).astype(bf16)
    project(mixed, lambda h: w_ref[h * cols : (h + 1) * cols, :], out_ref)


def gate_kernel(all_ref, gain_ref, w_ref, acts_ref, gate_ref):
    acts = unit(all_ref, gain_ref)
    gate = nn(acts, w_ref[...])
    acts_ref[...] = acts
    gate_ref[...] = gate / (1.0 + jnp.exp(-gate))


def feed_kernel(acts_ref, gate_ref, w_ref, out_ref):
    cols = out_ref.shape[2]
    ff = gate_ref.shape[1]
    hidden = (gate_ref[...] * nn(acts_ref[...], w_ref[:, :ff])).astype(bf16)
    project(hidden, lambda h: w_ref[h * cols : (h + 1) * cols, ff:], out_ref)


def swap(x, axis):
    return lax.all_to_all(x, axis, 0, 0)


def body(
    context, w_attn, w_out, w_latent, w_latent_out, w_mlp, w_down, gains, valid_len, last_visible
):
    tokens, width = context.shape
    cols = w_attn.shape[2]
    ff = w_mlp.shape[2]
    latents = last_visible.shape[0]
    ctxs = lax.axis_size("ctx")
    heads = lax.axis_size("head")
    rows = latents // ctxs
    ctx_index = lax.axis_index("ctx")
    shape = jax.ShapeDtypeStruct
    ys = [[i * 8 + j for j in range(8)] for i in range(4)]
    xs = [[i * 8 + j for i in range(4)] for j in range(8)]

    piece = w_attn.shape[1]
    mids = ff + 5 * cols
    pieces = (w_attn, w_out.T, w_latent, w_latent_out.T, w_mlp, w_down.T)
    early, mid, late = call(
        pack_kernel,
        (
            shape((8, 3, piece, cols), bf16),
            shape((piece, mids), bf16),
            shape((piece, 2 * ff), bf16),
        ),
        *pieces,
        specs=[whole(x) for x in pieces],
        outs=(VMEM, part((piece, mids), 0, 0), part((piece, 2 * ff), 0, 0)),
        room=LATE,
    )
    mid = lax.all_gather(mid, "ctx", axis=0, tiled=True)

    near = lax.all_to_all(early, "ctx", 0, 0, axis_index_groups=ys)
    pick = jnp.clip(last_visible - (ctxs - 1) * tokens, 0, tokens - 1)
    mine = lax.dynamic_slice_in_dim(context, lax.axis_index("head") * cols, cols, 1)
    raw = jnp.take(mine, pick, axis=0, mode="clip").reshape(ctxs, rows, cols)
    near, late, raw = lax.optimization_barrier((near, late, raw))
    late = lax.all_gather(late, "ctx", axis=0, tiled=True)
    own_raw = swap(raw, "ctx")[ctxs - 1]
    near = jnp.broadcast_to(near[None], (4,) + near.shape)
    near, own_raw = lax.optimization_barrier((near, own_raw))
    far = lax.all_to_all(near, "ctx", 0, 0, axis_index_groups=xs)
    kinds = [part((4, 8, 1, piece, cols), 0, 0, i, 0, 0) for i in range(3)]
    raw_rows = lax.all_gather(own_raw, "head", axis=1, tiled=True)
    queries = call(
        query_kernel,
        shape((ctxs, rows, cols), bf16),
        raw_rows, gains[:1], far,
        specs=[VMEM, VMEM, kinds[0]],
    )
    queries = swap(queries, "ctx")
    step = 256
    keys, values = call(
        keyval_kernel,
        (shape((tokens, cols), bf16), shape((cols, tokens), bf16)),
        context, gains[:1], far, far,
        specs=[
            pl.BlockSpec((step, width), lambda i: (i, 0)),
            part((1, width), 0, 0),
            kinds[1],
            kinds[2],
        ],
        outs=(
            pl.BlockSpec((step, cols), lambda i: (i, 0)),
            pl.BlockSpec((cols, step), lambda i: (0, i)),
        ),
        grid=(tokens // step,),
    )

    is_last = (ctx_index == ctxs - 1).astype(jnp.int32)
    info = jnp.stack([valid_len[0], ctx_index * tokens, is_last])
    seen = last_visible.reshape(1, latents)
    sent = call(
        attend_kernel,
        shape((ctxs, rows + TAIL, cols), bf16),
        info, seen, queries.reshape(latents, cols), keys, values,
        specs=[SMEM, VMEM, VMEM, VMEM, VMEM],
    )
    got = swap(sent, "ctx")
    cut = [0, ff, ff + 3 * cols, ff + 4 * cols, mids]
    gate_w, qkv_w, mix_w, out_w = [mid[:, i:j] for i, j in zip(cut, cut[1:])]
    spot = lax.rem(ctx_index, cols // rows).reshape(1)
    chunk = shape((heads, rows, cols), bf16)
    own = shape((rows, cols), bf16)
    terms = call(
        merge_kernel, chunk, spot, got, out_w, specs=[SMEM, VMEM, VMEM]
    )
    first, wide = call(add_kernel, (own, chunk), own_raw, swap(terms, "head"))
    query, pair = call(
        latent_kernel,
        (own, shape((ctxs, rows, 2 * cols), bf16)),
        swap(wide, "head"), gains[1:2], qkv_w,
    )
    place = lax.dynamic_slice_in_dim(last_visible, ctx_index * rows, rows, 0).reshape(rows, 1)
    terms = call(
        mix_kernel,
        chunk,
        place, seen, query, swap(pair, "ctx"), mix_w,
    )
    second, wide = call(add_kernel, (own, chunk), first, swap(terms, "head"))
    acts, gate = call(
        gate_kernel,
        (shape((rows, width), bf16), shape((rows, ff), f32)),
        swap(wide, "head"), gains[2:3], gate_w,
    )
    terms = call(feed_kernel, chunk, acts, gate, late)
    return call(last_kernel, own, second, swap(terms, "head"))


def solution(mesh):
    in_specs = (
        P("ctx", None),
        P(None, "ctx", "head"),
        P("head", "ctx"),
        P(None, "ctx", "head"),
        P("head", "ctx"),
        P(None, "ctx", "head"),
        P("head", "ctx"),
        P(),
        P("ctx"),
        P(),
    )
    out_specs = P("ctx", "head")
    return jax.shard_map(body, mesh=mesh, in_specs=in_specs, out_specs=out_specs, check_vma=False)
```
